128 devices in a mesh: lat: 8 (over x, core), lon: 16 (over y, z).
Axes of the slice: x: 4, y: 4, z: 4, core: 2. Of those that a mesh axis runs over, the one named last changes fastest.
Arguments:
- positions: int32 [9216], P(('lat', 'lon')), may hold values from 0 to 36863, as said below
- encoded: float32 [9216, 1280], P(('lat', 'lon')), may hold values from -6 to 6
- mask_token: float32 [1280], replicated, may hold values from -4 to 4
- norm_gain: float32 [1280], replicated, may hold values from 0.1 to 1.9
- w_query: float32 [1280, 640], replicated
- w_key: float32 [1280, 640], replicated
- w_value: float32 [1280, 640], replicated, may hold values from -0.15625 to 0.15625
- w_out: float32 [640, 1280], replicated, may hold values from -0.25 to 0.25
- cotangent: float32 [96, 384, 1280], P('lat', 'lon'), may hold values from -6 to 6
Outputs:
- decoded: float32 [96, 384, 1280], P('lat', 'lon')
- grad_query: float32 [1280, 640], P('lon')
- grad_key: float32 [1280, 640], P('lon')
- grad_value: float32 [1280, 640], P('lon')
- grad_out: float32 [640, 1280], P('lon')
- grad_mask: float32 [1280], P('lon')
- grad_gain: float32 [1280], P('lon')
- grad_encoded: float32 [9216, 1280], P(('lat', 'lon'))
The draws below stay inside these ranges and needn't reach their ends.
Inputs may be any that keep to these rules, and one draw needn't show every extreme that they name: All positions are distinct cells, a quarter of the grid. Tile (a, b) is the block of 12 x (24) cells of index a along lat and b along lon. The 72 tokens of one encoder shard hold at most 2 cells of any one tile, and some tile holds exactly 2 from every shard.
All inputs are finite; a program needn't handle non-finite values.
Results may differ from the reference program's by a relative error of at most 0.0003.
Values sent between devices are 32-bit elements; how exact they have to be, the bound alone decides.
A program may use at most 192 MiB of HBM per device.

```python
import math
import jax
import jax.numpy as jnp
from jax import lax

D = 1280
HEADS = 8
HEAD = 80
WIN = 12
TILE = 288
V_DEV = 72
CAP = 2
VISIBLE = 9216
NLAT = 96
NLON = 384
N_LON = 16
DEVICES = 128


def weight_pair(key):
    return jax.random.normal(key, (D, HEADS * HEAD), jnp.float32) / math.sqrt(D)


def draw_w_query(key, part):
    shared = weight_pair(key)
    return shared


def draw_w_key(key, part):
    key = jax.random.fold_in(key, 22)
    first = jax.random.fold_in(key, 0)
    own = jax.random.normal(first, (D, HEADS * HEAD), jnp.float32) / math.sqrt(D)
    return own


def draw_positions(key, part):
    key = jax.random.fold_in(key, 11)
    pick_key, weight_key, order_key, cell_key = jax.random.split(key, 4)
    tile_ids = jnp.arange(DEVICES, dtype=jnp.int32)
    busiest = jax.random.randint(pick_key, (), 0, DEVICES)
    shares = jnp.where(tile_ids == busiest, 0, jax.random.randint(weight_key, (DEVICES,), 1, 8))
    heaviest = CAP * DEVICES
    remainder = VISIBLE - heaviest
    counts = remainder * shares // jnp.sum(shares)
    leftover = remainder - jnp.sum(counts)
    ranking = jax.random.permutation(order_key, DEVICES).astype(jnp.int32)
    ranking = ranking - (ranking > ranking[busiest]).astype(jnp.int32)
    extra = jnp.logical_and(ranking < leftover, tile_ids != busiest)
    counts = counts + extra.astype(jnp.int32) + jnp.where(tile_ids == busiest, heaviest, 0)
    starts = jnp.cumsum(counts) - counts
    serial = jnp.arange(VISIBLE, dtype=jnp.int32)
    owner = jnp.sum((starts[None, :] <= serial[:, None]).astype(jnp.int32), axis=1) - 1
    offset = serial - starts[owner]
    shuffles = jax.vmap(lambda tile_index: jax.random.permutation(jax.random.fold_in(cell_key, tile_index), TILE).astype(jnp.int32))(tile_ids)
    cell = shuffles[owner, offset]
    tile_width = TILE // WIN
    lat_cell = owner // N_LON * WIN + cell // tile_width
    lon_cell = owner % N_LON * tile_width + cell % tile_width
    flat_cells = lat_cell * NLON + lon_cell
    return flat_cells.reshape(V_DEV, DEVICES).T.reshape(VISIBLE)


def level_of(own_key, shape, shards, low, high):
    factor_of, own = 1.0, jax.random.fold_in(own_key, 6)
    for dim, blocks in shards:
        draws = jnp.exp(jax.random.uniform(jax.random.fold_in(own, dim), (blocks,), jnp.float32, low / len(shards), high / len(shards)))
        factor_of = factor_of * jnp.repeat(draws, shape[dim] // blocks).reshape([-1 if axis == dim else 1 for axis in range(len(shape))])
    return factor_of


def bell_draw(own_key, shape, scale, limit, cuts=(), kind=jnp.bfloat16):
    loudness = level_of(own_key, shape, cuts, -0.22, 0.18) if cuts else 1.0
    drawn = jax.random.normal(own_key, shape, jnp.float32) * scale * loudness
    return jnp.minimum(jnp.maximum(drawn, -limit), limit).astype(kind)


def setup_inputs(seed: int = 0) -> dict:
    arg_keys = jax.random.split(jax.random.key(seed), 10)
    return {
        "positions": draw_positions(jax.random.fold_in(arg_keys[9], 71), 0),
        "encoded": bell_draw(arg_keys[1], (VISIBLE, D), 1.0, 6.0, ((0, 128),), jnp.float32),
        "mask_token": bell_draw(arg_keys[2], (D,), 1.0, 4.0, (), jnp.float32),
        "norm_gain": jnp.clip(1.0 + 0.18 * jax.random.normal(arg_keys[3], (D,), jnp.float32), 0.1, 1.9),
        "w_query": draw_w_query(jax.random.fold_in(arg_keys[9], 71), 0),
        "w_key": draw_w_key(jax.random.fold_in(arg_keys[9], 71), 0),
        "w_value": bell_draw(arg_keys[6], (D, HEADS * HEAD), D ** -0.5, 0.15625, (), jnp.float32),
        "w_out": bell_draw(arg_keys[7], (HEADS * HEAD, D), (HEADS * HEAD) ** -0.5, 0.25, (), jnp.float32),
        "cotangent": bell_draw(arg_keys[8], (NLAT, NLON, D), 1.0, 6.0, ((0, 8), (1, 16)), jnp.float32),
    }


highest = lax.Precision.HIGHEST

def window_block(tile_grid, gain_vec, query_w, key_w, value_w, out_w, is_last):
    tile_rows, tile_cols, model_width = tile_grid.shape
    window_count = tile_cols // tile_rows
    window_area = tile_rows * tile_rows
    tokens = tile_grid.reshape(tile_rows, window_count, tile_rows, model_width).transpose(1, 0, 2, 3)
    tokens = tokens.reshape(window_count, window_area, model_width)
    centred = tokens - lax.optimization_barrier(jnp.mean(tokens, axis=-1, keepdims=True))
    variance = lax.optimization_barrier(jnp.mean(centred * centred, axis=-1, keepdims=True))
    normed = centred * lax.rsqrt(variance + 1e-05) * gain_vec
    flat_rows = normed.reshape(window_count * window_area, model_width)
    inner_width = query_w.shape[1]
    head_count = inner_width // HEAD
    query = jnp.dot(flat_rows, query_w, precision=highest).reshape(window_count, window_area, head_count, HEAD)
    key_rows = jnp.dot(flat_rows, key_w, precision=highest).reshape(window_count, window_area, head_count, HEAD)
    values = jnp.dot(flat_rows, value_w, precision=highest).reshape(window_count, window_area, head_count, HEAD)
    scores = jnp.einsum('wqhe,wkhe->whqk', query, key_rows, precision=highest) / math.sqrt(HEAD)
    window_row = jnp.arange(window_area) // tile_rows
    wrapped = jnp.logical_and(window_row >= tile_rows - tile_rows // 2, is_last)
    allowed = wrapped[:, None] == wrapped[None, :]
    scores = jnp.where(allowed, scores, -1e+30)
    row_max = lax.stop_gradient(lax.optimization_barrier(jnp.max(scores, axis=-1, keepdims=True)))
    exponent = jnp.exp(scores - row_max)
    weights = exponent / lax.optimization_barrier(jnp.sum(exponent, axis=-1, keepdims=True))
    attended = jnp.einsum('whqk,wkhe->wqhe', weights, values, precision=highest)
    attended = attended.reshape(window_count * window_area, inner_width)
    update = jnp.dot(attended, out_w, precision=highest).reshape(window_count, window_area, model_width)
    result = tokens + update
    result = result.reshape(window_count, tile_rows, tile_rows, model_width).transpose(1, 0, 2, 3)
    return result.reshape(tile_rows, tile_cols, model_width)

def reference(positions, encoded, mask_token, norm_gain, w_query, w_key, w_value, w_out, cotangent):
    grid_lat, grid_lon, model_width = cotangent.shape
    cells = grid_lat * grid_lon
    margin = WIN // 2
    filled = jnp.broadcast_to(mask_token, (cells, model_width)).at[positions].set(encoded)
    visible = jnp.zeros((cells,), jnp.float32).at[positions].set(1.0)
    rolled = jnp.roll(filled.reshape(grid_lat, grid_lon, model_width), (-margin, -margin), axis=(0, 1))
    grad_rolled = jnp.roll(cotangent, (-margin, -margin), axis=(0, 1))
    band_count = grid_lat // WIN
    bands = rolled.reshape(band_count, WIN, grid_lon, model_width)
    grad_bands = grad_rolled.reshape(band_count, WIN, grid_lon, model_width)

    def band_step(carry, inputs):
        band_index, band, grad_band = inputs
        is_last = band_index == band_count - 1

        def forward(tile_grid, gain_vec, query_w, key_w, value_w, out_w):
            return window_block(tile_grid, gain_vec, query_w, key_w, value_w, out_w, is_last)
        result, pullback = jax.vjp(forward, band, norm_gain, w_query, w_key, w_value, w_out)
        grads = pullback(grad_band)
        carry = tuple((total + part for total, part in zip(carry, grads[1:])))
        return (carry, (result, grads[0]))
    zeros = (jnp.zeros_like(norm_gain), jnp.zeros_like(w_query), jnp.zeros_like(w_key), jnp.zeros_like(w_value), jnp.zeros_like(w_out))
    totals, (outputs, grad_parts) = lax.scan(band_step, zeros, (jnp.arange(band_count, dtype=jnp.int32), bands, grad_bands))
    decoded = jnp.roll(outputs.reshape(grid_lat, grid_lon, model_width), (margin, margin), axis=(0, 1))
    grad_cells = jnp.roll(grad_parts.reshape(grid_lat, grid_lon, model_width), (margin, margin), axis=(0, 1))
    grad_cells = grad_cells.reshape(cells, model_width)
    scale = 1.0 / math.sqrt(cells)
    grad_mask = lax.optimization_barrier(jnp.sum((1.0 - visible)[:, None] * grad_cells, axis=0)) * scale
    grad_encoded = grad_cells[positions]
    grad_gain, grad_query, grad_key, grad_value, grad_out = totals
    return (decoded, grad_query * scale, grad_key * scale, grad_value * scale, grad_out * scale, grad_mask, grad_gain * scale, grad_encoded)
```

```python
import functools, math
import jax, jax.numpy as jnp
import numpy as np
from jax import lax
from jax.experimental import pallas as pl
from jax.experimental.pallas import tpu as pltpu
from jax.sharding import PartitionSpec as P

HEAD = 80
F32 = jnp.float32
BF16 = jnp.bfloat16


def split(x):
    hi = x.astype(BF16)
    return hi, (x - hi.astype(F32)).astype(BF16)


NN = (((1,), (0,)), ((), ()))
NT = (((1,), (1,)), ((), ()))
TN = (((0,), (0,)), ((), ()))


def dot(a, b, dims):
    return lax.dot_general(a, b, dims, preferred_element_type=F32)


def dot3(a, b, dims):
    return dot(a[0], b[0], dims) + (dot(a[0], b[1], dims) + dot(a[1], b[0], dims))


def head_lanes(h):
    low = h * HEAD // 128 * 128
    high = -(-(h + 1) * HEAD // 128) * 128
    return low, high


def compute_kernel(
    flag_ref, t_ref, g_ref, gain_ref, wq_hbm, wk_hbm, wv_hbm, wo_hbm,
    out_ref, dt_ref, dgain_ref, n_hi, n_lo, g_hi, g_lo, a_hi, a_lo, d_hi, d_lo,
    stage_a, stage_b, wqkv_hi, wqkv_lo, wo_hi, wo_lo,
    xhat_ref, rstd_ref, qkv_ref, att_ref, datt_ref, dqkv_ref, sems,
):
    rows, width = t_ref.shape
    inner = wo_hbm.shape[0]
    heads = inner // HEAD
    half = rows // 2

    load_o = pltpu.make_async_copy(wo_hbm, stage_b, sems.at[0])
    load_q = pltpu.make_async_copy(wq_hbm, stage_a.at[0], sems.at[1])
    load_k = pltpu.make_async_copy(wk_hbm, stage_a.at[1], sems.at[2])
    load_o.start()
    load_q.start()
    load_k.start()

    step = 32
    @pl.loop(0, rows // step)
    def _(i):
        r = pl.ds(pl.multiple_of(i * step, step), step)
        t = t_ref[r, :]
        c = t - jnp.mean(t, axis=-1, keepdims=True)
        rstd = lax.rsqrt(jnp.mean(c * c, axis=-1, keepdims=True) + 1e-5)
        xhat = c * rstd
        xhat_ref[r, :] = xhat
        rstd_ref[r, :] = rstd
        n_hi[r, :], n_lo[r, :] = split(xhat * gain_ref[...])
        g_hi[r, :], g_lo[r, :] = split(g_ref[r, :])

    load_o.wait()

    @pl.loop(0, inner // 32)
    def _(i):
        r = pl.ds(pl.multiple_of(i * 32, 32), 32)
        wo_hi[r, :], wo_lo[r, :] = split(stage_b[r, :])

    @pl.loop(0, inner // 128)
    def _(j):
        c = pl.ds(pl.multiple_of(j * 128, 128), 128)
        datt_ref[:, c] = dot3((g_hi[...], g_lo[...]), (wo_hi[c, :], wo_lo[c, :]), NT)

    def project(which, load, slot):
        load.wait()

        @pl.loop(0, width // 64)
        def _(i):
            r = pl.ds(pl.multiple_of(i * 64, 64), 64)
            c = slice(which * inner, (which + 1) * inner)
            wqkv_hi[r, c], wqkv_lo[r, c] = split(stage_a[slot, r, :])

    project(0, load_q, 0)
    load_v = pltpu.make_async_copy(wv_hbm, stage_a.at[0], sems.at[1])
    load_v.start()
    project(1, load_k, 1)
    project(2, load_v, 0)

    wide = 3 * inner
    full = wide // 256

    @pl.loop(0, full)
    def _(j):
        c = pl.ds(pl.multiple_of(j * 256, 256), 256)
        qkv_ref[:, c] = dot3((n_hi[...], n_lo[...]), (wqkv_hi[:, c], wqkv_lo[:, c]), NN)

    if wide % 256:
        c = slice(full * 256, wide)
        qkv_ref[:, c] = dot3((n_hi[...], n_lo[...]), (wqkv_hi[:, c], wqkv_lo[:, c]), NN)

    att_ref[...] = jnp.zeros_like(att_ref)
    dqkv_ref[...] = jnp.zeros_like(dqkv_ref)
    is_last = flag_ref[0] > 0
    low_q = lax.broadcasted_iota(jnp.int32, (half, half), 0) >= half // 2
    low_k = lax.broadcasted_iota(jnp.int32, (half, half), 1) >= half // 2
    blocked = jnp.logical_and(low_q != low_k, is_last)
    norm = 1.0 / math.sqrt(HEAD)

    @pl.loop(0, 2)
    def _(w):
        r = pl.ds(pl.multiple_of(w * half, 16), half)
        for h in range(heads):
            lo, hi = head_lanes(h)
            lane = lax.broadcasted_iota(jnp.int32, (half, hi - lo), 1) + lo
            mine = jnp.logical_and(lane >= h * HEAD, lane < (h + 1) * HEAD)

            def part(i):
                return qkv_ref[r, i * inner + lo:i * inner + hi]

            q = split(jnp.where(mine, part(0) * norm, 0.0))
            k = split(part(1))
            v = split(part(2))
            do = split(jnp.where(mine, datt_ref[r, lo:hi], 0.0))
            s = dot3(q, k, NT)
            s = jnp.where(blocked, -1e30, s)
            e = jnp.exp(s - jnp.max(s, axis=-1, keepdims=True))
            p32 = e / jnp.sum(e, axis=-1, keepdims=True)
            p = split(p32)
            o = dot3(p, v, NN)
            att_ref[r, lo:hi] += jnp.where(mine, o, 0.0)
            dp = dot3(do, v, NT)
            delta = jnp.sum(dp * p32, axis=-1, keepdims=True)
            ds = split(p32 * (dp - delta))
            dv = dot3(p, do, TN)
            dq = jnp.where(mine, dot3(ds, k, NN) * norm, 0.0)
            dk = dot3(ds, q, TN)
            dqkv_ref[r, lo:hi] += dq
            dqkv_ref[r, inner + lo:inner + hi] += dk
            dqkv_ref[r, 2 * inner + lo:2 * inner + hi] += dv

    a = split(att_ref[...])
    a_hi[...], a_lo[...] = a

    @pl.loop(0, width // 256)
    def _(j):
        c = pl.ds(pl.multiple_of(j * 256, 256), 256)
        out_ref[:, c] = t_ref[:, c] + dot3(a, (wo_hi[:, c], wo_lo[:, c]), NN)

    d_hi[...], d_lo[...] = split(dqkv_ref[...])

    @pl.loop(0, width // 256)
    def _(j):
        c = pl.ds(pl.multiple_of(j * 256, 256), 256)
        dt_ref[:, c] = dot3((d_hi[...], d_lo[...]), (wqkv_hi[c, :], wqkv_lo[c, :]), NT)

    dgain_ref[...] = jnp.zeros_like(dgain_ref)

    @pl.loop(0, rows // step)
    def _(i):
        r = pl.ds(pl.multiple_of(i * step, step), step)
        dn = dt_ref[r, :]
        xhat = xhat_ref[r, :]
        dgain_ref[...] += jnp.sum(dn * xhat, axis=0, keepdims=True)
        dx = dn * gain_ref[...]
        m1 = jnp.mean(dx, axis=-1, keepdims=True)
        m2 = jnp.mean(dx * xhat, axis=-1, keepdims=True)
        dt_ref[r, :] = g_ref[r, :] + rstd_ref[r, :] * (dx - m1 - xhat * m2)


def compute(flag, t, g, gain, wq, wk, wv, wo):
    rows, width = t.shape
    inner = wo.shape[0]
    vm = pl.BlockSpec(memory_space=pltpu.VMEM)
    anyspace = pl.BlockSpec(memory_space=pl.ANY)
    f = jax.ShapeDtypeStruct
    return pl.pallas_call(
        compute_kernel,
        out_shape=(
            f((rows, width), F32), f((rows, width), F32), f((1, width), F32),
            f((rows, width), BF16), f((rows, width), BF16), f((rows, width), BF16), f((rows, width), BF16),
            f((rows, inner), BF16), f((rows, inner), BF16),
            f((rows, 3 * inner), BF16), f((rows, 3 * inner), BF16),
        ),
        in_specs=[pl.BlockSpec(memory_space=pltpu.SMEM), vm, vm, vm] + [anyspace] * 4,
        out_specs=[vm] * 11,
        scratch_shapes=[
            pltpu.VMEM((2, width, inner), F32), pltpu.VMEM((inner, width), F32),
            pltpu.VMEM((width, 3 * inner), BF16), pltpu.VMEM((width, 3 * inner), BF16),
            pltpu.VMEM((inner, width), BF16), pltpu.VMEM((inner, width), BF16),
            pltpu.VMEM((rows, width), F32), pltpu.VMEM((rows, 1), F32),
            pltpu.VMEM((rows, 3 * inner), F32), pltpu.VMEM((rows, inner), F32),
            pltpu.VMEM((rows, inner), F32), pltpu.VMEM((rows, 3 * inner), F32),
            pltpu.SemaphoreType.DMA((4,)),
        ],
        compiler_params=pltpu.CompilerParams(vmem_limit_bytes=60 * 2**20),
        name="window_block",
    )(flag, t, g, gain, wq, wk, wv, wo)


MESH = pl.DeviceIdType.MESH
SLOTS = 256
TROWS = 304
SHARD = 40


def tile_rows_map():
    def block(r0, c0, cols):
        return [(r0 + i) * 24 + c0 + j for i in range(6) for j in range(cols)]

    none = [-5] * 4
    order = block(6, 6, 12) + block(6, 18, 6) + none + block(0, 6, 12) + block(0, 18, 6) + none
    order += none + block(6, 0, 6) + none + block(0, 0, 6)
    return np.array(order, np.int32)


def split3(x):
    hi = x.astype(BF16)
    rest = x - hi.astype(F32)
    mid = rest.astype(BF16)
    return hi, mid, (rest - mid.astype(F32)).astype(BF16)


def pick(onehot, x, dims):
    hi, mid, lo = split3(x)
    return (dot(onehot, hi, dims) + dot(onehot, mid, dims)) + dot(onehot, lo, dims)


def onehot(cond):
    return jnp.where(cond, 1.0, 0.0).astype(BF16)


def swap_matrix():
    j = lax.broadcasted_iota(jnp.int32, (SLOTS, SLOTS), 0)
    i = lax.broadcasted_iota(jnp.int32, (SLOTS, SLOTS), 1)
    b = jnp.right_shift(j, 4)
    a = jnp.bitwise_and(jnp.right_shift(j, 1), 7)
    return onehot(i == a * 32 + b * 2 + jnp.bitwise_and(j, 1))


def flip_low(i):
    return i + 1 - 2 * (i % 2)


def flip_far(i):
    return 3 - i


def remote(src, dst, send, recv, device):
    copy = pltpu.make_async_remote_copy(
        src_ref=src, dst_ref=dst, send_sem=send, recv_sem=recv, device_id=device, device_id_type=MESH
    )
    copy.start()
    return copy


def enter(a, b, diagonal):
    barrier = pltpu.get_barrier_semaphore()
    peers = [(a, (b + k) % 16) for k in range(1, 16)] + [((a + k) % 8, b) for k in range(1, 8)]
    if diagonal:
        peers += [((a + 1) % 8, (b + 1) % 16), ((a + 7) % 8, (b + 15) % 16)]
    for peer in peers:
        pl.semaphore_signal(barrier, inc=1, device_id=peer, device_id_type=MESH)
    pl.semaphore_wait(barrier, len(peers))


def rows_at(start, size):
    return pl.ds(pl.multiple_of(start, size), size)


def send_lon(src, dst, send, recv, a, b):
    copies = []
    for k in range(1, 16):
        peer = (b + k) % 16
        copies.append(remote(
            src.at[rows_at(peer * 16, 16)], dst.at[rows_at(b * 16, 16)], send.at[k - 1], recv.at[k - 1], (a, peer)
        ))
    dst[rows_at(b * 16, 16), :] = src[rows_at(b * 16, 16), :]
    return copies


def send_lat(src, dst, send, recv, a, b):
    copies = []
    for k in range(1, 8):
        peer = (a + k) % 8
        copies.append(remote(
            src.at[rows_at(peer * 32, 32)], dst.at[rows_at(a * 32, 32)], send.at[k - 1], recv.at[k - 1], (peer, b)
        ))
    dst[rows_at(a * 32, 32), :] = src[rows_at(a * 32, 32), :]
    return copies


def finish(copies):
    for copy in copies:
        copy.wait()


def front_kernel(
    cell_ref, row_ref, slot_ref, enc_ref, mask_ref, cot_ref,
    t_ref, g_ref, seat_ref,
    tile_t, tile_g, land_t, land_g, sa0, ra0, sb0, rb0, sa1, ra1, sb1, rb1,
    halo_s, halo_r, lon_s, lon_r, lat_s, lat_r,
):
    a, b = lax.axis_index("lat"), lax.axis_index("lon")
    width = cot_ref.shape[1]
    part = width // 2
    enter(a, b, True)

    seats = lax.broadcasted_iota(jnp.int32, (SLOTS, enc_ref.shape[0]), 0)
    to2 = onehot(seats == row_ref[1:2, :])
    sa0[:, :part] = pick(to2, enc_ref[:, :part], NN)
    cells = jnp.broadcast_to(slot_ref[...] + 1, (enc_ref.shape[0], 128)).astype(F32)
    sa0[:, part:] = pick(to2, cells, NN)
    go0 = send_lon(sa0, ra0, lon_s.at[0], lon_r.at[0], a, b)
    to1 = onehot(seats == row_ref[0:1, :])
    sa1[...] = pick(to1, enc_ref[:, part:], NN)
    go1 = send_lat(sa1, ra1, lat_s.at[0], lat_r.at[0], a, b)

    down, left = (a + 7) % 8, (b + 15) % 16

    def halo(tile, land, whole, first):
        moves = (
            (224, 40, land.at[pl.ds(0, 40)], (a, left)), (112, 72, whole.at[pl.ds(72, 72)], (down, b)),
            (184, 40, land.at[pl.ds(40, 40)], (down, b)), (264, 40, land.at[pl.ds(80, 40)], (down, left)),
        )
        return [
            remote(tile.at[pl.ds(row, size)], dst, halo_s.at[first + i], halo_r.at[first + i], device)
            for i, (row, size, dst, device) in enumerate(moves)
        ]

    def settle(tile, land, whole):
        whole[0:72, :] = tile[0:72, :]
        whole[144:180, :] = tile[72:108, :]
        whole[180:216, :] = land[4:40, :]
        whole[216:252, :] = land[40:76, :]
        whole[252:288, :] = land[84:120, :]

    grid = lax.broadcasted_iota(jnp.int32, (cot_ref.shape[0], TROWS), 0)
    place = onehot(grid == cell_ref[...])
    for j in range(0, width, 256):
        tile_g[:, j:j + 256] = pick(place, cot_ref[:, j:j + 256], TN)
    halo_g = halo(tile_g, land_g, g_ref, 0)

    swap = swap_matrix()
    finish(go0)
    sb0[...] = pick(swap, ra0[...], TN)
    go0 = send_lat(sb0, rb0, lat_s.at[1], lat_r.at[1], a, b)
    finish(go1)
    sb1[...] = pick(swap, ra1[...], NN)
    go1 = send_lon(sb1, rb1, lon_s.at[1], lon_r.at[1], a, b)

    finish(halo_g)
    settle(tile_g, land_g, g_ref)

    finish(go0)
    seat_ref[...] = rb0[:, part:]
    table = onehot(rb0[:, part:part + 1] == (cell_ref[...] + 1).astype(F32))
    seen = jnp.sum(table.astype(F32), axis=0, keepdims=True)
    first = lax.broadcasted_iota(jnp.int32, (16, 1), 0) == 0
    unseen = jnp.where(first, 1.0 - seen, 0.0).astype(BF16)
    mask = jnp.broadcast_to(mask_ref[...], (16, width))
    tile_t[:, :part] = pick(table, rb0[:, :part], TN) + pick(unseen, mask[:, :part], TN)
    table2 = dot(swap, table, NN).astype(BF16)
    finish(go1)
    tile_t[:, part:] = pick(table2, rb1[...], TN) + pick(unseen, mask[:, part:], TN)
    halo_t = halo(tile_t, land_t, t_ref, 4)
    finish(halo_t)
    settle(tile_t, land_t, t_ref)


def front(cell, row, slot, enc, mask, cot):
    rows, width = cot.shape
    part = width // 2
    vm = pl.BlockSpec(memory_space=pltpu.VMEM)
    f = jax.ShapeDtypeStruct
    dma = pltpu.SemaphoreType.DMA
    v = pltpu.VMEM
    return pl.pallas_call(
        front_kernel,
        out_shape=(f((rows, width), F32), f((rows, width), F32), f((SLOTS, 128), F32)),
        in_specs=[vm] * 6,
        out_specs=[vm] * 3,
        scratch_shapes=[
            v((TROWS, width), F32), v((TROWS, width), F32), v((120, width), F32), v((120, width), F32),
        ] + [v((SLOTS, part + 128), F32)] * 4 + [v((SLOTS, part), F32)] * 4 + [
            dma((8,)), dma((8,)), dma((2, 15)), dma((2, 15)), dma((2, 7)), dma((2, 7)),
        ],
        compiler_params=pltpu.CompilerParams(
            vmem_limit_bytes=60 * 2**20, collective_id=0, has_side_effects=True
        ),
        name="front",
    )(cell, row, slot, enc, mask, cot)


def tail_kernel(
    cell_ref, seat_ref, index_ref, out_ref, dt_ref, dgain_ref,
    n_hi, n_lo, g_hi, g_lo, a_hi, a_lo, d_hi, d_lo,
    decoded_ref, grads_ref, vec_ref, enc_ref,
    tile_d, tile_o, sa, ra, sb, rb, grad, acc, r1, r2, r3, r4, r5, vr,
    halo_s, halo_r, lon_s, lon_r, lat_s, lat_r, sum_s, sum_r, vec_s, vec_r,
):
    a, b = lax.axis_index("lat"), lax.axis_index("lon")
    x, c = a // 2, a % 2
    y, z = b // 4, b % 4
    width = dt_ref.shape[1]
    inner = a_hi.shape[1]
    part = width // 2
    scale = 1.0 / 192.0

    enter(a, b, True)

    up, right = (a + 1) % 8, (b + 1) % 16

    def halo(src, tile, first):
        moves = (
            (72, 72, 112, (up, b)), (216, 40, 184, (up, b)), (176, 40, 224, (a, right)), (248, 40, 264, (up, right)),
        )
        copies = []
        for i, (row, size, to, device) in enumerate(moves):
            copies.append(remote(
                src.at[pl.ds(row, size)], tile.at[pl.ds(to, size)], halo_s.at[first + i], halo_r.at[first + i], device
            ))
        tile[0:72, :] = src[0:72, :]
        tile[72:112, :] = src[144:184, :]
        return copies

    halo_d = halo(dt_ref, tile_d, 0)
    halo_o = halo(out_ref, tile_o, 4)

    def weight_grad(m):
        if m == 0:
            left = jnp.concatenate([a_hi[...], a_hi[...], a_lo[...]], axis=0)
            for i in range(2):
                cols = slice(i * part, (i + 1) * part)
                gh, gl = g_hi[:, cols], g_lo[:, cols]
                res = dot(left, jnp.concatenate([gh, gl, gh], axis=0), TN)
                grad[m, :, :, i] = res.reshape(4, 4, SHARD, inner)
        else:
            which = 3 - m
            cols = slice(which * inner, (which + 1) * inner)
            dh, dl = d_hi[:, cols], d_lo[:, cols]
            right3 = jnp.concatenate([dh, dl, dh], axis=0)
            for i in range(2):
                half = slice(i * part, (i + 1) * part)
                nh, nl = n_hi[:, half], n_lo[:, half]
                res = dot(jnp.concatenate([nh, nh, nl], axis=0), right3, TN)
                grad[m, 2 * i:2 * i + 2] = res.reshape(2, 4, 2, SHARD, inner)

    class Sum:
        def __init__(self, m):
            self.m = m
            self.first = m % 2 == 0
            self.q1, self.q2 = (flip_low, flip_far) if m < 2 else (flip_far, flip_low)
            self.stage = 0
            self.copies = []

        def chunk(self, i):
            return acc.at[self.m, i] if self.first else acc.at[self.m, :, i]

        def piece(self, i):
            return acc.at[self.m, y, i] if self.first else acc.at[self.m, i, z]

        def device1(self, i):
            return (a, i * 4 + z) if self.first else (a, y * 4 + i)

        def device2(self, i):
            return (a, y * 4 + i) if self.first else (a, i * 4 + z)

        def send(self, k, src, dst, device):
            self.copies.append(remote(src, dst, sum_s.at[self.m, k], sum_r.at[self.m, k], device))

        def begin(self):
            m, s = self.m, self.stage
            me1, me2 = (y, z) if self.first else (z, y)
            if s == 0:
                self.send(0, grad.at[m, :, :, 1 - c], acc.at[m], (a + 1 - 2 * c, b))
            elif s == 1:
                p = self.q1(me1)
                self.send(1, self.chunk(p), r1.at[m, 0], self.device1(p))
                self.send(2, self.chunk(self.q2(p)), r1.at[m, 1], self.device1(p))
            elif s == 2:
                p = self.q2(me1)
                self.send(3, self.chunk(p), r2.at[m], self.device1(p))
            elif s == 3:
                p = self.q1(me2)
                self.send(4, self.piece(p), r3.at[m, 0], self.device2(p))
                self.send(5, self.piece(self.q2(p)), r3.at[m, 1], self.device2(p))
            elif s == 4:
                p = self.q2(me2)
                self.send(6, self.piece(p), r4.at[m], self.device2(p))
            elif s == 5:
                self.send(7, self.piece(me2), r5.at[m, 0], (flip_low(x) * 2 + c, b))
            elif s == 6:
                self.send(8, self.piece(me2), r5.at[m, 1], (flip_far(x) * 2 + c, b))
            elif s == 7:
                self.send(9, grads_ref.at[m, c], grads_ref.at[m, c], (a + 1 - 2 * c, b))

        def end(self):
            m, s = self.m, self.stage
            me1, me2 = (y, z) if self.first else (z, y)
            finish(self.copies)
            self.copies = []
            if s == 0:
                @pl.loop(0, 4)
                def _(i):
                    acc[m, i] += grad[m, i, :, c]
            elif s == 1:
                for i in range(4):
                    for k, me in enumerate((me1, self.q2(me1))):
                        if self.first:
                            acc[m, me, i] += r1[m, k, i]
                        else:
                            acc[m, i, me] += r1[m, k, i]
            elif s == 2:
                for i in range(4):
                    if self.first:
                        acc[m, me1, i] += r2[m, i]
                    else:
                        acc[m, i, me1] += r2[m, i]
            elif s == 3:
                for k, me in enumerate((me2, self.q2(me2))):
                    if self.first:
                        acc[m, y, me] += r3[m, k]
                    else:
                        acc[m, me, z] += r3[m, k]
            elif s == 4:
                acc[m, y, z] += r4[m]
            elif s == 5:
                acc[m, y, z] += r5[m, 0]
            elif s == 6:
                grads_ref[m, c] = (acc[m, y, z] + r5[m, 1]) * scale
            self.stage += 1

        def step(self):
            self.end()
            if self.stage < 8:
                self.begin()

    sums = [Sum(m) for m in range(4)]

    vec_devices = [
        (a + 1 - 2 * c, b), (flip_low(x) * 2 + c, b), (flip_far(x) * 2 + c, b),
        (a, flip_low(y) * 4 + z), (a, flip_far(y) * 4 + z), (a, y * 4 + flip_low(z)), (a, y * 4 + flip_far(z)),
    ]
    vec_copies = []

    def vec_begin(k):
        vec_copies.append(remote(vec_ref, vr.at[k], vec_s.at[k], vec_r.at[k], vec_devices[k]))

    def vec_step():
        k = len(vec_copies) - 1
        vec_copies[k].wait()
        vec_ref[...] += vr[k]
        if k < 6:
            vec_begin(k + 1)

    weight_grad(0)
    sums[0].begin()

    finish(halo_d)
    table = onehot(seat_ref[:, 0:1] == (cell_ref[...] + 1).astype(F32))
    swap = swap_matrix()
    table2 = dot(swap, table, NN).astype(BF16)
    sa[0] = pick(table, tile_d[:, :part], NN)
    back0 = send_lat(sa.at[0], ra.at[0], lat_s.at[0], lat_r.at[0], a, b)
    sa[1] = pick(table2, tile_d[:, part:], NN)
    back1 = send_lon(sa.at[1], ra.at[1], lon_s.at[1], lon_r.at[1], a, b)
    seen = jnp.sum(table.astype(F32), axis=0, keepdims=True)
    masked = jnp.where(cell_ref[...] >= 0, 1.0 - seen, 0.0)
    masked = jnp.broadcast_to(masked, (8, TROWS)).astype(BF16)
    vec_ref[...] = pick(masked, tile_d[...], NN) * scale
    vec_ref[1:2, :] = dgain_ref[...] * scale
    vec_begin(0)

    weight_grad(1)
    sums[1].begin()
    sums[0].step()
    weight_grad(2)
    sums[2].begin()
    sums[1].step()

    finish(back0)
    sb[0] = pick(swap, ra[0], NN)
    back0 = send_lon(sb.at[0], rb.at[0], lon_s.at[0], lon_r.at[0], a, b)
    finish(back1)
    sb[1] = pick(swap, ra[1], TN)
    back1 = send_lat(sb.at[1], rb.at[1], lat_s.at[1], lat_r.at[1], a, b)

    weight_grad(3)
    sums[3].begin()
    sums[2].step()
    vec_step()

    finish(halo_o)
    cells = lax.broadcasted_iota(jnp.int32, (decoded_ref.shape[0], TROWS), 0)
    place = onehot(cells == cell_ref[...])
    for j in range(0, width, 256):
        decoded_ref[:, j:j + 256] = pick(place, tile_o[:, j:j + 256], NN)

    sums[3].step()
    sums[0].step()
    vec_step()

    finish(back0)
    finish(back1)
    slots = lax.broadcasted_iota(jnp.int32, (enc_ref.shape[0], SLOTS), 1)
    enc_ref[:, :part] = pick(onehot(slots == index_ref[:, 1:2]), rb[0], NN)
    enc_ref[:, part:] = pick(onehot(slots == index_ref[:, 0:1]), rb[1], NN)

    while any(total.stage < 8 for total in sums):
        front = min(total.stage for total in sums)
        for total in sums:
            if total.stage == front:
                total.step()
        if len(vec_copies) < 7:
            vec_step()
    vec_step()


def tail(cell, slot, index, out, dt, dgain, acts):
    rows, width = dt.shape
    inner = acts[4].shape[1]
    part = width // 2
    vm = pl.BlockSpec(memory_space=pltpu.VMEM)
    f = jax.ShapeDtypeStruct
    dma = pltpu.SemaphoreType.DMA
    v = pltpu.VMEM
    return pl.pallas_call(
        tail_kernel,
        out_shape=(
            f((rows, width), F32), f((4, 2, SHARD, inner), F32), f((8, width), F32), f((index.shape[0], width), F32),
        ),
        in_specs=[vm] * 14,
        out_specs=[vm] * 4,
        scratch_shapes=[
            v((TROWS, width), F32), v((TROWS, width), F32),
            v((2, SLOTS, part), F32), v((2, SLOTS, part), F32), v((2, SLOTS, part), F32), v((2, SLOTS, part), F32),
            v((4, 4, 4, 2, SHARD, inner), F32), v((4, 4, 4, SHARD, inner), F32),
            v((4, 2, 4, SHARD, inner), F32), v((4, 4, SHARD, inner), F32),
            v((4, 2, SHARD, inner), F32), v((4, SHARD, inner), F32), v((4, 2, SHARD, inner), F32),
            v((7, 8, width), F32),
            dma((8,)), dma((8,)), dma((2, 15)), dma((2, 15)), dma((2, 7)), dma((2, 7)),
            dma((4, 10)), dma((4, 10)), dma((7,)), dma((7,)),
        ],
        compiler_params=pltpu.CompilerParams(
            vmem_limit_bytes=60 * 2**20, collective_id=1, has_side_effects=True
        ),
        name="tail",
    )(cell, slot, index, out, dt, dgain, *acts)


def body(positions, encoded, mask_token, norm_gain, w_query, w_key, w_value, w_out, cotangent):
    tile_rows, tile_cols, model_width = cotangent.shape
    lat_count = lax.axis_size("lat")
    lon_count = lax.axis_size("lon")
    devices = lat_count * lon_count
    grid_lat = lat_count * tile_rows
    grid_lon = lon_count * tile_cols
    tile_size = tile_rows * tile_cols
    capacity = tile_size // devices
    lat_cell = positions // grid_lon
    lon_cell = positions % grid_lon
    target = lat_cell // tile_rows * lon_count + lon_cell // tile_cols
    cell_slot = lat_cell % tile_rows * tile_cols + lon_cell % tile_cols
    serial = jnp.arange(positions.shape[0])
    earlier = jnp.logical_and(target[None, :] == target[:, None], serial[None, :] < serial[:, None])
    rank = jnp.sum(earlier.astype(jnp.int32), axis=1)
    buffer_index = target * capacity + rank
    index2 = (target % lon_count) * (lat_count * capacity) + (target // lon_count) * capacity + rank
    row = jnp.stack([buffer_index, index2], axis=0)
    tile_map = jnp.asarray(tile_rows_map())[None]
    tokens, grad_rolled, seat = front(
        tile_map, row, cell_slot[:, None], encoded, mask_token[None], cotangent.reshape(tile_size, model_width)
    )
    is_last = lax.axis_index("lat") == lat_count - 1
    flag = is_last.astype(jnp.int32).reshape(1)
    out_rolled, grad_tile, grad_gain, *acts = compute(
        flag, tokens, grad_rolled, norm_gain[None], w_query, w_key, w_value, w_out
    )
    decoded, grads, vec, grad_encoded = tail(tile_map, seat, row.T, out_rolled, grad_tile, grad_gain, acts)
    decoded = decoded.reshape(tile_rows, tile_cols, model_width)
    b = lax.axis_index("lon")
    share = model_width // lon_count
    own = lax.dynamic_slice(vec, (0, b * share), (2, share))
    rows = grads.reshape(4, share, -1)
    grad_out = jnp.concatenate([grads[0, 0], grads[0, 1]], axis=1)
    return (decoded, rows[3], rows[2], rows[1], grad_out, own[0], own[1], grad_encoded)


def solution(mesh):
    return jax.shard_map(
        body,
        mesh=mesh,
        in_specs=(
            P(("lat", "lon")),
            P(("lat", "lon"), None),
            P(),
            P(),
            P(),
            P(),
            P(),
            P(),
            P("lat", "lon", None),
        ),
        out_specs=(
            P("lat", "lon", None),
            P("lon", None),
            P("lon", None),
            P("lon", None),
            P("lon", None),
            P("lon"),
            P("lon"),
            P(("lat", "lon"), None),
        ),
        check_vma=False,
    )
```

```python
import functools, math
import jax, jax.numpy as jnp
import numpy as np
from jax import lax
from jax.experimental import pallas as pl
from jax.experimental.pallas import tpu as pltpu
from jax.sharding import PartitionSpec as P

HEAD = 80
F32 = jnp.float32
BF16 = jnp.bfloat16


def split(x):
    hi = x.astype(BF16)
    return hi, (x - hi.astype(F32)).astype(BF16)


NN = (((1,), (0,)), ((), ()))
NT = (((1,), (1,)), ((), ()))
TN = (((0,), (0,)), ((), ()))


def dot(a, b, dims):
    return lax.dot_general(a, b, dims, preferred_element_type=F32)


def dot3(a, b, dims):
    return dot(a[0], b[0], dims) + (dot(a[0], b[1], dims) + dot(a[1], b[0], dims))


def head_lanes(h):
    low = h * HEAD // 128 * 128
    high = -(-(h + 1) * HEAD // 128) * 128
    return low, high


MESH = pl.DeviceIdType.MESH
SLOTS = 256
TROWS = 304
SHARD = 40
SCALE = 1.0 / 192.0


def tile_rows_map():
    def block(r0, c0, cols):
        return [(r0 + i) * 24 + c0 + j for i in range(6) for j in range(cols)]

    none = [-5] * 4
    order = block(6, 6, 12) + block(6, 18, 6) + none + block(0, 6, 12) + block(0, 18, 6) + none
    order += none + block(6, 0, 6) + none + block(0, 0, 6)
    return np.array(order, np.int32)


def split3(x):
    hi = x.astype(BF16)
    rest = x - hi.astype(F32)
    mid = rest.astype(BF16)
    return hi, mid, (rest - mid.astype(F32)).astype(BF16)


def pick(onehot, x, dims):
    hi, mid, lo = split3(x)
    return (dot(onehot, hi, dims) + dot(onehot, mid, dims)) + dot(onehot, lo, dims)


def onehot(cond):
    return jnp.where(cond, 1.0, 0.0).astype(BF16)


def swap_matrix():
    j = lax.broadcasted_iota(jnp.int32, (SLOTS, SLOTS), 0)
    i = lax.broadcasted_iota(jnp.int32, (SLOTS, SLOTS), 1)
    b = jnp.right_shift(j, 4)
    a = jnp.bitwise_and(jnp.right_shift(j, 1), 7)
    return onehot(i == a * 32 + b * 2 + jnp.bitwise_and(j, 1))


def flip_low(i):
    return i + 1 - 2 * (i % 2)


def flip_far(i):
    return 3 - i


def remote(src, dst, send, recv, device):
    copy = pltpu.make_async_remote_copy(
        src_ref=src, dst_ref=dst, send_sem=send, recv_sem=recv, device_id=device, device_id_type=MESH
    )
    copy.start()
    return copy


def rows_at(start, size):
    return pl.ds(pl.multiple_of(start, size), size)


def send_lon(src, dst, send, recv, a, b, lanes=None):
    cols = pl.ds(0, lanes or src.shape[1])
    copies = []
    for k in range(1, 16):
        peer = (b + k) % 16
        copies.append(remote(
            src.at[rows_at(peer * 16, 16), cols], dst.at[rows_at(b * 16, 16), cols], send.at[k - 1], recv.at[k - 1], (a, peer)
        ))
    dst[rows_at(b * 16, 16), :] = src[rows_at(b * 16, 16), :]
    return copies


def send_lat(src, dst, send, recv, a, b, lanes=None):
    cols = pl.ds(0, lanes or src.shape[1])
    copies = []
    for k in range(1, 8):
        peer = (a + k) % 8
        copies.append(remote(
            src.at[rows_at(peer * 32, 32), cols], dst.at[rows_at(a * 32, 32), cols], send.at[k - 1], recv.at[k - 1], (peer, b)
        ))
    dst[rows_at(a * 32, 32), :] = src[rows_at(a * 32, 32), :]
    return copies


def finish(copies):
    for copy in copies:
        copy.wait()


class Sum:
    def __init__(self, m, place, w, acc, r1, r2, r3, r4, r5, fin, send_sem, recv_sem):
        self.m, self.place = m, place
        self.w, self.acc, self.r = w, acc, (r1, r2, r3, r4, r5)
        self.fin, self.send_sem, self.recv_sem = fin, send_sem, recv_sem
        self.first = m % 2 == 0
        self.stage, self.slot, self.copies = 0, 0, []

    def chunk(self, i, half):
        rest = pl.ds(2 * half, 2)
        return (self.m, i, rest) if self.first else (self.m, rest, i)

    def piece(self, i, half):
        a, b, x, c, y, z = self.place
        rows = pl.ds(0, 24) if half == 0 else pl.ds(24, 16)
        return (self.m, y, i, rows) if self.first else (self.m, i, z, rows)

    def near(self, ring, i):
        a, b, x, c, y, z = self.place
        return (a, i * 4 + z) if ring == self.first else (a, y * 4 + i)

    def send(self, src, dst, device):
        k = self.slot
        self.slot += 1
        self.copies.append(remote(src, dst, self.send_sem.at[self.m, k], self.recv_sem.at[self.m, k], device))

    def begin(self):
        a, b, x, c, y, z = self.place
        m, acc, (r1, r2, r3, r4, r5) = self.m, self.acc, self.r
        me1, me2 = (y, z) if self.first else (z, y)
        s = self.stage
        if s == 0:
            self.send(self.w.at[m, :, :, 1 - c], acc.at[m], (a + 1 - 2 * c, b))
            return
        if s == 7:
            self.send(self.fin.at[m, c], self.fin.at[m, c], (a + 1 - 2 * c, b))
            return
        for half in range(2):
            q1, q2 = (flip_low, flip_far) if half == 0 else (flip_far, flip_low)
            rows = pl.ds(0, 24) if half == 0 else pl.ds(24, 16)
            if s == 1:
                p = q1(me1)
                self.send(acc.at[self.chunk(p, half)], r1.at[m, 0, half], self.near(True, p))
                self.send(acc.at[self.chunk(q2(p), half)], r1.at[m, 1, half], self.near(True, p))
            elif s == 2:
                p = q2(me1)
                self.send(acc.at[self.chunk(p, half)], r2.at[m, half], self.near(True, p))
            elif s == 3:
                p = q1(me2)
                self.send(acc.at[self.piece(p, half)], r3.at[m, 0, rows], self.near(False, p))
                self.send(acc.at[self.piece(q2(p), half)], r3.at[m, 1, rows], self.near(False, p))
            elif s == 4:
                p = q2(me2)
                self.send(acc.at[self.piece(p, half)], r4.at[m, rows], self.near(False, p))
            elif s == 5:
                self.send(acc.at[self.piece(me2, half)], r5.at[m, 0, rows], (q1(x) * 2 + c, b))
            elif s == 6:
                self.send(acc.at[self.piece(me2, half)], r5.at[m, 1, rows], (q2(x) * 2 + c, b))

    def end(self):
        a, b, x, c, y, z = self.place
        m, acc, (r1, r2, r3, r4, r5) = self.m, self.acc, self.r
        me1, me2 = (y, z) if self.first else (z, y)
        s = self.stage
        finish(self.copies)
        self.copies = []
        if s == 0:
            @pl.loop(0, 4)
            def _(i):
                acc[m, i] += self.w[m, i, :, c]
        for half in range(2):
            q2 = flip_far if half == 0 else flip_low
            rows = pl.ds(0, 24) if half == 0 else pl.ds(24, 16)
            if s == 1:
                acc[self.chunk(me1, half)] += r1[m, 0, half]
                acc[self.chunk(q2(me1), half)] += r1[m, 1, half]
            elif s == 2:
                acc[self.chunk(me1, half)] += r2[m, half]
            elif s == 3:
                acc[self.piece(me2, half)] += r3[m, 0, rows]
                acc[self.piece(q2(me2), half)] += r3[m, 1, rows]
            elif s == 4:
                acc[self.piece(me2, half)] += r4[m, rows]
            elif s == 5:
                acc[self.piece(me2, half)] += r5[m, 0, rows]
            elif s == 6:
                self.fin[m, c, rows] = (acc[self.piece(me2, half)] + r5[m, 1, rows]) * SCALE
        self.stage += 1

    def step(self):
        self.end()
        if self.stage < 8:
            self.begin()


def step_kernel(
    cell_ref, row_ref, index_ref, slot_ref, enc_ref, mask_ref, gain_ref, cot_hbm, wq_hbm, wk_hbm, wv_hbm, wo_hbm,
    decoded_hbm, dq_ref, dk_ref, dv_ref, do_ref, vec_ref, denc_ref,
    w, acc, r1, r2, r3, r4, r5, fin, vr,
    tile_t, tile_g, land_t, land_g, sa0, ra0, rb0, sa1, ra1, rb1,
    t_ref, g_ref, xhat_ref, dn_ref, rstd_ref, n_hi, n_lo, qkv_ref, p_ref, att_ref, datt_ref, dqkv_ref,
    load_s, halo_s, halo_r, lon_s, lon_r, lat_s, lat_r, sum_s, sum_r, vec_s, vec_r, free_s,
):
    a, b = lax.axis_index("lat"), lax.axis_index("lon")
    x, c = a // 2, a % 2
    y, z = b // 4, b % 4
    rows, width = t_ref.shape
    inner = att_ref.shape[1]
    part = width // 2
    heads = inner // HEAD
    half = rows // 2
    up, right = (a + 1) % 8, (b + 1) % 16
    down, left = (a + 7) % 8, (b + 15) % 16

    loads = [
        pltpu.make_async_copy(cot_hbm, xhat_ref, load_s.at[0]),
        pltpu.make_async_copy(wo_hbm.at[:, :, :, pl.ds(0, part)], w.at[0, :, :, 0], load_s.at[1]),
        pltpu.make_async_copy(wo_hbm.at[:, :, :, pl.ds(part, part)], w.at[0, :, :, 1], load_s.at[2]),
        pltpu.make_async_copy(wv_hbm, w.at[1], load_s.at[3]),
        pltpu.make_async_copy(wk_hbm, w.at[2], load_s.at[4]),
        pltpu.make_async_copy(wq_hbm, w.at[3], load_s.at[5]),
    ]
    for load in loads:
        load.start()

    peers = [(a, (b + k) % 16) for k in range(1, 16)] + [((a + k) % 8, b) for k in range(1, 8)]
    peers += [(up, right), (down, left)]
    barrier = pltpu.get_barrier_semaphore()
    for peer in peers:
        pl.semaphore_signal(barrier, inc=1, device_id=peer, device_id_type=MESH)

    seats = lax.broadcasted_iota(jnp.int32, (SLOTS, enc_ref.shape[0]), 0)
    to2 = onehot(seats == row_ref[1:2, :])
    sa0[:, :part] = pick(to2, enc_ref[:, :part], NN)
    cells = jnp.broadcast_to(slot_ref[...] + 1, (enc_ref.shape[0], 128)).astype(F32)
    sa0[:, part:] = pick(to2, cells, NN)
    to1 = onehot(seats == row_ref[0:1, :])
    sa1[...] = pick(to1, enc_ref[:, part:], NN)

    pl.semaphore_wait(barrier, len(peers))
    go0 = send_lon(sa0, ra0, lon_s.at[0], lon_r.at[0], a, b)
    go1 = send_lat(sa1, ra1, lat_s.at[0], lat_r.at[0], a, b)

    def halo(tile, land, whole, first):
        moves = (
            (224, 40, land.at[pl.ds(0, 40)], (a, left)), (112, 72, whole.at[pl.ds(72, 72)], (down, b)),
            (184, 40, land.at[pl.ds(40, 40)], (down, b)), (264, 40, land.at[pl.ds(80, 40)], (down, left)),
        )
        return [
            remote(tile.at[pl.ds(row, size)], dst, halo_s.at[first + i], halo_r.at[first + i], device)
            for i, (row, size, dst, device) in enumerate(moves)
        ]

    def settle(tile, land, whole):
        whole[0:72, :] = tile[0:72, :]
        whole[144:180, :] = tile[72:108, :]
        whole[180:216, :] = land[4:40, :]
        whole[216:252, :] = land[40:76, :]
        whole[252:288, :] = land[84:120, :]

    def halo_back(src, tile, first):
        moves = (
            (72, 72, 112, (up, b)), (216, 40, 184, (up, b)), (176, 40, 224, (a, right)), (248, 40, 264, (up, right)),
        )
        copies = [
            remote(src.at[pl.ds(row, size)], tile.at[pl.ds(to, size)], halo_s.at[first + i], halo_r.at[first + i], device)
            for i, (row, size, to, device) in enumerate(moves)
        ]
        tile[0:72, :] = src[0:72, :]
        tile[72:112, :] = src[144:184, :]
        return copies

    place = onehot(lax.broadcasted_iota(jnp.int32, (rows, TROWS), 0) == cell_ref[...])
    loads[0].wait()
    for j in range(0, width, 256):
        tile_g[:, j:j + 256] = pick(place, xhat_ref[:, j:j + 256], TN)
    halo_g = halo(tile_g, land_g, g_ref, 0)

    swap = swap_matrix()
    finish(go0)
    sa0[...] = pick(swap, ra0[...], TN)
    go0 = send_lat(sa0, rb0, lat_s.at[1], lat_r.at[1], a, b)
    finish(go1)
    sa1[...] = pick(swap, ra1[...], NN)
    go1 = send_lon(sa1, rb1, lon_s.at[1], lon_r.at[1], a, b)

    finish(halo_g)
    settle(tile_g, land_g, g_ref)

    def out_weight(i):
        return split(w[0, :, :, i].reshape(inner, part))

    loads[1].wait()
    loads[2].wait()
    datt_ref[...] = dot3(split(g_ref[:, :part]), out_weight(0), NT)
    datt_ref[...] += dot3(split(g_ref[:, part:]), out_weight(1), NT)

    finish(go0)
    table = onehot(rb0[:, part:part + 1] == (cell_ref[...] + 1).astype(F32))
    table2 = dot(swap, table, NN).astype(BF16)
    seen = jnp.sum(table.astype(F32), axis=0, keepdims=True)
    lead = lax.broadcasted_iota(jnp.int32, (16, 1), 0) == 0
    unseen = jnp.where(lead, 1.0 - seen, 0.0).astype(BF16)
    mask = jnp.broadcast_to(mask_ref[...], (16, width))
    tile_t[:, :part] = pick(table, rb0[:, :part], TN) + pick(unseen, mask[:, :part], TN)
    finish(go1)
    tile_t[:, part:] = pick(table2, rb1[...], TN) + pick(unseen, mask[:, part:], TN)
    halo_t = halo(tile_t, land_t, t_ref, 4)
    loads[3].wait()
    loads[4].wait()
    loads[5].wait()
    finish(halo_t)
    settle(tile_t, land_t, t_ref)

    for peer in peers:
        pl.semaphore_signal(free_s, inc=1, device_id=peer, device_id_type=MESH)

    step = 32

    @pl.loop(0, rows // step)
    def _(i):
        r = pl.ds(pl.multiple_of(i * step, step), step)
        t = t_ref[r, :]
        centred = t - jnp.mean(t, axis=-1, keepdims=True)
        rstd = lax.rsqrt(jnp.mean(centred * centred, axis=-1, keepdims=True) + 1e-5)
        xhat = centred * rstd
        xhat_ref[r, :] = xhat
        rstd_ref[r, :] = rstd
        n_hi[r, :], n_lo[r, :] = split(xhat * gain_ref[...])

    for which in range(3):
        for lo in range(0, inner, 256):
            hi = min(lo + 256, inner)
            weight = split(w[3 - which, :, :, :, :, lo:hi].reshape(width, hi - lo))
            qkv_ref[:, which * inner + lo:which * inner + hi] = dot3((n_hi[...], n_lo[...]), weight, NN)

    att_ref[...] = jnp.zeros_like(att_ref)
    dqkv_ref[...] = jnp.zeros_like(dqkv_ref)
    is_last = a == 7
    low_q = lax.broadcasted_iota(jnp.int32, (half, half), 0) >= half // 2
    low_k = lax.broadcasted_iota(jnp.int32, (half, half), 1) >= half // 2
    blocked = jnp.logical_and(low_q != low_k, is_last)
    norm = 1.0 / math.sqrt(HEAD)

    def head(h):
        lo, hi = head_lanes(h)
        lane = lax.broadcasted_iota(jnp.int32, (half, hi - lo), 1) + lo
        return lo, hi, jnp.logical_and(lane >= h * HEAD, lane < (h + 1) * HEAD)

    @pl.loop(0, 2)
    def _(wd):
        r = pl.ds(pl.multiple_of(wd * half, 16), half)
        for h in range(heads):
            lo, hi, mine = head(h)
            q = split(jnp.where(mine, qkv_ref[r, lo:hi] * norm, 0.0))
            k = split(qkv_ref[r, inner + lo:inner + hi])
            v = split(qkv_ref[r, 2 * inner + lo:2 * inner + hi])
            do = split(jnp.where(mine, datt_ref[r, lo:hi], 0.0))
            s = dot3(q, k, NT)
            s = jnp.where(blocked, -1e30, s)
            e = jnp.exp(s - jnp.max(s, axis=-1, keepdims=True))
            p32 = e / jnp.sum(e, axis=-1, keepdims=True)
            p_ref[wd * heads + h] = p32
            p = split(p32)
            att_ref[r, lo:hi] += jnp.where(mine, dot3(p, v, NN), 0.0)
            dqkv_ref[r, 2 * inner + lo:2 * inner + hi] += dot3(p, do, TN)

    att = split(att_ref[...])
    for i in range(2):
        t_ref[:, i * part:(i + 1) * part] += dot3(att, out_weight(i), NN)
    pl.semaphore_wait(free_s, len(peers))
    halo_o = halo_back(t_ref, tile_g, 12)

    sums = [
        Sum(m, (a, b, x, c, y, z), w, acc, r1, r2, r3, r4, r5, fin, sum_s, sum_r) for m in range(4)
    ]

    att3 = jnp.concatenate([att[0], att[0], att[1]], axis=0)
    for i in range(2):
        gh, gl = split(g_ref[:, i * part:(i + 1) * part])
        res = dot(att3, jnp.concatenate([gh, gl, gh], axis=0), TN)
        w[0, :, :, i] = res.reshape(4, 4, SHARD, inner)
    sums[0].begin()

    def grad_rows(which):
        return split(dqkv_ref[:, which * inner:(which + 1) * inner])

    def to_tokens(which, dh, dl, add):
        d3 = jnp.concatenate([dh, dh, dl], axis=1)
        for i in range(2):
            wh, wl = split(w[3 - which, 2 * i:2 * i + 2].reshape(part, inner))
            res = dot(d3, jnp.concatenate([wh, wl, wh], axis=1), NT)
            cols = slice(i * part, (i + 1) * part)
            dn_ref[:, cols] = dn_ref[:, cols] + res if add else res

    def to_weight(which, dh, dl):
        d3 = jnp.concatenate([dh, dl, dh], axis=0)
        for i in range(2):
            cols = slice(i * part, (i + 1) * part)
            nh, nl = n_hi[:, cols], n_lo[:, cols]
            res = dot(jnp.concatenate([nh, nh, nl], axis=0), d3, TN)
            w[3 - which, 2 * i:2 * i + 2] = res.reshape(2, 4, 2, SHARD, inner)

    dh, dl = grad_rows(2)
    to_tokens(2, dh, dl, False)
    to_weight(2, dh, dl)
    sums[1].begin()
    sums[0].step()

    @pl.loop(0, 2)
    def _(wd):
        r = pl.ds(pl.multiple_of(wd * half, 16), half)
        for h in range(heads):
            lo, hi, mine = head(h)
            q = split(jnp.where(mine, qkv_ref[r, lo:hi] * norm, 0.0))
            k = split(qkv_ref[r, inner + lo:inner + hi])
            v = split(qkv_ref[r, 2 * inner + lo:2 * inner + hi])
            do = split(jnp.where(mine, datt_ref[r, lo:hi], 0.0))
            p32 = p_ref[wd * heads + h]
            dp = dot3(do, v, NT)
            ds = split(p32 * (dp - jnp.sum(dp * p32, axis=-1, keepdims=True)))
            dqkv_ref[r, lo:hi] += jnp.where(mine, dot3(ds, k, NN) * norm, 0.0)
            dqkv_ref[r, inner + lo:inner + hi] += dot3(ds, q, TN)

    sums[1].step()
    kh, kl = grad_rows(1)
    to_tokens(1, kh, kl, True)
    qh, ql = grad_rows(0)
    to_tokens(0, qh, ql, True)

    vec_ref[...] = jnp.zeros_like(vec_ref)

    @pl.loop(0, rows // step)
    def _(i):
        r = pl.ds(pl.multiple_of(i * step, step), step)
        dn = dn_ref[r, :]
        xhat = xhat_ref[r, :]
        vec_ref[1:2, :] += jnp.sum(dn * xhat, axis=0, keepdims=True)
        dx = dn * gain_ref[...]
        m1 = jnp.mean(dx, axis=-1, keepdims=True)
        m2 = jnp.mean(dx * xhat, axis=-1, keepdims=True)
        g_ref[r, :] += rstd_ref[r, :] * (dx - m1 - xhat * m2)

    halo_d = halo_back(g_ref, tile_t, 8)

    to_weight(1, kh, kl)
    sums[2].begin()
    sums[0].step()
    sums[1].step()
    to_weight(0, qh, ql)
    sums[3].begin()
    sums[2].step()

    finish(halo_d)
    sa1[...] = pick(table, tile_t[:, :part], NN)
    back0 = send_lat(sa1, ra1, lat_s.at[2], lat_r.at[2], a, b)
    sa0[:, :part] = pick(table2, tile_t[:, part:], NN)
    back1 = send_lon(sa0, ra0, lon_s.at[2], lon_r.at[2], a, b, part)
    sums[3].step()
    masked = jnp.where(cell_ref[...] >= 0, 1.0 - seen, 0.0)
    masked = jnp.where(lead, masked, 0.0)[:8].astype(BF16)
    vec_ref[...] += pick(masked, tile_t[...], NN)

    vec_devices = [
        (a + 1 - 2 * c, b), (flip_low(x) * 2 + c, b), (flip_far(x) * 2 + c, b),
        (a, flip_low(y) * 4 + z), (a, flip_far(y) * 4 + z), (a, y * 4 + flip_low(z)), (a, y * 4 + flip_far(z)),
    ]
    vec_copies = []

    def vec_begin(k):
        vec_copies.append(remote(vec_ref, vr.at[k], vec_s.at[k], vec_r.at[k], vec_devices[k]))

    def vec_step():
        k = len(vec_copies) - 1
        vec_copies[k].wait()
        vec_ref[...] += vr[k]
        if k < 6:
            vec_begin(k + 1)

    vec_begin(0)
    sums[0].step()
    sums[1].step()

    finish(halo_o)
    for j in range(0, width, 256):
        xhat_ref[:, j:j + 256] = pick(place, tile_g[:, j:j + 256], NN)
    store = pltpu.make_async_copy(xhat_ref, decoded_hbm, load_s.at[0])
    store.start()

    sums[0].step()
    sums[1].step()
    vec_step()

    finish(back0)
    sa1[...] = pick(swap, ra1[...], NN)
    back0 = send_lon(sa1, rb1, lon_s.at[3], lon_r.at[3], a, b)
    finish(back1)
    sa0[:, :part] = pick(swap, ra0[:, :part], TN)
    back1 = send_lat(sa0, rb0, lat_s.at[3], lat_r.at[3], a, b, part)

    sums[2].step()
    sums[3].step()
    sums[0].step()
    sums[1].step()
    vec_step()
    sums[2].step()
    sums[3].step()
    sums[0].step()
    sums[1].step()
    vec_step()

    finish(back0)
    finish(back1)
    slots = lax.broadcasted_iota(jnp.int32, (denc_ref.shape[0], SLOTS), 1)
    denc_ref[:, :part] = pick(onehot(slots == index_ref[:, 1:2]), rb1[...], NN)
    denc_ref[:, part:] = pick(onehot(slots == index_ref[:, 0:1]), rb0[:, :part], NN)

    while any(total.stage < 8 for total in sums):
        front = min(total.stage for total in sums)
        for total in sums:
            if total.stage == front:
                total.step()
        if len(vec_copies) < 7:
            vec_step()
    while len(vec_copies) < 7:
        vec_step()
    vec_step()
    vec_ref[...] = vec_ref[...] * SCALE
    do_ref[:, :part] = fin[0, 0]
    do_ref[:, part:] = fin[0, 1]
    dv_ref[...] = fin[1]
    dk_ref[...] = fin[2]
    dq_ref[...] = fin[3]
    store.wait()


def decoder_step(cell, row, index, slot, enc, mask, gain, cot, wq, wk, wv, wo):
    rows, width = cot.shape
    part = width // 2
    inner = wo.shape[2] * 16
    vm = pl.BlockSpec(memory_space=pltpu.VMEM)
    anyspace = pl.BlockSpec(memory_space=pl.ANY)
    f = jax.ShapeDtypeStruct
    dma = pltpu.SemaphoreType.DMA
    v = pltpu.VMEM
    third = f((2, SHARD, inner), F32)
    return pl.pallas_call(
        step_kernel,
        out_shape=(
            f((rows, width), F32), third, third, third, f((SHARD, width), F32), f((8, width), F32),
            f((enc.shape[0], width), F32),
        ),
        in_specs=[vm] * 7 + [anyspace] * 5,
        out_specs=[anyspace] + [vm] * 6,
        scratch_shapes=[
            v((4, 4, 4, 2, SHARD, inner), F32), v((4, 4, 4, SHARD, inner), F32),
            v((4, 2, 2, 2, SHARD, inner), F32), v((4, 2, 2, SHARD, inner), F32),
            v((4, 2, SHARD, inner), F32), v((4, SHARD, inner), F32), v((4, 2, SHARD, inner), F32),
            v((4, 2, SHARD, inner), F32), v((7, 8, width), F32),
            v((TROWS, width), F32), v((TROWS, width), F32), v((120, width), F32), v((120, width), F32),
            v((SLOTS, part + 128), F32), v((SLOTS, part + 128), F32), v((SLOTS, part + 128), F32),
            v((SLOTS, part), F32), v((SLOTS, part), F32), v((SLOTS, part), F32),
            v((rows, width), F32), v((rows, width), F32), v((rows, width), F32), v((rows, width), F32),
            v((rows, 1), F32), v((rows, width), BF16), v((rows, width), BF16),
            v((rows, 3 * inner), F32), v((2 * inner // HEAD, rows // 2, rows // 2), F32),
            v((rows, inner), F32), v((rows, inner), F32), v((rows, 3 * inner), F32),
            dma((6,)), dma((16,)), dma((16,)), dma((4, 15)), dma((4, 15)), dma((4, 7)), dma((4, 7)),
            dma((4, 18)), dma((4, 18)), dma((7,)), dma((7,)), pltpu.SemaphoreType.REGULAR,
        ],
        compiler_params=pltpu.CompilerParams(
            vmem_limit_bytes=63 * 2**20, collective_id=0, has_side_effects=True
        ),
        name="decoder_step",
    )(cell, row, index, slot, enc, mask, gain, cot, wq, wk, wv, wo)


def body(positions, encoded, mask_token, norm_gain, w_query, w_key, w_value, w_out, cotangent):
    tile_rows, tile_cols, model_width = cotangent.shape
    lat_count = lax.axis_size("lat")
    lon_count = lax.axis_size("lon")
    devices = lat_count * lon_count
    grid_lat = lat_count * tile_rows
    grid_lon = lon_count * tile_cols
    tile_size = tile_rows * tile_cols
    capacity = tile_size // devices
    lat_cell = positions // grid_lon
    lon_cell = positions % grid_lon
    target = lat_cell // tile_rows * lon_count + lon_cell // tile_cols
    cell_slot = lat_cell % tile_rows * tile_cols + lon_cell % tile_cols
    serial = jnp.arange(positions.shape[0])
    earlier = jnp.logical_and(target[None, :] == target[:, None], serial[None, :] < serial[:, None])
    rank = jnp.sum(earlier.astype(jnp.int32), axis=1)
    buffer_index = target * capacity + rank
    index2 = (target % lon_count) * (lat_count * capacity) + (target // lon_count) * capacity + rank
    row = jnp.stack([buffer_index, index2], axis=0)
    tile_map = jnp.asarray(tile_rows_map())[None]
    share = model_width // lon_count
    shard = (lon_count // 4, 4, 2, share // 2, -1)
    decoded, grad_query, grad_key, grad_value, grad_out, vec, grad_encoded = decoder_step(
        tile_map, row, row.T, cell_slot[:, None], encoded, mask_token[None], norm_gain[None],
        cotangent.reshape(tile_size, model_width), w_query.reshape(shard), w_key.reshape(shard),
        w_value.reshape(shard), w_out.reshape(lon_count // 4, 4, share // 2, model_width),
    )
    own = lax.dynamic_slice(vec, (0, lax.axis_index("lon") * share), (2, share))
    matrices = (g.reshape(share, -1) for g in (grad_query, grad_key, grad_value))
    return (decoded.reshape(cotangent.shape), *matrices, grad_out, own[0], own[1], grad_encoded)


def solution(mesh):
    return jax.shard_map(
        body,
        mesh=mesh,
        in_specs=(
            P(("lat", "lon")),
            P(("lat", "lon"), None),
            P(),
            P(),
            P(),
            P(),
            P(),
            P(),
            P("lat", "lon", None),
        ),
        out_specs=(
            P("lat", "lon", None),
            P("lon", None),
            P("lon", None),
            P("lon", None),
            P("lon", None),
            P("lon"),
            P("lon"),
            P(("lat", "lon"), None),
        ),
        check_vma=False,
    )
```

```python
import functools, math
import jax, jax.numpy as jnp
import numpy as np
from jax import lax
from jax.experimental import pallas as pl
from jax.experimental.pallas import tpu as pltpu
from jax.sharding import PartitionSpec as P

HEAD = 80
F32 = jnp.float32
BF16 = jnp.bfloat16


def split(x):
    hi = x.astype(BF16)
    return hi, (x - hi.astype(F32)).astype(BF16)


NN = (((1,), (0,)), ((), ()))
NT = (((1,), (1,)), ((), ()))
TN = (((0,), (0,)), ((), ()))


def dot(a, b, dims):
    return lax.dot_general(a, b, dims, preferred_element_type=F32)


def dot3(a, b, dims):
    return dot(a[0], b[0], dims) + (dot(a[0], b[1], dims) + dot(a[1], b[0], dims))


def head_lanes(h):
    low = h * HEAD // 128 * 128
    high = -(-(h + 1) * HEAD // 128) * 128
    return low, high


MESH = pl.DeviceIdType.MESH
SLOTS = 256
TROWS = 304
SHARD = 40
SCALE = 1.0 / 192.0


def tile_rows_map():
    def block(r0, c0, cols):
        return [(r0 + i) * 24 + c0 + j for i in range(6) for j in range(cols)]

    none = [-5] * 4
    order = block(6, 6, 12) + block(6, 18, 6) + none + block(0, 6, 12) + block(0, 18, 6) + none
    order += none + block(6, 0, 6) + none + block(0, 0, 6)
    return np.array(order, np.int32)


def split3(x):
    hi = x.astype(BF16)
    rest = x - hi.astype(F32)
    mid = rest.astype(BF16)
    return hi, mid, (rest - mid.astype(F32)).astype(BF16)


def pick(onehot, x, dims):
    hi, mid, lo = split3(x)
    return (dot(onehot, hi, dims) + dot(onehot, mid, dims)) + dot(onehot, lo, dims)


def onehot(cond):
    return jnp.where(cond, 1.0, 0.0).astype(BF16)


def swap_matrix():
    j = lax.broadcasted_iota(jnp.int32, (SLOTS, SLOTS), 0)
    i = lax.broadcasted_iota(jnp.int32, (SLOTS, SLOTS), 1)
    b = jnp.right_shift(j, 4)
    a = jnp.bitwise_and(jnp.right_shift(j, 1), 7)
    return onehot(i == a * 32 + b * 2 + jnp.bitwise_and(j, 1))


def flip_low(i):
    return i + 1 - 2 * (i % 2)


def flip_far(i):
    return 3 - i


def remote(src, dst, send, recv, device):
    copy = pltpu.make_async_remote_copy(
        src_ref=src, dst_ref=dst, send_sem=send, recv_sem=recv, device_id=device, device_id_type=MESH
    )
    copy.start()
    return copy


def rows_at(start, size):
    return pl.ds(pl.multiple_of(start, size), size)


def send_lon(src, dst, send, recv, a, b, lanes=None):
    cols = pl.ds(0, lanes or src.shape[1])
    copies = []
    for k in range(1, 16):
        peer = (b + k) % 16
        copies.append(remote(
            src.at[rows_at(peer * 16, 16), cols], dst.at[rows_at(b * 16, 16), cols], send.at[k - 1], recv.at[k - 1], (a, peer)
        ))
    dst[rows_at(b * 16, 16), :] = src[rows_at(b * 16, 16), :]
    return copies


def send_lat(src, dst, send, recv, a, b, lanes=None):
    cols = pl.ds(0, lanes or src.shape[1])
    copies = []
    for k in range(1, 8):
        peer = (a + k) % 8
        copies.append(remote(
            src.at[rows_at(peer * 32, 32), cols], dst.at[rows_at(a * 32, 32), cols], send.at[k - 1], recv.at[k - 1], (peer, b)
        ))
    dst[rows_at(a * 32, 32), :] = src[rows_at(a * 32, 32), :]
    return copies


def finish(copies):
    for copy in copies:
        copy.wait()


class Sum:
    def __init__(self, m, home, place, w, acc, r1, r2, r3, r4, r5, fin, send_sem, recv_sem):
        self.m, self.home, self.place = m, home, place
        self.w, self.acc, self.r = w, acc, (r1, r2, r3, r4, r5)
        self.fin, self.send_sem, self.recv_sem = fin, send_sem, recv_sem
        self.first = m % 2 == 0
        self.stage, self.slot, self.copies = 0, 0, []

    def chunk(self, i, half):
        rest = pl.ds(2 * half, 2)
        return (self.m, i, rest) if self.first else (self.m, rest, i)

    def piece(self, i, half):
        a, b, x, c, y, z = self.place
        rows = pl.ds(0, 24) if half == 0 else pl.ds(24, 16)
        return (self.m, y, i, rows) if self.first else (self.m, i, z, rows)

    def near(self, ring, i):
        a, b, x, c, y, z = self.place
        return (a, i * 4 + z) if ring == self.first else (a, y * 4 + i)

    def send(self, src, dst, device):
        k = self.slot
        self.slot += 1
        self.copies.append(remote(src, dst, self.send_sem.at[self.m, k], self.recv_sem.at[self.m, k], device))

    def begin(self):
        a, b, x, c, y, z = self.place
        m, acc, (r1, r2, r3, r4, r5) = self.m, self.acc, self.r
        me1, me2 = (y, z) if self.first else (z, y)
        s = self.stage
        if s == 0:
            self.send(self.w.at[self.home, :, :, 1 - c], acc.at[m], (a + 1 - 2 * c, b))
            return
        if s == 7:
            self.send(self.fin.at[m, c], self.fin.at[m, c], (a + 1 - 2 * c, b))
            return
        for half in range(2):
            q1, q2 = (flip_low, flip_far) if half == 0 else (flip_far, flip_low)
            rows = pl.ds(0, 24) if half == 0 else pl.ds(24, 16)
            if s == 1:
                p = q1(me1)
                self.send(acc.at[self.chunk(p, half)], r1.at[m, 0, half], self.near(True, p))
                self.send(acc.at[self.chunk(q2(p), half)], r1.at[m, 1, half], self.near(True, p))
            elif s == 2:
                p = q2(me1)
                self.send(acc.at[self.chunk(p, half)], r2.at[m, half], self.near(True, p))
            elif s == 3:
                p = q1(me2)
                self.send(acc.at[self.piece(p, half)], r3.at[m, 0, rows], self.near(False, p))
                self.send(acc.at[self.piece(q2(p), half)], r3.at[m, 1, rows], self.near(False, p))
            elif s == 4:
                p = q2(me2)
                self.send(acc.at[self.piece(p, half)], r4.at[m, rows], self.near(False, p))
            elif s == 5:
                self.send(acc.at[self.piece(me2, half)], r5.at[m, 0, rows], (q1(x) * 2 + c, b))
            elif s == 6:
                self.send(acc.at[self.piece(me2, half)], r5.at[m, 1, rows], (q2(x) * 2 + c, b))

    def end(self):
        a, b, x, c, y, z = self.place
        m, acc, (r1, r2, r3, r4, r5) = self.m, self.acc, self.r
        me1, me2 = (y, z) if self.first else (z, y)
        s = self.stage
        finish(self.copies)
        self.copies = []
        if s == 0:
            @pl.loop(0, 4)
            def _(i):
                acc[m, i] += self.w[self.home, i, :, c]
        for half in range(2):
            q2 = flip_far if half == 0 else flip_low
            rows = pl.ds(0, 24) if half == 0 else pl.ds(24, 16)
            if s == 1:
                acc[self.chunk(me1, half)] += r1[m, 0, half]
                acc[self.chunk(q2(me1), half)] += r1[m, 1, half]
            elif s == 2:
                acc[self.chunk(me1, half)] += r2[m, half]
            elif s == 3:
                acc[self.piece(me2, half)] += r3[m, 0, rows]
                acc[self.piece(q2(me2), half)] += r3[m, 1, rows]
            elif s == 4:
                acc[self.piece(me2, half)] += r4[m, rows]
            elif s == 5:
                acc[self.piece(me2, half)] += r5[m, 0, rows]
            elif s == 6:
                self.fin[m, c, rows] = (acc[self.piece(me2, half)] + r5[m, 1, rows]) * SCALE
        self.stage += 1

    def step(self):
        self.end()
        if self.stage < 8:
            self.begin()


def step_kernel(
    cell_ref, pos_ref, enc_ref, mask_ref, gain_ref, cot_hbm, wq_hbm, wk_hbm, wv_hbm, wo_hbm,
    decoded_hbm, dq_ref, dk_ref, dv_ref, do_ref, denc_ref, own_ref,
    w, w_hi, w_lo, o_hi, o_lo, acc, r1, r2, r3, r4, r5, fin, vr,
    tile_t, tile_g, land_t, land_g, sa0, ra0, rb0, sa1, ra1, rb1,
    t_ref, g_ref, xhat_ref, dn_ref, rstd_ref, n_hi, n_lo, qkv_ref, p_ref, att_ref, datt_ref, dqkv_ref,
    vec_ref, load_s, halo_s, halo_r, lon_s, lon_r, lat_s, lat_r, sum_s, sum_r, vec_s, vec_r, free_s,
):
    a, b = lax.axis_index("lat"), lax.axis_index("lon")
    x, c = a // 2, a % 2
    y, z = b // 4, b % 4
    rows, width = t_ref.shape
    inner = att_ref.shape[1]
    part = width // 2
    heads = inner // HEAD
    half = rows // 2
    up, right = (a + 1) % 8, (b + 1) % 16
    down, left = (a + 7) % 8, (b + 15) % 16

    load_cot = pltpu.make_async_copy(cot_hbm, xhat_ref, load_s.at[0])
    load_o = [
        pltpu.make_async_copy(wo_hbm.at[:, :, :, pl.ds(i * part, part)], w.at[0, :, :, i], load_s.at[1 + i])
        for i in range(2)
    ]
    load_v = pltpu.make_async_copy(wv_hbm, w.at[1], load_s.at[3])
    load_k = pltpu.make_async_copy(wk_hbm, w.at[0], load_s.at[4])
    load_q = pltpu.make_async_copy(wq_hbm, w.at[1], load_s.at[5])
    load_cot.start()
    load_o[0].start()
    load_o[1].start()
    load_v.start()

    def take_weight(load, home, which):
        load.wait()

        @pl.loop(0, 16)
        def _(i):
            r = pl.ds(pl.multiple_of(i * 80, 80), 80)
            cols = slice(which * inner, (which + 1) * inner)
            w_hi[r, cols], w_lo[r, cols] = split(w[home, i // 4, i % 4].reshape(80, inner))

    peers = [(a, (b + k) % 16) for k in range(1, 16)] + [((a + k) % 8, b) for k in range(1, 8)]
    peers += [(up, right), (down, left)]
    barrier = pltpu.get_barrier_semaphore()
    for peer in peers:
        pl.semaphore_signal(barrier, inc=1, device_id=peer, device_id_type=MESH)

    count = enc_ref.shape[0]
    pos = pos_ref[...].astype(F32)
    lat = jnp.floor((pos + 0.5) * (1.0 / 384.0))
    lon = pos - lat * 384.0
    tile_a = jnp.floor((lat + 0.5) * (1.0 / 12.0))
    tile_b = jnp.floor((lon + 0.5) * (1.0 / 24.0))
    cell = (lat - tile_a * 12.0) * 24.0 + lon - tile_b * 24.0
    target = tile_a * 16.0 + tile_b
    line = lax.broadcasted_iota(jnp.int32, (count, count), 0)
    lane = lax.broadcasted_iota(jnp.int32, (count, count), 1)

    def column(v):
        return jnp.sum(jnp.where(line == lane, v, 0.0), axis=1, keepdims=True)

    earlier = jnp.logical_and(column(target) == target, line < lane)
    rank = jnp.sum(jnp.where(earlier, 1.0, 0.0), axis=0, keepdims=True)
    index1 = target * 2.0 + rank
    index2 = tile_b * 16.0 + tile_a * 2.0 + rank
    column1, column2 = column(index1), column(index2)

    seats = lax.broadcasted_iota(jnp.int32, (SLOTS, count), 0).astype(F32)
    to2 = onehot(seats == index2)
    sa0[:, :part] = pick(to2, enc_ref[:, :part], NN)
    sa0[:, part:] = pick(to2, jnp.broadcast_to(column(cell) + 1.0, (count, 128)), NN)
    to1 = onehot(seats == index1)
    sa1[...] = pick(to1, enc_ref[:, part:], NN)

    pl.semaphore_wait(barrier, len(peers))
    go0 = send_lon(sa0, ra0, lon_s.at[0], lon_r.at[0], a, b)
    go1 = send_lat(sa1, ra1, lat_s.at[0], lat_r.at[0], a, b)

    def halo(tile, land, whole, first):
        moves = (
            (224, 40, land.at[pl.ds(0, 40)], (a, left)), (112, 72, whole.at[pl.ds(72, 72)], (down, b)),
            (184, 40, land.at[pl.ds(40, 40)], (down, b)), (264, 40, land.at[pl.ds(80, 40)], (down, left)),
        )
        return [
            remote(tile.at[pl.ds(row, size)], dst, halo_s.at[first + i], halo_r.at[first + i], device)
            for i, (row, size, dst, device) in enumerate(moves)
        ]

    def settle(tile, land, whole):
        whole[0:72, :] = tile[0:72, :]
        whole[144:180, :] = tile[72:108, :]
        whole[180:216, :] = land[4:40, :]
        whole[216:252, :] = land[40:76, :]
        whole[252:288, :] = land[84:120, :]

    def halo_back(src, tile, first):
        moves = (
            (72, 72, 112, (up, b)), (216, 40, 184, (up, b)), (176, 40, 224, (a, right)), (248, 40, 264, (up, right)),
        )
        copies = [
            remote(src.at[pl.ds(row, size)], tile.at[pl.ds(to, size)], halo_s.at[first + i], halo_r.at[first + i], device)
            for i, (row, size, to, device) in enumerate(moves)
        ]
        tile[0:72, :] = src[0:72, :]
        tile[72:112, :] = src[144:184, :]
        return copies

    place = onehot(lax.broadcasted_iota(jnp.int32, (rows, TROWS), 0) == cell_ref[...])
    load_cot.wait()
    for j in range(0, width, 256):
        tile_g[:, j:j + 256] = pick(place, xhat_ref[:, j:j + 256], TN)

    load_o[0].wait()
    load_o[1].wait()
    for i in range(2):
        for j in range(4):
            r = slice(j * 160, (j + 1) * 160)
            o_hi[i, r, :], o_lo[i, r, :] = split(w[0, j, :, i].reshape(160, part))
    load_k.start()
    take_weight(load_v, 1, 2)
    load_q.start()

    swap = swap_matrix()
    finish(go0)
    sa0[...] = pick(swap, ra0[...], TN)
    go0 = send_lat(sa0, rb0, lat_s.at[1], lat_r.at[1], a, b)
    finish(go1)
    sa1[...] = pick(swap, ra1[...], NN)
    go1 = send_lon(sa1, rb1, lon_s.at[1], lon_r.at[1], a, b)

    take_weight(load_k, 0, 1)
    take_weight(load_q, 1, 0)

    def out_weight(i):
        return o_hi[i], o_lo[i]

    finish(go0)
    table = onehot(rb0[:, part:part + 1] == (cell_ref[...] + 1).astype(F32))
    table2 = dot(swap, table, NN).astype(BF16)
    seen = jnp.sum(table.astype(F32), axis=0, keepdims=True)
    lead = lax.broadcasted_iota(jnp.int32, (16, 1), 0) == 0
    unseen = jnp.where(lead, 1.0 - seen, 0.0).astype(BF16)
    mask = jnp.broadcast_to(jnp.concatenate([mask_ref[i:i + 1, :] for i in range(10)], axis=1), (16, width))
    gain = jnp.concatenate([gain_ref[i:i + 1, :] for i in range(10)], axis=1)
    tile_t[:, :part] = pick(table, rb0[:, :part], TN) + pick(unseen, mask[:, :part], TN)
    finish(go1)
    tile_t[:, part:] = pick(table2, rb1[...], TN) + pick(unseen, mask[:, part:], TN)
    halo_t = halo(tile_t, land_t, t_ref, 4)
    finish(halo_t)
    halo_g = halo(tile_g, land_g, g_ref, 0)
    settle(tile_t, land_t, t_ref)

    step = 32

    @pl.loop(0, rows // step)
    def _(i):
        r = pl.ds(pl.multiple_of(i * step, step), step)
        t = t_ref[r, :]
        centred = t - jnp.mean(t, axis=-1, keepdims=True)
        rstd = lax.rsqrt(jnp.mean(centred * centred, axis=-1, keepdims=True) + 1e-5)
        xhat = centred * rstd
        xhat_ref[r, :] = xhat
        rstd_ref[r, :] = rstd
        n_hi[r, :], n_lo[r, :] = split(xhat * gain)

    @pl.loop(0, 3 * inner // 256)
    def _(j):
        cols = pl.ds(pl.multiple_of(j * 256, 256), 256)
        qkv_ref[:, cols] = dot3((n_hi[...], n_lo[...]), (w_hi[:, cols], w_lo[:, cols]), NN)

    qkv_ref[:, 1792:] = dot3((n_hi[...], n_lo[...]), (w_hi[:, 1792:], w_lo[:, 1792:]), NN)

    finish(halo_g)
    settle(tile_g, land_g, g_ref)

    for peer in peers:
        pl.semaphore_signal(free_s, inc=1, device_id=peer, device_id_type=MESH)

    datt_ref[...] = dot3(split(g_ref[:, :part]), out_weight(0), NT)
    datt_ref[...] += dot3(split(g_ref[:, part:]), out_weight(1), NT)

    att_ref[...] = jnp.zeros_like(att_ref)
    dqkv_ref[...] = jnp.zeros_like(dqkv_ref)
    is_last = a == 7
    low_q = lax.broadcasted_iota(jnp.int32, (half, half), 0) >= half // 2
    low_k = lax.broadcasted_iota(jnp.int32, (half, half), 1) >= half // 2
    blocked = jnp.logical_and(low_q != low_k, is_last)
    norm = 1.0 / math.sqrt(HEAD)

    def head(h):
        lo, hi = head_lanes(h)
        lane = lax.broadcasted_iota(jnp.int32, (half, hi - lo), 1) + lo
        return lo, hi, jnp.logical_and(lane >= h * HEAD, lane < (h + 1) * HEAD)

    @pl.loop(0, 2)
    def _(wd):
        r = pl.ds(pl.multiple_of(wd * half, 16), half)
        for h in range(heads):
            lo, hi, mine = head(h)
            q = split(jnp.where(mine, qkv_ref[r, lo:hi] * norm, 0.0))
            k = split(qkv_ref[r, inner + lo:inner + hi])
            v = split(qkv_ref[r, 2 * inner + lo:2 * inner + hi])
            do = split(jnp.where(mine, datt_ref[r, lo:hi], 0.0))
            s = dot3(q, k, NT)
            s = jnp.where(blocked, -1e30, s)
            e = jnp.exp(s - jnp.max(s, axis=-1, keepdims=True))
            p32 = e / jnp.sum(e, axis=-1, keepdims=True)
            p_ref[wd * heads + h] = p32
            p = split(p32)
            att_ref[r, lo:hi] += jnp.where(mine, dot3(p, v, NN), 0.0)
            dqkv_ref[r, 2 * inner + lo:2 * inner + hi] += dot3(p, do, TN)

    att = split(att_ref[...])
    for i in range(2):
        t_ref[:, i * part:(i + 1) * part] += dot3(att, out_weight(i), NN)
    pl.semaphore_wait(free_s, len(peers))
    halo_o = halo_back(t_ref, tile_g, 12)

    sums = [
        Sum(m, m % 2, (a, b, x, c, y, z), w, acc, r1, r2, r3, r4, r5, fin, sum_s, sum_r) for m in range(4)
    ]

    att3 = jnp.concatenate([att[0], att[0], att[1]], axis=0)
    for i in range(2):
        gh, gl = split(g_ref[:, i * part:(i + 1) * part])
        res = dot(att3, jnp.concatenate([gh, gl, gh], axis=0), TN)
        w[0, :, :, i] = res.reshape(4, 4, SHARD, inner)
    sums[0].begin()

    def grad_rows(which):
        return split(dqkv_ref[:, which * inner:(which + 1) * inner])

    def to_tokens(which, dh, dl, add):
        d3 = jnp.concatenate([dh, dh, dl], axis=1)
        cols = slice(which * inner, (which + 1) * inner)
        for lo in range(0, width, 256):
            r = slice(lo, lo + 256)
            wh, wl = w_hi[r, cols], w_lo[r, cols]
            res = dot(d3, jnp.concatenate([wh, wl, wh], axis=1), NT)
            dn_ref[:, r] = dn_ref[:, r] + res if add else res

    def to_weight(which, dh, dl):
        d3 = jnp.concatenate([dh, dl, dh], axis=0)
        for i in range(2):
            cols = slice(i * part, (i + 1) * part)
            nh, nl = n_hi[:, cols], n_lo[:, cols]
            res = dot(jnp.concatenate([nh, nh, nl], axis=0), d3, TN)
            w[(3 - which) % 2, 2 * i:2 * i + 2] = res.reshape(2, 4, 2, SHARD, inner)

    dh, dl = grad_rows(2)
    to_weight(2, dh, dl)
    sums[1].begin()
    sums[0].step()
    to_tokens(2, dh, dl, False)
    sums[1].step()

    @pl.loop(0, 2)
    def _(wd):
        r = pl.ds(pl.multiple_of(wd * half, 16), half)
        for h in range(heads):
            lo, hi, mine = head(h)
            q = split(jnp.where(mine, qkv_ref[r, lo:hi] * norm, 0.0))
            k = split(qkv_ref[r, inner + lo:inner + hi])
            v = split(qkv_ref[r, 2 * inner + lo:2 * inner + hi])
            do = split(jnp.where(mine, datt_ref[r, lo:hi], 0.0))
            p32 = p_ref[wd * heads + h]
            dp = dot3(do, v, NT)
            ds = split(p32 * (dp - jnp.sum(dp * p32, axis=-1, keepdims=True)))
            dqkv_ref[r, lo:hi] += jnp.where(mine, dot3(ds, k, NN) * norm, 0.0)
            dqkv_ref[r, inner + lo:inner + hi] += dot3(ds, q, TN)

    kh, kl = grad_rows(1)
    to_weight(1, kh, kl)
    sums[2].begin()
    sums[0].step()
    qh, ql = grad_rows(0)
    to_weight(0, qh, ql)
    sums[3].begin()
    sums[2].step()
    sums[1].step()
    to_tokens(1, kh, kl, True)
    sums[3].step()
    sums[0].step()
    to_tokens(0, qh, ql, True)
    sums[1].step()

    vec_ref[...] = jnp.zeros_like(vec_ref)

    @pl.loop(0, rows // step)
    def _(i):
        r = pl.ds(pl.multiple_of(i * step, step), step)
        dn = dn_ref[r, :]
        xhat = xhat_ref[r, :]
        vec_ref[1:2, :] += jnp.sum(dn * xhat, axis=0, keepdims=True)
        dx = dn * gain
        m1 = jnp.mean(dx, axis=-1, keepdims=True)
        m2 = jnp.mean(dx * xhat, axis=-1, keepdims=True)
        g_ref[r, :] += rstd_ref[r, :] * (dx - m1 - xhat * m2)

    halo_d = halo_back(g_ref, tile_t, 8)

    sums[0].step()
    sums[1].step()

    finish(halo_o)
    for j in range(0, width, 256):
        xhat_ref[:, j:j + 256] = pick(place, tile_g[:, j:j + 256], NN)
    store = pltpu.make_async_copy(xhat_ref, decoded_hbm, load_s.at[0])
    store.start()
    sums[2].step()
    sums[3].step()

    finish(halo_d)
    sa1[...] = pick(table, tile_t[:, :part], NN)
    back0 = send_lat(sa1, ra1, lat_s.at[2], lat_r.at[2], a, b)
    sa0[:, :part] = pick(table2, tile_t[:, part:], NN)
    back1 = send_lon(sa0, ra0, lon_s.at[2], lon_r.at[2], a, b, part)
    masked = jnp.where(cell_ref[...] >= 0, 1.0 - seen, 0.0)
    masked = jnp.where(lead, masked, 0.0)[:8].astype(BF16)
    vec_ref[...] += pick(masked, tile_t[...], NN)

    vec_devices = [
        (a + 1 - 2 * c, b), (flip_low(x) * 2 + c, b), (flip_far(x) * 2 + c, b),
        (a, flip_low(y) * 4 + z), (a, flip_far(y) * 4 + z), (a, y * 4 + flip_low(z)), (a, y * 4 + flip_far(z)),
    ]
    vec_copies = []

    def vec_begin(k):
        vec_copies.append(remote(vec_ref, vr.at[k], vec_s.at[k], vec_r.at[k], vec_devices[k]))

    def vec_step():
        k = len(vec_copies) - 1
        vec_copies[k].wait()
        vec_ref[...] += vr[k]
        if k < 6:
            vec_begin(k + 1)

    vec_begin(0)
    sums[0].step()
    sums[1].step()
    sums[2].step()
    sums[3].step()
    vec_step()

    finish(back0)
    sa1[...] = pick(swap, ra1[...], NN)
    back0 = send_lon(sa1, rb1, lon_s.at[3], lon_r.at[3], a, b)
    finish(back1)
    sa0[:, :part] = pick(swap, ra0[:, :part], TN)
    back1 = send_lat(sa0, rb0, lat_s.at[3], lat_r.at[3], a, b, part)

    for _ in range(2):
        for total in sums:
            if total.stage < 8:
                total.step()
        vec_step()

    finish(back0)
    finish(back1)
    slots = lax.broadcasted_iota(jnp.int32, (count, SLOTS), 1).astype(F32)
    denc_ref[:, :part] = pick(onehot(slots == column2), rb1[...], NN)
    denc_ref[:, part:] = pick(onehot(slots == column1), rb0[:, :part], NN)

    while any(total.stage < 8 for total in sums):
        front = min(total.stage for total in sums)
        for total in sums:
            if total.stage == front:
                total.step()
        if len(vec_copies) < 7:
            vec_step()
    while len(vec_copies) < 7:
        vec_step()
    vec_step()
    lanes = lax.broadcasted_iota(jnp.int32, (width, 128), 1)
    mine = jnp.logical_and(lax.broadcasted_iota(jnp.int32, (width, 128), 0) == b * 80 + lanes, lanes < 80)
    mine = onehot(mine)
    hi, mid, lo = split3(vec_ref[...] * SCALE)
    own_ref[...] = (dot(hi, mine, NN) + dot(mid, mine, NN)) + dot(lo, mine, NN)
    do_ref[:, :part] = fin[0, 0]
    do_ref[:, part:] = fin[0, 1]
    dv_ref[...] = fin[1]
    dk_ref[...] = fin[2]
    dq_ref[...] = fin[3]
    store.wait()


def decoder_step(cell, pos, enc, mask, gain, cot, wq, wk, wv, wo):
    rows, width = cot.shape
    part = width // 2
    inner = wo.shape[2] * 16
    vm = pl.BlockSpec(memory_space=pltpu.VMEM)
    anyspace = pl.BlockSpec(memory_space=pl.ANY)
    f = jax.ShapeDtypeStruct
    dma = pltpu.SemaphoreType.DMA
    v = pltpu.VMEM
    third = f((2, SHARD, inner), F32)
    return pl.pallas_call(
        step_kernel,
        out_shape=(
            f((rows, width), F32), third, third, third, f((SHARD, width), F32), f((enc.shape[0], width), F32),
            f((8, 128), F32),
        ),
        in_specs=[vm] * 5 + [anyspace] * 5,
        out_specs=[anyspace] + [vm] * 6,
        scratch_shapes=[
            v((2, 4, 4, 2, SHARD, inner), F32), v((width, 3 * inner), BF16), v((width, 3 * inner), BF16),
            v((2, inner, part), BF16), v((2, inner, part), BF16), v((4, 4, 4, SHARD, inner), F32),
            v((4, 2, 2, 2, SHARD, inner), F32), v((4, 2, 2, SHARD, inner), F32),
            v((4, 2, SHARD, inner), F32), v((4, SHARD, inner), F32), v((4, 2, SHARD, inner), F32),
            v((4, 2, SHARD, inner), F32), v((7, 8, width), F32),
            v((TROWS, width), F32), v((TROWS, width), F32), v((120, width), F32), v((120, width), F32),
            v((SLOTS, part + 128), F32), v((SLOTS, part + 128), F32), v((SLOTS, part + 128), F32),
            v((SLOTS, part), F32), v((SLOTS, part), F32), v((SLOTS, part), F32),
            v((rows, width), F32), v((rows, width), F32), v((rows, width), F32), v((rows, width), F32),
            v((rows, 1), F32), v((rows, width), BF16), v((rows, width), BF16),
            v((rows, 3 * inner), F32), v((2 * inner // HEAD, rows // 2, rows // 2), F32),
            v((rows, inner), F32), v((rows, inner), F32), v((rows, 3 * inner), F32),
            v((8, width), F32), dma((6,)), dma((16,)), dma((16,)), dma((4, 15)), dma((4, 15)), dma((4, 7)), dma((4, 7)),
            dma((4, 18)), dma((4, 18)), dma((7,)), dma((7,)), pltpu.SemaphoreType.REGULAR,
        ],
        compiler_params=pltpu.CompilerParams(
            vmem_limit_bytes=63 * 2**20, collective_id=0, has_side_effects=True
        ),
        name="decoder_step",
    )(cell, pos, enc, mask, gain, cot, wq, wk, wv, wo)


def copy_kernel(*refs):
    ins, outs, sems = refs[:6], refs[7:13], refs[15]
    copies = [pltpu.make_async_copy(i, o, sems.at[k]) for k, (i, o) in enumerate(zip(ins, outs))]
    for copy in copies:
        copy.start()
    refs[13][...] = refs[6][0:1, :80].reshape(80)
    refs[14][...] = refs[6][1:2, :80].reshape(80)
    for copy in copies:
        copy.wait()


def hand_over(arrays, own):
    vm = pl.BlockSpec(memory_space=pltpu.VMEM)
    anyspace = pl.BlockSpec(memory_space=pl.ANY)
    short = jax.ShapeDtypeStruct((80,), F32)
    return pl.pallas_call(
        copy_kernel,
        out_shape=tuple(jax.ShapeDtypeStruct(x.shape, x.dtype) for x in arrays) + (short, short),
        in_specs=[anyspace] * 6 + [vm],
        out_specs=[anyspace] * 6 + [vm] * 2,
        scratch_shapes=[pltpu.SemaphoreType.DMA((6,))],
        compiler_params=pltpu.CompilerParams(vmem_limit_bytes=60 * 2**20),
        name="hand_over",
    )(*arrays, own)


def body(positions, encoded, mask_token, norm_gain, w_query, w_key, w_value, w_out, cotangent):
    model_width = encoded.shape[1]
    inner = w_out.shape[0]
    shard = (4, 4, 2, SHARD, inner)
    tile_map = jnp.asarray(tile_rows_map())[None]
    *arrays, own = decoder_step(
        tile_map, positions[None], encoded, mask_token.reshape(-1, 128), norm_gain.reshape(-1, 128),
        cotangent.reshape(-1, model_width), w_query.reshape(shard), w_key.reshape(shard),
        w_value.reshape(shard), w_out.reshape(4, 4, SHARD, model_width),
    )
    decoded, grad_query, grad_key, grad_value, grad_out, grad_encoded, grad_mask, grad_gain = hand_over(arrays, own)
    matrices = (g.reshape(-1, inner) for g in (grad_query, grad_key, grad_value))
    return (decoded.reshape(cotangent.shape), *matrices, grad_out, grad_mask, grad_gain, grad_encoded)


def solution(mesh):
    return jax.shard_map(
        body,
        mesh=mesh,
        in_specs=(
            P(("lat", "lon")),
            P(("lat", "lon"), None),
            P(),
            P(),
            P(),
            P(),
            P(),
            P(),
            P("lat", "lon", None),
        ),
        out_specs=(
            P("lat", "lon", None),
            P("lon", None),
            P("lon", None),
            P("lon", None),
            P("lon", None),
            P("lon"),
            P("lon"),
            P(("lat", "lon"), None),
        ),
        check_vma=False,
    )
```

```python
import functools, math
import jax, jax.numpy as jnp
import numpy as np
from jax import lax
from jax.experimental import pallas as pl
from jax.experimental.pallas import tpu as pltpu
from jax.sharding import PartitionSpec as P

HEAD = 80
F32 = jnp.float32
BF16 = jnp.bfloat16


def split(x):
    hi = x.astype(BF16)
    return hi, (x - hi.astype(F32)).astype(BF16)


NN = (((1,), (0,)), ((), ()))
NT = (((1,), (1,)), ((), ()))
TN = (((0,), (0,)), ((), ()))


def dot(a, b, dims):
    return lax.dot_general(a, b, dims, preferred_element_type=F32)


def dot3(a, b, dims):
    return dot(a[0], b[0], dims) + (dot(a[0], b[1], dims) + dot(a[1], b[0], dims))


def head_lanes(h):
    low = h * HEAD // 128 * 128
    high = -(-(h + 1) * HEAD // 128) * 128
    return low, high


MESH = pl.DeviceIdType.MESH
SLOTS = 256
TROWS = 304
SHARD = 40
SCALE = 1.0 / 192.0


def tile_rows_map():
    def block(r0, c0, cols):
        return [(r0 + i) * 24 + c0 + j for i in range(6) for j in range(cols)]

    none = [-5] * 4
    order = block(6, 6, 12) + block(6, 18, 6) + none + block(0, 6, 12) + block(0, 18, 6) + none
    order += none + block(6, 0, 6) + none + block(0, 0, 6)
    return np.array(order, np.int32)


def split3(x):
    hi = x.astype(BF16)
    rest = x - hi.astype(F32)
    mid = rest.astype(BF16)
    return hi, mid, (rest - mid.astype(F32)).astype(BF16)


def pick(onehot, x, dims):
    hi, mid, lo = split3(x)
    return (dot(onehot, hi, dims) + dot(onehot, mid, dims)) + dot(onehot, lo, dims)


def onehot(cond):
    return jnp.where(cond, 1.0, 0.0).astype(BF16)


def swap_matrix():
    j = lax.broadcasted_iota(jnp.int32, (SLOTS, SLOTS), 0)
    i = lax.broadcasted_iota(jnp.int32, (SLOTS, SLOTS), 1)
    b = jnp.right_shift(j, 4)
    a = jnp.bitwise_and(jnp.right_shift(j, 1), 7)
    return onehot(i == a * 32 + b * 2 + jnp.bitwise_and(j, 1))


def flip_low(i):
    return i + 1 - 2 * (i % 2)


def flip_far(i):
    return 3 - i


def remote(src, dst, send, recv, device):
    copy = pltpu.make_async_remote_copy(
        src_ref=src, dst_ref=dst, send_sem=send, recv_sem=recv, device_id=device, device_id_type=MESH
    )
    copy.start()
    return copy


def rows_at(start, size):
    return pl.ds(pl.multiple_of(start, size), size)


def send_lon(src, dst, send, recv, a, b, lanes=None):
    cols = pl.ds(0, lanes or src.shape[1])
    copies = []
    for k in range(1, 16):
        peer = (b + k) % 16
        copies.append(remote(
            src.at[rows_at(peer * 16, 16), cols], dst.at[rows_at(b * 16, 16), cols], send.at[k - 1], recv.at[k - 1], (a, peer)
        ))
    dst[rows_at(b * 16, 16), :] = src[rows_at(b * 16, 16), :]
    return copies


def send_lat(src, dst, send, recv, a, b, lanes=None):
    cols = pl.ds(0, lanes or src.shape[1])
    copies = []
    for k in range(1, 8):
        peer = (a + k) % 8
        copies.append(remote(
            src.at[rows_at(peer * 32, 32), cols], dst.at[rows_at(a * 32, 32), cols], send.at[k - 1], recv.at[k - 1], (peer, b)
        ))
    dst[rows_at(a * 32, 32), :] = src[rows_at(a * 32, 32), :]
    return copies


def finish(copies):
    for copy in copies:
        copy.wait()


class Sum:
    def __init__(self, m, home, place, w, acc, r1, r2, r3, r4, r5, fin, send_sem, recv_sem):
        self.m, self.home, self.place = m, home, place
        self.w, self.acc, self.r = w, acc, (r1, r2, r3, r4, r5)
        self.fin, self.send_sem, self.recv_sem = fin, send_sem, recv_sem
        self.first = m % 2 == 0
        self.stage, self.slot, self.copies = 0, 0, []

    def chunk(self, i, half):
        rest = pl.ds(2 * half, 2)
        return (self.m, i, rest) if self.first else (self.m, rest, i)

    def piece(self, i, half):
        a, b, x, c, y, z = self.place
        rows = pl.ds(0, 24) if half == 0 else pl.ds(24, 16)
        return (self.m, y, i, rows) if self.first else (self.m, i, z, rows)

    def near(self, ring, i):
        a, b, x, c, y, z = self.place
        return (a, i * 4 + z) if ring == self.first else (a, y * 4 + i)

    def send(self, src, dst, device):
        k = self.slot
        self.slot += 1
        self.copies.append(remote(src, dst, self.send_sem.at[self.m, k], self.recv_sem.at[self.m, k], device))

    def begin(self):
        a, b, x, c, y, z = self.place
        m, acc, (r1, r2, r3, r4, r5) = self.m, self.acc, self.r
        me1, me2 = (y, z) if self.first else (z, y)
        s = self.stage
        if s == 0:
            self.send(self.w.at[self.home, :, :, 1 - c], acc.at[m], (a + 1 - 2 * c, b))
            return
        if s == 7:
            self.send(self.fin.at[m, c], self.fin.at[m, c], (a + 1 - 2 * c, b))
            return
        for half in range(2):
            q1, q2 = (flip_low, flip_far) if half == 0 else (flip_far, flip_low)
            rows = pl.ds(0, 24) if half == 0 else pl.ds(24, 16)
            if s == 1:
                p = q1(me1)
                self.send(acc.at[self.chunk(p, half)], r1.at[m, 0, half], self.near(True, p))
                self.send(acc.at[self.chunk(q2(p), half)], r1.at[m, 1, half], self.near(True, p))
            elif s == 2:
                p = q2(me1)
                self.send(acc.at[self.chunk(p, half)], r2.at[m, half], self.near(True, p))
            elif s == 3:
                p = q1(me2)
                self.send(acc.at[self.piece(p, half)], r3.at[m, 0, rows], self.near(False, p))
                self.send(acc.at[self.piece(q2(p), half)], r3.at[m, 1, rows], self.near(False, p))
            elif s == 4:
                p = q2(me2)
                self.send(acc.at[self.piece(p, half)], r4.at[m, rows], self.near(False, p))
            elif s == 5:
                self.send(acc.at[self.piece(me2, half)], r5.at[m, 0, rows], (q1(x) * 2 + c, b))
            elif s == 6:
                self.send(acc.at[self.piece(me2, half)], r5.at[m, 1, rows], (q2(x) * 2 + c, b))

    def end(self):
        a, b, x, c, y, z = self.place
        m, acc, (r1, r2, r3, r4, r5) = self.m, self.acc, self.r
        me1, me2 = (y, z) if self.first else (z, y)
        s = self.stage
        finish(self.copies)
        self.copies = []
        if s == 0:
            @pl.loop(0, 4)
            def _(i):
                acc[m, i] += self.w[self.home, i, :, c]
        for half in range(2):
            q2 = flip_far if half == 0 else flip_low
            rows = pl.ds(0, 24) if half == 0 else pl.ds(24, 16)
            if s == 1:
                acc[self.chunk(me1, half)] += r1[m, 0, half]
                acc[self.chunk(q2(me1), half)] += r1[m, 1, half]
            elif s == 2:
                acc[self.chunk(me1, half)] += r2[m, half]
            elif s == 3:
                acc[self.piece(me2, half)] += r3[m, 0, rows]
                acc[self.piece(q2(me2), half)] += r3[m, 1, rows]
            elif s == 4:
                acc[self.piece(me2, half)] += r4[m, rows]
            elif s == 5:
                acc[self.piece(me2, half)] += r5[m, 0, rows]
            elif s == 6:
                self.fin[m, c, rows] = (acc[self.piece(me2, half)] + r5[m, 1, rows]) * SCALE
        self.stage += 1

    def step(self):
        self.end()
        if self.stage < 8:
            self.begin()


def step_kernel(
    cell_ref, pos_ref, enc_ref, mask_ref, gain_ref, cot_hbm, wq_hbm, wk_hbm, wv_hbm, wo_hbm,
    decoded_hbm, dq_ref, dk_ref, dv_ref, do_ref, denc_ref, own_ref,
    w, w_hi, w_lo, o_hi, o_lo, acc, r1, r2, r3, r4, r5, fin, vr,
    tile_t, tile_g, land_t, land_g, sa0, ra0, rb0, sa1, ra1, rb1,
    t_ref, g_ref, xhat_ref, dn_ref, rstd_ref, n_hi, n_lo, qkv_ref, p_ref, att_ref, datt_ref, dqkv_ref,
    vec_ref, load_s, halo_s, halo_r, lon_s, lon_r, lat_s, lat_r, sum_s, sum_r, vec_s, vec_r, free_s,
):
    a, b = lax.axis_index("lat"), lax.axis_index("lon")
    x, c = a // 2, a % 2
    y, z = b // 4, b % 4
    rows, width = t_ref.shape
    inner = att_ref.shape[1]
    part = width // 2
    heads = inner // HEAD
    half = rows // 2
    up, right = (a + 1) % 8, (b + 1) % 16
    down, left = (a + 7) % 8, (b + 15) % 16

    load_cot = pltpu.make_async_copy(cot_hbm, xhat_ref, load_s.at[0])
    load_o = [
        pltpu.make_async_copy(wo_hbm.at[:, :, :, pl.ds(i * part, part)], w.at[0, :, :, i], load_s.at[1 + i])
        for i in range(2)
    ]
    load_v = pltpu.make_async_copy(wv_hbm, w.at[1], load_s.at[3])
    load_k = pltpu.make_async_copy(wk_hbm, w.at[0], load_s.at[4])
    load_q = pltpu.make_async_copy(wq_hbm, w.at[1], load_s.at[5])
    load_cot.start()
    load_o[0].start()
    load_o[1].start()
    load_v.start()

    def take_weight(load, home, which):
        load.wait()

        @pl.loop(0, 16)
        def _(i):
            r = pl.ds(pl.multiple_of(i * 80, 80), 80)
            cols = slice(which * inner, (which + 1) * inner)
            w_hi[r, cols], w_lo[r, cols] = split(w[home, i // 4, i % 4].reshape(80, inner))

    peers = [(a, (b + k) % 16) for k in range(1, 16)] + [((a + k) % 8, b) for k in range(1, 8)]
    peers += [(up, right), (down, left)]
    barrier = pltpu.get_barrier_semaphore()
    for peer in peers:
        pl.semaphore_signal(barrier, inc=1, device_id=peer, device_id_type=MESH)

    count = enc_ref.shape[0]
    pos = pos_ref[...].astype(F32)
    lat = jnp.floor((pos + 0.5) * (1.0 / 384.0))
    lon = pos - lat * 384.0
    tile_a = jnp.floor((lat + 0.5) * (1.0 / 12.0))
    tile_b = jnp.floor((lon + 0.5) * (1.0 / 24.0))
    cell = (lat - tile_a * 12.0) * 24.0 + lon - tile_b * 24.0
    target = tile_a * 16.0 + tile_b
    line = lax.broadcasted_iota(jnp.int32, (count, count), 0)
    lane = lax.broadcasted_iota(jnp.int32, (count, count), 1)

    def column(v):
        return jnp.sum(jnp.where(line == lane, v, 0.0), axis=1, keepdims=True)

    earlier = jnp.logical_and(column(target) == target, line < lane)
    rank = jnp.sum(jnp.where(earlier, 1.0, 0.0), axis=0, keepdims=True)
    index1 = target * 2.0 + rank
    index2 = tile_b * 16.0 + tile_a * 2.0 + rank
    column1, column2 = column(index1), column(index2)

    seats = lax.broadcasted_iota(jnp.int32, (SLOTS, count), 0).astype(F32)
    to2 = onehot(seats == index2)
    sa0[:, :part] = pick(to2, enc_ref[:, :part], NN)
    sa0[:, part:] = pick(to2, jnp.broadcast_to(column(cell) + 1.0, (count, 128)), NN)
    to1 = onehot(seats == index1)
    sa1[...] = pick(to1, enc_ref[:, part:], NN)

    pl.semaphore_wait(barrier, len(peers))
    go0 = send_lon(sa0, ra0, lon_s.at[0], lon_r.at[0], a, b)
    go1 = send_lat(sa1, ra1, lat_s.at[0], lat_r.at[0], a, b)

    def halo(tile, land, whole, first):
        moves = (
            (224, 40, land.at[pl.ds(0, 40)], (a, left)), (112, 72, whole.at[pl.ds(72, 72)], (down, b)),
            (184, 40, land.at[pl.ds(40, 40)], (down, b)), (264, 40, land.at[pl.ds(80, 40)], (down, left)),
        )
        return [
            remote(tile.at[pl.ds(row, size)], dst, halo_s.at[first + i], halo_r.at[first + i], device)
            for i, (row, size, dst, device) in enumerate(moves)
        ]

    def settle(tile, land, whole):
        whole[0:72, :] = tile[0:72, :]
        whole[144:180, :] = tile[72:108, :]
        whole[180:216, :] = land[4:40, :]
        whole[216:252, :] = land[40:76, :]
        whole[252:288, :] = land[84:120, :]

    def halo_back(src, tile, first, cols):
        moves = (
            (72, 72, 112, (up, b)), (216, 40, 184, (up, b)), (176, 40, 224, (a, right)), (248, 40, 264, (up, right)),
        )
        return [
            remote(
                src.at[pl.ds(row, size), cols], tile.at[pl.ds(to, size), cols],
                halo_s.at[first + i], halo_r.at[first + i], device,
            )
            for i, (row, size, to, device) in enumerate(moves)
        ]

    def keep_own(src, tile):
        tile[0:72, :] = src[0:72, :]
        tile[72:112, :] = src[144:184, :]

    place = onehot(lax.broadcasted_iota(jnp.int32, (rows, TROWS), 0) == cell_ref[...])
    load_cot.wait()
    for j in range(0, width, 256):
        tile_g[:, j:j + 256] = pick(place, xhat_ref[:, j:j + 256], TN)

    load_o[0].wait()
    load_o[1].wait()
    for i in range(2):
        for j in range(4):
            r = slice(j * 160, (j + 1) * 160)
            cols = slice(i * part, (i + 1) * part)
            o_hi[r, cols], o_lo[r, cols] = split(w[0, j, :, i].reshape(160, part))
    load_k.start()
    take_weight(load_v, 1, 2)
    load_q.start()

    swap = swap_matrix()
    finish(go0)
    sa0[...] = pick(swap, ra0[...], TN)
    go0 = send_lat(sa0, rb0, lat_s.at[1], lat_r.at[1], a, b)
    finish(go1)
    sa1[...] = pick(swap, ra1[...], NN)
    go1 = send_lon(sa1, rb1, lon_s.at[1], lon_r.at[1], a, b)

    take_weight(load_k, 0, 1)
    take_weight(load_q, 1, 0)

    finish(go0)
    table = onehot(rb0[:, part:part + 1] == (cell_ref[...] + 1).astype(F32))
    table2 = dot(swap, table, NN).astype(BF16)
    seen = jnp.sum(table.astype(F32), axis=0, keepdims=True)
    lead = lax.broadcasted_iota(jnp.int32, (16, 1), 0) == 0
    unseen = jnp.where(lead, 1.0 - seen, 0.0).astype(BF16)
    mask = jnp.broadcast_to(jnp.concatenate([mask_ref[i:i + 1, :] for i in range(10)], axis=1), (16, width))
    gain = jnp.concatenate([gain_ref[i:i + 1, :] for i in range(10)], axis=1)
    tile_t[:, :part] = pick(table, rb0[:, :part], TN) + pick(unseen, mask[:, :part], TN)
    finish(go1)
    tile_t[:, part:] = pick(table2, rb1[...], TN) + pick(unseen, mask[:, part:], TN)
    halo_t = halo(tile_t, land_t, t_ref, 4)
    finish(halo_t)
    halo_g = halo(tile_g, land_g, g_ref, 0)
    settle(tile_t, land_t, t_ref)

    step = 32

    @pl.loop(0, rows // step)
    def _(i):
        r = pl.ds(pl.multiple_of(i * step, step), step)
        t = t_ref[r, :]
        centred = t - jnp.mean(t, axis=-1, keepdims=True)
        rstd = lax.rsqrt(jnp.mean(centred * centred, axis=-1, keepdims=True) + 1e-5)
        xhat = centred * rstd
        xhat_ref[r, :] = xhat
        rstd_ref[r, :] = rstd
        n_hi[r, :], n_lo[r, :] = split(xhat * gain)

    @pl.loop(0, 3 * inner // 256)
    def _(j):
        cols = pl.ds(pl.multiple_of(j * 256, 256), 256)
        qkv_ref[:, cols] = dot3((n_hi[...], n_lo[...]), (w_hi[:, cols], w_lo[:, cols]), NN)

    qkv_ref[:, 1792:] = dot3((n_hi[...], n_lo[...]), (w_hi[:, 1792:], w_lo[:, 1792:]), NN)

    finish(halo_g)
    settle(tile_g, land_g, g_ref)

    for peer in peers:
        pl.semaphore_signal(free_s, inc=1, device_id=peer, device_id_type=MESH)

    datt_ref[...] = dot3(split(g_ref[...]), (o_hi[...], o_lo[...]), NT)

    att_ref[...] = jnp.zeros_like(att_ref)
    dqkv_ref[...] = jnp.zeros_like(dqkv_ref)
    is_last = a == 7
    low_q = lax.broadcasted_iota(jnp.int32, (half, half), 0) >= half // 2
    low_k = lax.broadcasted_iota(jnp.int32, (half, half), 1) >= half // 2
    blocked = jnp.logical_and(low_q != low_k, is_last)
    norm = 1.0 / math.sqrt(HEAD)

    def head(h):
        lo, hi = head_lanes(h)
        lane = lax.broadcasted_iota(jnp.int32, (half, hi - lo), 1) + lo
        return lo, hi, jnp.logical_and(lane >= h * HEAD, lane < (h + 1) * HEAD)

    @pl.loop(0, 2)
    def _(wd):
        r = pl.ds(pl.multiple_of(wd * half, 16), half)
        for h in range(heads):
            lo, hi, mine = head(h)
            q = split(jnp.where(mine, qkv_ref[r, lo:hi] * norm, 0.0))
            k = split(qkv_ref[r, inner + lo:inner + hi])
            v = split(qkv_ref[r, 2 * inner + lo:2 * inner + hi])
            do = split(jnp.where(mine, datt_ref[r, lo:hi], 0.0))
            s = dot3(q, k, NT)
            s = jnp.where(blocked, -1e30, s)
            e = jnp.exp(s - jnp.max(s, axis=-1, keepdims=True))
            p32 = e / jnp.sum(e, axis=-1, keepdims=True)
            p_ref[wd * heads + h] = p32
            p = split(p32)
            att_ref[r, lo:hi] += jnp.where(mine, dot3(p, v, NN), 0.0)
            dqkv_ref[r, 2 * inner + lo:2 * inner + hi] += dot3(p, do, TN)

    att = split(att_ref[...])
    att_row = jnp.concatenate([att[0], att[0], att[1]], axis=1)

    @pl.loop(0, width // 256)
    def _(j):
        cols = pl.ds(pl.multiple_of(j * 256, 256), 256)
        oh, ol = o_hi[:, cols], o_lo[:, cols]
        t_ref[:, cols] += dot(att_row, jnp.concatenate([oh, ol, oh], axis=0), NN)

    pl.semaphore_wait(free_s, len(peers))
    halo_o = halo_back(t_ref, tile_g, 12, pl.ds(0, width))
    keep_own(t_ref, tile_g)

    sums = [
        Sum(m, m % 2, (a, b, x, c, y, z), w, acc, r1, r2, r3, r4, r5, fin, sum_s, sum_r) for m in range(4)
    ]

    att3 = jnp.concatenate([att[0], att[0], att[1]], axis=0)
    gh, gl = split(g_ref[...])
    res = dot(att3, jnp.concatenate([gh, gl, gh], axis=0), TN)
    for i in range(2):
        w[0, :, :, i] = res[:, i * part:(i + 1) * part].reshape(4, 4, SHARD, part)
    sums[0].begin()

    def grad_rows(which):
        return split(dqkv_ref[:, which * inner:(which + 1) * inner])

    def to_tokens(which, dh, dl, add):
        d3 = jnp.concatenate([dh, dh, dl], axis=1)
        cols = slice(which * inner, (which + 1) * inner)
        for lo in range(0, width, 256):
            r = slice(lo, lo + 256)
            wh, wl = w_hi[r, cols], w_lo[r, cols]
            res = dot(d3, jnp.concatenate([wh, wl, wh], axis=1), NT)
            dn_ref[:, r] = dn_ref[:, r] + res if add else res

    def to_weight(cols, homes):
        dh, dl = split(dqkv_ref[:, cols])
        d3 = jnp.concatenate([dh, dl, dh], axis=0)
        for i in range(2):
            half = slice(i * part, (i + 1) * part)
            nh, nl = n_hi[:, half], n_lo[:, half]
            res = dot(jnp.concatenate([nh, nh, nl], axis=0), d3, TN)
            for j, home in enumerate(homes):
                block = res[:, j * inner:(j + 1) * inner]
                w[home, 2 * i:2 * i + 2] = block.reshape(2, 4, 2, SHARD, inner)

    to_weight(slice(2 * inner, 3 * inner), (1,))
    sums[1].begin()
    sums[0].step()
    dh, dl = grad_rows(2)
    to_tokens(2, dh, dl, False)
    sums[1].step()

    @pl.loop(0, 2)
    def _(wd):
        r = pl.ds(pl.multiple_of(wd * half, 16), half)
        for h in range(heads):
            lo, hi, mine = head(h)
            q = split(jnp.where(mine, qkv_ref[r, lo:hi] * norm, 0.0))
            k = split(qkv_ref[r, inner + lo:inner + hi])
            v = split(qkv_ref[r, 2 * inner + lo:2 * inner + hi])
            do = split(jnp.where(mine, datt_ref[r, lo:hi], 0.0))
            p32 = p_ref[wd * heads + h]
            dp = dot3(do, v, NT)
            ds = split(p32 * (dp - jnp.sum(dp * p32, axis=-1, keepdims=True)))
            dqkv_ref[r, lo:hi] += jnp.where(mine, dot3(ds, k, NN) * norm, 0.0)
            dqkv_ref[r, inner + lo:inner + hi] += dot3(ds, q, TN)

    to_weight(slice(0, 2 * inner), (1, 0))
    sums[2].begin()
    sums[3].begin()
    sums[0].step()
    sums[1].step()
    kh, kl = grad_rows(1)
    to_tokens(1, kh, kl, True)
    sums[2].step()
    sums[3].step()
    qh, ql = grad_rows(0)
    to_tokens(0, qh, ql, True)
    sums[0].step()
    sums[1].step()

    vec_ref[...] = jnp.zeros_like(vec_ref)

    @pl.loop(0, rows // step)
    def _(i):
        r = pl.ds(pl.multiple_of(i * step, step), step)
        dn = dn_ref[r, :]
        xhat = xhat_ref[r, :]
        vec_ref[1:2, :] += jnp.sum(dn * xhat, axis=0, keepdims=True)
        dx = dn * gain
        m1 = jnp.mean(dx, axis=-1, keepdims=True)
        m2 = jnp.mean(dx * xhat, axis=-1, keepdims=True)
        g_ref[r, :] += rstd_ref[r, :] * (dx - m1 - xhat * m2)

    halo_d = [halo_back(g_ref, tile_t, first, pl.ds(lane, part)) for first, lane in ((8, 0), (16, part))]
    keep_own(g_ref, tile_t)

    sums[0].step()
    sums[1].step()

    finish(halo_o)
    for j in range(0, width, 256):
        xhat_ref[:, j:j + 256] = pick(place, tile_g[:, j:j + 256], NN)
    store = pltpu.make_async_copy(xhat_ref, decoded_hbm, load_s.at[0])
    store.start()
    sums[2].step()
    sums[3].step()

    finish(halo_d[0])
    sa1[...] = pick(table, tile_t[:, :part], NN)
    back0 = send_lat(sa1, ra1, lat_s.at[2], lat_r.at[2], a, b)
    finish(halo_d[1])
    sa0[:, :part] = pick(table2, tile_t[:, part:], NN)
    back1 = send_lon(sa0, ra0, lon_s.at[2], lon_r.at[2], a, b, part)
    masked = jnp.where(cell_ref[...] >= 0, 1.0 - seen, 0.0)
    masked = jnp.where(lead, masked, 0.0)[:8].astype(BF16)
    vec_ref[...] += pick(masked, tile_t[...], NN)

    vec_devices = [
        (a + 1 - 2 * c, b), (flip_low(x) * 2 + c, b), (flip_far(x) * 2 + c, b),
        (a, flip_low(y) * 4 + z), (a, flip_far(y) * 4 + z), (a, y * 4 + flip_low(z)), (a, y * 4 + flip_far(z)),
    ]
    vec_copies = []

    def vec_begin(k):
        vec_copies.append(remote(vec_ref, vr.at[k], vec_s.at[k], vec_r.at[k], vec_devices[k]))

    def vec_step():
        k = len(vec_copies) - 1
        vec_copies[k].wait()
        vec_ref[...] += vr[k]
        if k < 6:
            vec_begin(k + 1)

    def round_of_sums():
        for total in sums:
            if total.stage < 8:
                total.step()
        if vec_copies and len(vec_copies) < 7:
            vec_step()

    vec_begin(0)
    round_of_sums()
    round_of_sums()

    finish(back0)
    sa1[...] = pick(swap, ra1[...], NN)
    back0 = send_lon(sa1, rb1, lon_s.at[3], lon_r.at[3], a, b)
    finish(back1)
    sa0[:, :part] = pick(swap, ra0[:, :part], TN)
    back1 = send_lat(sa0, rb0, lat_s.at[3], lat_r.at[3], a, b, part)

    for _ in range(4):
        round_of_sums()

    finish(back0)
    finish(back1)
    slots = lax.broadcasted_iota(jnp.int32, (count, SLOTS), 1).astype(F32)
    denc_ref[:, :part] = pick(onehot(slots == column2), rb1[...], NN)
    denc_ref[:, part:] = pick(onehot(slots == column1), rb0[:, :part], NN)

    while any(total.stage < 8 for total in sums) or len(vec_copies) < 7:
        round_of_sums()
    vec_step()
    lanes = lax.broadcasted_iota(jnp.int32, (width, 128), 1)
    mine = jnp.logical_and(lax.broadcasted_iota(jnp.int32, (width, 128), 0) == b * 80 + lanes, lanes < 80)
    mine = onehot(mine)
    hi, mid, lo = split3(vec_ref[...] * SCALE)
    own_ref[...] = (dot(hi, mine, NN) + dot(mid, mine, NN)) + dot(lo, mine, NN)
    do_ref[:, :part] = fin[0, 0]
    do_ref[:, part:] = fin[0, 1]
    dv_ref[...] = fin[1]
    dk_ref[...] = fin[2]
    dq_ref[...] = fin[3]
    store.wait()


def decoder_step(cell, pos, enc, mask, gain, cot, wq, wk, wv, wo):
    rows, width = cot.shape
    part = width // 2
    inner = wo.shape[2] * 16
    vm = pl.BlockSpec(memory_space=pltpu.VMEM)
    anyspace = pl.BlockSpec(memory_space=pl.ANY)
    f = jax.ShapeDtypeStruct
    dma = pltpu.SemaphoreType.DMA
    v = pltpu.VMEM
    third = f((2, SHARD, inner), F32)
    return pl.pallas_call(
        step_kernel,
        out_shape=(
            f((rows, width), F32), third, third, third, f((SHARD, width), F32), f((enc.shape[0], width), F32),
            f((8, 128), F32),
        ),
        in_specs=[vm] * 5 + [anyspace] * 5,
        out_specs=[anyspace] + [vm] * 6,
        scratch_shapes=[
            v((2, 4, 4, 2, SHARD, inner), F32), v((width, 3 * inner), BF16), v((width, 3 * inner), BF16),
            v((inner, width), BF16), v((inner, width), BF16), v((4, 4, 4, SHARD, inner), F32),
            v((4, 2, 2, 2, SHARD, inner), F32), v((4, 2, 2, SHARD, inner), F32),
            v((4, 2, SHARD, inner), F32), v((4, SHARD, inner), F32), v((4, 2, SHARD, inner), F32),
            v((4, 2, SHARD, inner), F32), v((7, 8, width), F32),
            v((TROWS, width), F32), v((TROWS, width), F32), v((120, width), F32), v((120, width), F32),
            v((SLOTS, part + 128), F32), v((SLOTS, part + 128), F32), v((SLOTS, part + 128), F32),
            v((SLOTS, part), F32), v((SLOTS, part), F32), v((SLOTS, part), F32),
            v((rows, width), F32), v((rows, width), F32), v((rows, width), F32), v((rows, width), F32),
            v((rows, 1), F32), v((rows, width), BF16), v((rows, width), BF16),
            v((rows, 3 * inner), F32), v((2 * inner // HEAD, rows // 2, rows // 2), F32),
            v((rows, inner), F32), v((rows, inner), F32), v((rows, 3 * inner), F32),
            v((8, width), F32), dma((6,)), dma((20,)), dma((20,)), dma((4, 15)), dma((4, 15)), dma((4, 7)), dma((4, 7)),
            dma((4, 18)), dma((4, 18)), dma((7,)), dma((7,)), pltpu.SemaphoreType.REGULAR,
        ],
        compiler_params=pltpu.CompilerParams(
            vmem_limit_bytes=63 * 2**20, collective_id=0, has_side_effects=True
        ),
        name="decoder_step",
    )(cell, pos, enc, mask, gain, cot, wq, wk, wv, wo)


def copy_kernel(*refs):
    for src, dst in zip(refs[:6], refs[7:13]):
        dst[...] = src[...]
    refs[13][...] = refs[6][0:1, :80].reshape(80)
    refs[14][...] = refs[6][1:2, :80].reshape(80)


def hand_over(arrays, own):
    vm = pl.BlockSpec(memory_space=pltpu.VMEM)
    short = jax.ShapeDtypeStruct((80,), F32)
    return pl.pallas_call(
        copy_kernel,
        out_shape=tuple(jax.ShapeDtypeStruct(x.shape, x.dtype) for x in arrays) + (short, short),
        in_specs=[vm] * 7,
        out_specs=[vm] * 8,
        compiler_params=pltpu.CompilerParams(vmem_limit_bytes=60 * 2**20),
        name="hand_over",
    )(*arrays, own)


def body(positions, encoded, mask_token, norm_gain, w_query, w_key, w_value, w_out, cotangent):
    model_width = encoded.shape[1]
    inner = w_out.shape[0]
    shard = (4, 4, 2, SHARD, inner)
    tile_map = jnp.asarray(tile_rows_map())[None]
    *arrays, own = decoder_step(
        tile_map, positions[None], encoded, mask_token.reshape(-1, 128), norm_gain.reshape(-1, 128),
        cotangent.reshape(-1, model_width), w_query.reshape(shard), w_key.reshape(shard),
        w_value.reshape(shard), w_out.reshape(4, 4, SHARD, model_width),
    )
    decoded, grad_query, grad_key, grad_value, grad_out, grad_encoded, grad_mask, grad_gain = hand_over(arrays, own)
    matrices = (g.reshape(-1, inner) for g in (grad_query, grad_key, grad_value))
    return (decoded.reshape(cotangent.shape), *matrices, grad_out, grad_mask, grad_gain, grad_encoded)


def solution(mesh):
    return jax.shard_map(
        body,
        mesh=mesh,
        in_specs=(
            P(("lat", "lon")),
            P(("lat", "lon"), None),
            P(),
            P(),
            P(),
            P(),
            P(),
            P(),
            P("lat", "lon", None),
        ),
        out_specs=(
            P("lat", "lon", None),
            P("lon", None),
            P("lon", None),
            P("lon", None),
            P("lon", None),
            P("lon"),
            P("lon"),
            P(("lat", "lon"), None),
        ),
        check_vma=False,
    )
```

```python
import functools, math
import jax, jax.numpy as jnp
import numpy as np
from jax import lax
from jax.experimental import pallas as pl
from jax.experimental.pallas import tpu as pltpu
from jax.sharding import PartitionSpec as P

HEAD = 80
F32 = jnp.float32
BF16 = jnp.bfloat16


def split(x):
    hi = x.astype(BF16)
    return hi, (x - hi.astype(F32)).astype(BF16)


NN = (((1,), (0,)), ((), ()))
NT = (((1,), (1,)), ((), ()))
TN = (((0,), (0,)), ((), ()))


def dot(a, b, dims):
    return lax.dot_general(a, b, dims, preferred_element_type=F32)


def dot3(a, b, dims):
    return dot(a[0], b[0], dims) + (dot(a[0], b[1], dims) + dot(a[1], b[0], dims))


def head_lanes(h):
    low = h * HEAD // 128 * 128
    high = -(-(h + 1) * HEAD // 128) * 128
    return low, high


MESH = pl.DeviceIdType.MESH
SLOTS = 256
TROWS = 304
SHARD = 40
SCALE = 1.0 / 192.0


def tile_rows_map():
    def block(r0, c0, cols):
        return [(r0 + i) * 24 + c0 + j for i in range(6) for j in range(cols)]

    none = [-5] * 4
    order = block(6, 6, 12) + block(6, 18, 6) + none + block(0, 6, 12) + block(0, 18, 6) + none
    order += none + block(6, 0, 6) + none + block(0, 0, 6)
    return np.array(order, np.int32)


def split3(x):
    hi = x.astype(BF16)
    rest = x - hi.astype(F32)
    mid = rest.astype(BF16)
    return hi, mid, (rest - mid.astype(F32)).astype(BF16)


def pick(onehot, x, dims):
    hi, mid, lo = split3(x)
    return (dot(onehot, hi, dims) + dot(onehot, mid, dims)) + dot(onehot, lo, dims)


def onehot(cond):
    return jnp.where(cond, 1.0, 0.0).astype(BF16)


def swap_matrix():
    j = lax.broadcasted_iota(jnp.int32, (SLOTS, SLOTS), 0)
    i = lax.broadcasted_iota(jnp.int32, (SLOTS, SLOTS), 1)
    b = jnp.right_shift(j, 4)
    a = jnp.bitwise_and(jnp.right_shift(j, 1), 7)
    return onehot(i == a * 32 + b * 2 + jnp.bitwise_and(j, 1))


def flip_low(i):
    return i + 1 - 2 * (i % 2)


def flip_far(i):
    return 3 - i


def remote(src, dst, send, recv, device):
    copy = pltpu.make_async_remote_copy(
        src_ref=src, dst_ref=dst, send_sem=send, recv_sem=recv, device_id=device, device_id_type=MESH
    )
    copy.start()
    return copy


def rows_at(start, size):
    return pl.ds(pl.multiple_of(start, size), size)


def send_lon(src, dst, send, recv, a, b, lanes=None):
    cols = pl.ds(0, lanes or src.shape[1])
    copies = []
    for k in range(1, 16):
        peer = (b + k) % 16
        copies.append(remote(
            src.at[rows_at(peer * 16, 16), cols], dst.at[rows_at(b * 16, 16), cols], send.at[k - 1], recv.at[k - 1], (a, peer)
        ))
    dst[rows_at(b * 16, 16), :] = src[rows_at(b * 16, 16), :]
    return copies


def send_lat(src, dst, send, recv, a, b, lanes=None):
    cols = pl.ds(0, lanes or src.shape[1])
    copies = []
    for k in range(1, 8):
        peer = (a + k) % 8
        copies.append(remote(
            src.at[rows_at(peer * 32, 32), cols], dst.at[rows_at(a * 32, 32), cols], send.at[k - 1], recv.at[k - 1], (peer, b)
        ))
    dst[rows_at(a * 32, 32), :] = src[rows_at(a * 32, 32), :]
    return copies


def finish(copies):
    for copy in copies:
        copy.wait()


class Sum:
    def __init__(self, m, place, acc, r1, r2, r3, r4, r5, fin, send_sem, recv_sem):
        self.m, self.place = m, place
        self.acc, self.r = acc, (r1, r2, r3, r4, r5)
        self.fin, self.send_sem, self.recv_sem = fin, send_sem, recv_sem
        self.stage, self.slot, self.copies = 1, 0, []
        a, b, x, c, y, z = place
        self.me1, self.me2 = y * (1 - c) + z * c, z * (1 - c) + y * c

    def chunk(self, i, half):
        return (self.m, i, pl.ds(2 * half, 2))

    def piece(self, i, half):
        return (self.m, self.me1, i, pl.ds(half * SHARD, SHARD))

    def near(self, first, i):
        a, b, x, c, y, z = self.place
        along_y, along_z = i * 4 + z, y * 4 + i
        core = c if first else 1 - c
        return (a, along_y * (1 - core) + along_z * core)

    def send(self, src, dst, device):
        k = self.slot
        self.slot += 1
        self.copies.append(remote(src, dst, self.send_sem.at[self.m, k], self.recv_sem.at[self.m, k], device))

    def begin(self):
        a, b, x, c, y, z = self.place
        m, acc, (r1, r2, r3, r4, r5) = self.m, self.acc, self.r
        me1, me2, s = self.me1, self.me2, self.stage
        if s == 7:
            self.send(self.fin.at[m, c], self.fin.at[m, c], (a + 1 - 2 * c, b))
            return
        for half in range(2):
            q1, q2 = (flip_low, flip_far) if half == 0 else (flip_far, flip_low)
            rows = pl.ds(half * SHARD, SHARD)
            if s == 1:
                p = q1(me1)
                self.send(acc.at[self.chunk(p, half)], r1.at[m, 0, half], self.near(True, p))
                self.send(acc.at[self.chunk(q2(p), half)], r1.at[m, 1, half], self.near(True, p))
            elif s == 2:
                p = q2(me1)
                self.send(acc.at[self.chunk(p, half)], r2.at[m, half], self.near(True, p))
            elif s == 3:
                p = q1(me2)
                self.send(acc.at[self.piece(p, half)], r3.at[m, 0, rows], self.near(False, p))
                self.send(acc.at[self.piece(q2(p), half)], r3.at[m, 1, rows], self.near(False, p))
            elif s == 4:
                p = q2(me2)
                self.send(acc.at[self.piece(p, half)], r4.at[m, rows], self.near(False, p))
            elif s == 5:
                self.send(acc.at[self.piece(me2, half)], r5.at[m, 0, rows], (q1(x) * 2 + c, b))
            elif s == 6:
                self.send(acc.at[self.piece(me2, half)], r5.at[m, 1, rows], (q2(x) * 2 + c, b))

    def end(self):
        a, b, x, c, y, z = self.place
        m, acc, (r1, r2, r3, r4, r5) = self.m, self.acc, self.r
        me1, me2, s = self.me1, self.me2, self.stage
        finish(self.copies)
        self.copies = []
        for half in range(2):
            q2 = flip_far if half == 0 else flip_low
            rows = pl.ds(half * SHARD, SHARD)
            if s == 1:
                acc[self.chunk(me1, half)] += r1[m, 0, half]
                acc[self.chunk(q2(me1), half)] += r1[m, 1, half]
            elif s == 2:
                acc[self.chunk(me1, half)] += r2[m, half]
            elif s == 3:
                acc[self.piece(me2, half)] += r3[m, 0, rows]
                acc[self.piece(q2(me2), half)] += r3[m, 1, rows]
            elif s == 4:
                acc[self.piece(me2, half)] += r4[m, rows]
            elif s == 5:
                acc[self.piece(me2, half)] += r5[m, 0, rows]
            elif s == 6:
                self.fin[m, c, rows] = (acc[self.piece(me2, half)] + r5[m, 1, rows]) * SCALE
        self.stage += 1

    def step(self):
        self.end()
        if self.stage < 8:
            self.begin()


def step_kernel(
    cell_ref, pos_ref, enc_ref, mask_ref, gain_ref, cot_hbm, wq_hbm, wk_hbm, wv_hbm, wo_hbm,
    decoded_hbm, dq_hbm, dk_hbm, dv_hbm, do_hbm, denc_hbm, own_ref,
    w_hi, w_lo, o_hi, o_lo, acc, r1, r2, r3, r4, r5, fin, vr,
    tile_t, tile_g, land_t, land_g, sa0, ra0, rb0, sa1, ra1, rb1,
    t_ref, g_ref, xhat_ref, rstd_ref, n_hi, n_lo, qkv_ref, p_ref, att_ref, datt_ref, dqkv_ref,
    vec_ref, px_ref, pg_ref, pa_ref, pd_ref, pair_s, pair_r, load_s, halo_s, halo_r, lon_s, lon_r, lat_s, lat_r, sum_s, sum_r, vec_s, vec_r, free_s,
):
    a, b = lax.axis_index("lat"), lax.axis_index("lon")
    x, c = a // 2, a % 2
    y, z = b // 4, b % 4
    rows, width = t_ref.shape
    inner = att_ref.shape[1]
    part = width // 2
    heads = inner // HEAD
    half = rows // 2
    up, right = (a + 1) % 8, (b + 1) % 16
    down, left = (a + 7) % 8, (b + 15) % 16

    load_cot = pltpu.make_async_copy(cot_hbm, xhat_ref, load_s.at[0])
    load_o = [
        pltpu.make_async_copy(wo_hbm.at[:, :, :, pl.ds(i * part, part)], acc.at[0, :, :, pl.ds(i * SHARD, SHARD)], load_s.at[1 + i])
        for i in range(2)
    ]
    load_v = pltpu.make_async_copy(wv_hbm, acc.at[1], load_s.at[3])
    load_k = pltpu.make_async_copy(wk_hbm, acc.at[0], load_s.at[4])
    load_q = pltpu.make_async_copy(wq_hbm, acc.at[1], load_s.at[5])
    load_cot.start()
    load_o[0].start()
    load_o[1].start()
    load_v.start()

    def take_weight(load, home, which):
        load.wait()

        @pl.loop(0, 16)
        def _(i):
            r = pl.ds(pl.multiple_of(i * 80, 80), 80)
            cols = slice(which * inner, (which + 1) * inner)
            w_hi[r, cols], w_lo[r, cols] = split(acc[home, i // 4, i % 4])

    peers = [(a, (b + k) % 16) for k in range(1, 16)] + [((a + k) % 8, b) for k in range(1, 8)]
    peers += [(up, right), (down, left)]
    barrier = pltpu.get_barrier_semaphore()
    for peer in peers:
        pl.semaphore_signal(barrier, inc=1, device_id=peer, device_id_type=MESH)

    count = enc_ref.shape[0]
    pos = pos_ref[...].astype(F32)
    lat = jnp.floor((pos + 0.5) * (1.0 / 384.0))
    lon = pos - lat * 384.0
    tile_a = jnp.floor((lat + 0.5) * (1.0 / 12.0))
    tile_b = jnp.floor((lon + 0.5) * (1.0 / 24.0))
    cell = (lat - tile_a * 12.0) * 24.0 + lon - tile_b * 24.0
    target = tile_a * 16.0 + tile_b
    line = lax.broadcasted_iota(jnp.int32, (count, count), 0)
    lane = lax.broadcasted_iota(jnp.int32, (count, count), 1)

    def column(v):
        return jnp.sum(jnp.where(line == lane, v, 0.0), axis=1, keepdims=True)

    earlier = jnp.logical_and(column(target) == target, line < lane)
    rank = jnp.sum(jnp.where(earlier, 1.0, 0.0), axis=0, keepdims=True)
    index1 = target * 2.0 + rank
    index2 = tile_b * 16.0 + tile_a * 2.0 + rank
    column1, column2 = column(index1), column(index2)

    seats = lax.broadcasted_iota(jnp.int32, (SLOTS, count), 0).astype(F32)
    to2 = onehot(seats == index2)
    sa0[:, :part] = pick(to2, enc_ref[:, :part], NN)
    sa0[:, part:] = pick(to2, jnp.broadcast_to(column(cell) + 1.0, (count, 128)), NN)
    to1 = onehot(seats == index1)
    sa1[...] = pick(to1, enc_ref[:, part:], NN)

    pl.semaphore_wait(barrier, len(peers))
    go0 = send_lon(sa0, ra0, lon_s.at[0], lon_r.at[0], a, b)
    go1 = send_lat(sa1, ra1, lat_s.at[0], lat_r.at[0], a, b)

    def halo(tile, land, whole, first):
        moves = (
            (224, 40, land.at[pl.ds(0, 40)], (a, left)), (112, 72, whole.at[pl.ds(72, 72)], (down, b)),
            (184, 40, land.at[pl.ds(40, 40)], (down, b)), (264, 40, land.at[pl.ds(80, 40)], (down, left)),
        )
        return [
            remote(tile.at[pl.ds(row, size)], dst, halo_s.at[first + i], halo_r.at[first + i], device)
            for i, (row, size, dst, device) in enumerate(moves)
        ]

    def settle(tile, land, whole):
        whole[0:72, :] = tile[0:72, :]
        whole[144:180, :] = tile[72:108, :]
        whole[180:216, :] = land[4:40, :]
        whole[216:252, :] = land[40:76, :]
        whole[252:288, :] = land[84:120, :]

    def halo_back(src, tile, first, cols):
        moves = (
            (72, 72, 112, (up, b)), (216, 40, 184, (up, b)), (176, 40, 224, (a, right)), (248, 40, 264, (up, right)),
        )
        return [
            remote(
                src.at[pl.ds(row, size), cols], tile.at[pl.ds(to, size), cols],
                halo_s.at[first + i], halo_r.at[first + i], device,
            )
            for i, (row, size, to, device) in enumerate(moves)
        ]

    def keep_own(src, tile):
        tile[0:72, :] = src[0:72, :]
        tile[72:112, :] = src[144:184, :]

    place = onehot(lax.broadcasted_iota(jnp.int32, (rows, TROWS), 0) == cell_ref[...])
    load_cot.wait()
    for j in range(0, width, 256):
        tile_g[:, j:j + 256] = pick(place, xhat_ref[:, j:j + 256], TN)

    load_o[0].wait()
    load_o[1].wait()
    for i in range(2):
        for j in range(4):
            r = slice(j * 160, (j + 1) * 160)
            cols = slice(i * part, (i + 1) * part)
            o_hi[r, cols], o_lo[r, cols] = split(acc[0, j, :, i * SHARD:(i + 1) * SHARD].reshape(160, part))
    load_k.start()
    take_weight(load_v, 1, 2)
    load_q.start()

    swap = swap_matrix()
    finish(go0)
    sa0[...] = pick(swap, ra0[...], TN)
    go0 = send_lat(sa0, rb0, lat_s.at[1], lat_r.at[1], a, b)
    finish(go1)
    sa1[...] = pick(swap, ra1[...], NN)
    go1 = send_lon(sa1, rb1, lon_s.at[1], lon_r.at[1], a, b)

    take_weight(load_k, 0, 1)
    take_weight(load_q, 1, 0)

    finish(go0)
    table = onehot(rb0[:, part:part + 1] == (cell_ref[...] + 1).astype(F32))
    table2 = dot(swap, table, NN).astype(BF16)
    seen = jnp.sum(table.astype(F32), axis=0, keepdims=True)
    lead = lax.broadcasted_iota(jnp.int32, (16, 1), 0) == 0
    unseen = jnp.where(lead, 1.0 - seen, 0.0).astype(BF16)
    mask = jnp.broadcast_to(jnp.concatenate([mask_ref[i:i + 1, :] for i in range(10)], axis=1), (16, width))
    gain = jnp.concatenate([gain_ref[i:i + 1, :] for i in range(10)], axis=1)
    tile_t[:, :part] = pick(table, rb0[:, :part], TN) + pick(unseen, mask[:, :part], TN)
    finish(go1)
    tile_t[:, part:] = pick(table2, rb1[...], TN) + pick(unseen, mask[:, part:], TN)
    halo_t = halo(tile_t, land_t, t_ref, 4)
    finish(halo_t)
    halo_g = halo(tile_g, land_g, g_ref, 0)
    settle(tile_t, land_t, t_ref)

    step = 32

    @pl.loop(0, rows // step)
    def _(i):
        r = pl.ds(pl.multiple_of(i * step, step), step)
        t = t_ref[r, :]
        centred = t - jnp.mean(t, axis=-1, keepdims=True)
        rstd = lax.rsqrt(jnp.mean(centred * centred, axis=-1, keepdims=True) + 1e-5)
        xhat = centred * rstd
        xhat_ref[r, :] = xhat
        rstd_ref[r, :] = rstd
        n_hi[r, :], n_lo[r, :] = split(xhat * gain)

    @pl.loop(0, 3 * inner // 256)
    def _(j):
        cols = pl.ds(pl.multiple_of(j * 256, 256), 256)
        qkv_ref[:, cols] = dot3((n_hi[...], n_lo[...]), (w_hi[:, cols], w_lo[:, cols]), NN)

    partner = (a + 1 - 2 * c, b)

    def give(src, dst, k):
        return remote(src, dst, pair_s.at[k], pair_r.at[k], partner)

    gifts = [give(xhat_ref, px_ref, 0)]

    qkv_ref[:, 1792:] = dot3((n_hi[...], n_lo[...]), (w_hi[:, 1792:], w_lo[:, 1792:]), NN)

    finish(halo_g)
    settle(tile_g, land_g, g_ref)

    for peer in peers:
        pl.semaphore_signal(free_s, inc=1, device_id=peer, device_id_type=MESH)

    gifts.append(give(g_ref, pg_ref, 1))
    datt_ref[...] = dot3(split(g_ref[...]), (o_hi[...], o_lo[...]), NT)

    att_ref[...] = jnp.zeros_like(att_ref)
    dqkv_ref[...] = jnp.zeros_like(dqkv_ref)
    is_last = a == 7
    low_q = lax.broadcasted_iota(jnp.int32, (half, half), 0) >= half // 2
    low_k = lax.broadcasted_iota(jnp.int32, (half, half), 1) >= half // 2
    blocked = jnp.logical_and(low_q != low_k, is_last)
    norm = 1.0 / math.sqrt(HEAD)

    def head(h):
        lo, hi = head_lanes(h)
        lane = lax.broadcasted_iota(jnp.int32, (half, hi - lo), 1) + lo
        return lo, hi, jnp.logical_and(lane >= h * HEAD, lane < (h + 1) * HEAD)

    @pl.loop(0, 2)
    def _(wd):
        r = pl.ds(pl.multiple_of(wd * half, 16), half)
        for h in range(heads):
            lo, hi, mine = head(h)
            q = split(jnp.where(mine, qkv_ref[r, lo:hi] * norm, 0.0))
            k = split(qkv_ref[r, inner + lo:inner + hi])
            v = split(qkv_ref[r, 2 * inner + lo:2 * inner + hi])
            do = split(jnp.where(mine, datt_ref[r, lo:hi], 0.0))
            s = dot3(q, k, NT)
            s = jnp.where(blocked, -1e30, s)
            e = jnp.exp(s - jnp.max(s, axis=-1, keepdims=True))
            p32 = e / jnp.sum(e, axis=-1, keepdims=True)
            p_ref[wd * heads + h] = p32
            p = split(p32)
            att_ref[r, lo:hi] += jnp.where(mine, dot3(p, v, NN), 0.0)
            dqkv_ref[r, 2 * inner + lo:2 * inner + hi] += dot3(p, do, TN)

    sa0[:, :inner] = jnp.where(c == 0, dqkv_ref[:SLOTS, 2 * inner:], att_ref[:SLOTS, :])
    sa1[:rows - SLOTS, :] = jnp.where(c == 0, dqkv_ref[SLOTS:, 2 * inner:], att_ref[SLOTS:, :])
    gifts.append(give(sa0.at[:, pl.ds(0, inner)], pa_ref.at[pl.ds(0, SLOTS)], 2))
    gifts.append(give(sa1.at[pl.ds(0, rows - SLOTS)], pa_ref.at[pl.ds(SLOTS, rows - SLOTS)], 4))

    att = split(att_ref[...])
    att_row = jnp.concatenate([att[0], att[0], att[1]], axis=1)

    @pl.loop(0, width // 256)
    def _(j):
        cols = pl.ds(pl.multiple_of(j * 256, 256), 256)
        oh, ol = o_hi[:, cols], o_lo[:, cols]
        t_ref[:, cols] += dot(att_row, jnp.concatenate([oh, ol, oh], axis=0), NN)

    pl.semaphore_wait(free_s, len(peers))
    halo_o = halo_back(t_ref, tile_g, 12, pl.ds(0, width))
    keep_own(t_ref, tile_g)

    sums = [Sum(m, (a, b, x, c, y, z), acc, r1, r2, r3, r4, r5, fin, sum_s, sum_r) for m in range(2)]

    def left_rows(own, other):
        return jnp.concatenate([own[0], own[0], own[1], other[0], other[0], other[1]], axis=0)

    def right_rows(own, other):
        return jnp.concatenate([own[0], own[1], own[0], other[0], other[1], other[0]], axis=0)

    def normed_rows(i):
        cols = slice(i * part, (i + 1) * part)
        return left_rows((n_hi[:, cols], n_lo[:, cols]), split(px_ref[:, cols] * gain[:, cols]))

    finish(gifts)

    @pl.when(c == 0)
    def _():
        left6 = left_rows(split(att_ref[...]), split(pa_ref[...]))
        for i in range(2):
            cols = slice(i * part, (i + 1) * part)
            right6 = right_rows(split(g_ref[:, cols]), split(pg_ref[:, cols]))
            acc[0, :, :, i * SHARD:(i + 1) * SHARD] = dot(left6, right6, TN).reshape(4, 4, SHARD, part)

    @pl.when(c == 1)
    def _():
        right6 = right_rows(split(dqkv_ref[:, 2 * inner:]), split(pa_ref[...]))
        for i in range(2):
            res = dot(normed_rows(i), right6, TN).reshape(2, 4, 2 * SHARD, inner)
            for j in range(2):
                acc[0, :, 2 * i + j] = res[j]

    sums[0].begin()

    def grad_rows(which):
        return split(dqkv_ref[:, which * inner:(which + 1) * inner])

    def to_tokens(which, dh, dl, add):
        d3 = jnp.concatenate([dh, dh, dl], axis=1)
        cols = slice(which * inner, (which + 1) * inner)
        for lo in range(0, width, 256):
            r = slice(lo, lo + 256)
            wh, wl = w_hi[r, cols], w_lo[r, cols]
            res = dot(d3, jnp.concatenate([wh, wl, wh], axis=1), NT)
            pg_ref[:, r] = pg_ref[:, r] + res if add else res

    dh, dl = grad_rows(2)
    to_tokens(2, dh, dl, False)

    @pl.loop(0, 2)
    def _(wd):
        r = pl.ds(pl.multiple_of(wd * half, 16), half)
        for h in range(heads):
            lo, hi, mine = head(h)
            q = split(jnp.where(mine, qkv_ref[r, lo:hi] * norm, 0.0))
            k = split(qkv_ref[r, inner + lo:inner + hi])
            v = split(qkv_ref[r, 2 * inner + lo:2 * inner + hi])
            do = split(jnp.where(mine, datt_ref[r, lo:hi], 0.0))
            p32 = p_ref[wd * heads + h]
            dp = dot3(do, v, NT)
            ds = split(p32 * (dp - jnp.sum(dp * p32, axis=-1, keepdims=True)))
            dqkv_ref[r, lo:hi] += jnp.where(mine, dot3(ds, k, NN) * norm, 0.0)
            dqkv_ref[r, inner + lo:inner + hi] += dot3(ds, q, TN)

    def lanes_of(core):
        return pl.ds(pl.multiple_of(core * inner, 128), inner)

    gift = give(dqkv_ref.at[:, lanes_of(1 - c)], pd_ref, 3)
    sums[0].step()
    kh, kl = grad_rows(1)
    to_tokens(1, kh, kl, True)
    qh, ql = grad_rows(0)
    to_tokens(0, qh, ql, True)
    sums[0].step()

    vec_ref[...] = jnp.zeros_like(vec_ref)

    @pl.loop(0, rows // step)
    def _(i):
        r = pl.ds(pl.multiple_of(i * step, step), step)
        dn = pg_ref[r, :]
        xhat = xhat_ref[r, :]
        vec_ref[1:2, :] += jnp.sum(dn * xhat, axis=0, keepdims=True)
        dx = dn * gain
        m1 = jnp.mean(dx, axis=-1, keepdims=True)
        m2 = jnp.mean(dx * xhat, axis=-1, keepdims=True)
        g_ref[r, :] += rstd_ref[r, :] * (dx - m1 - xhat * m2)

    halo_d = [halo_back(g_ref, tile_t, first, pl.ds(lane, part)) for first, lane in ((8, 0), (16, part))]
    keep_own(g_ref, tile_t)

    gift.wait()
    right6 = right_rows(split(dqkv_ref[:, lanes_of(c)]), split(pd_ref[...]))
    for i in range(2):
        res = dot(normed_rows(i), right6, TN).reshape(2, 4, 2 * SHARD, inner)
        for j in range(2):
            for k in range(4):
                at_y, at_z = 2 * i + j, k
                acc[1, at_y * (1 - c) + at_z * c, at_z * (1 - c) + at_y * c] = res[j, k]
    sums[1].begin()
    sums[0].step()

    finish(halo_o)
    for j in range(0, width, 256):
        xhat_ref[:, j:j + 256] = pick(place, tile_g[:, j:j + 256], NN)
    store = pltpu.make_async_copy(xhat_ref, decoded_hbm, load_s.at[0])
    store.start()
    sums[0].step()

    finish(halo_d[0])
    sa1[...] = pick(table, tile_t[:, :part], NN)
    back0 = send_lat(sa1, ra1, lat_s.at[2], lat_r.at[2], a, b)
    finish(halo_d[1])
    sa0[:, :part] = pick(table2, tile_t[:, part:], NN)
    back1 = send_lon(sa0, ra0, lon_s.at[2], lon_r.at[2], a, b, part)
    masked = jnp.where(cell_ref[...] >= 0, 1.0 - seen, 0.0)
    masked = jnp.where(lead, masked, 0.0)[:8].astype(BF16)
    vec_ref[...] += pick(masked, tile_t[...], NN)

    vec_devices = [
        (a + 1 - 2 * c, b), (flip_low(x) * 2 + c, b), (flip_far(x) * 2 + c, b),
        (a, flip_low(y) * 4 + z), (a, flip_far(y) * 4 + z), (a, y * 4 + flip_low(z)), (a, y * 4 + flip_far(z)),
    ]
    vec_copies = []

    def vec_begin(k):
        vec_copies.append(remote(vec_ref, vr.at[k], vec_s.at[k], vec_r.at[k], vec_devices[k]))

    def vec_step():
        k = len(vec_copies) - 1
        vec_copies[k].wait()
        vec_ref[...] += vr[k]
        if k < 6:
            vec_begin(k + 1)

    def round_of_sums():
        for total in sums:
            if total.stage < 8:
                total.step()
        if vec_copies and len(vec_copies) < 7:
            vec_step()

    vec_begin(0)
    round_of_sums()

    finish(back0)
    sa1[...] = pick(swap, ra1[...], NN)
    back0 = send_lon(sa1, rb1, lon_s.at[3], lon_r.at[3], a, b)
    finish(back1)
    sa0[:, :part] = pick(swap, ra0[:, :part], TN)
    back1 = send_lat(sa0, rb0, lat_s.at[3], lat_r.at[3], a, b, part)

    for _ in range(5):
        round_of_sums()

    finish(back0)
    finish(back1)
    slots = lax.broadcasted_iota(jnp.int32, (count, SLOTS), 1).astype(F32)
    tile_g[:count, :part] = pick(onehot(slots == column2), rb1[...], NN)
    tile_g[:count, part:] = pick(onehot(slots == column1), rb0[:, :part], NN)
    store_enc = pltpu.make_async_copy(tile_g.at[pl.ds(0, count)], denc_hbm, load_s.at[6])
    store_enc.start()

    while any(total.stage < 8 for total in sums) or len(vec_copies) < 7:
        round_of_sums()
    vec_step()
    lanes = lax.broadcasted_iota(jnp.int32, (width, 128), 1)
    mine = jnp.logical_and(lax.broadcasted_iota(jnp.int32, (width, 128), 0) == b * 80 + lanes, lanes < 80)
    mine = onehot(mine)
    hi, mid, lo = split3(vec_ref[...] * SCALE)
    own_ref[...] = (dot(hi, mine, NN) + dot(mid, mine, NN)) + dot(lo, mine, NN)
    stores = [
        pltpu.make_async_copy(fin.at[0, 0, pl.ds(0, SHARD)], do_hbm.at[:, pl.ds(0, part)], load_s.at[1]),
        pltpu.make_async_copy(fin.at[0, 0, pl.ds(SHARD, SHARD)], do_hbm.at[:, pl.ds(part, part)], load_s.at[2]),
        pltpu.make_async_copy(fin.at[0, 1], dv_hbm, load_s.at[3]),
        pltpu.make_async_copy(fin.at[1, 0], dq_hbm, load_s.at[4]),
        pltpu.make_async_copy(fin.at[1, 1], dk_hbm, load_s.at[5]),
    ]
    for copy in stores:
        copy.start()
    store.wait()
    store_enc.wait()
    for copy in stores:
        copy.wait()


def decoder_step(cell, pos, enc, mask, gain, cot, wq, wk, wv, wo):
    rows, width = cot.shape
    part = width // 2
    inner = wo.shape[2] * 16
    vm = pl.BlockSpec(memory_space=pltpu.VMEM)
    anyspace = pl.BlockSpec(memory_space=pl.ANY)
    f = jax.ShapeDtypeStruct
    dma = pltpu.SemaphoreType.DMA
    v = pltpu.VMEM
    third = f((2 * SHARD, inner), F32)
    return pl.pallas_call(
        step_kernel,
        out_shape=(
            f((rows, width), F32), third, third, third, f((SHARD, width), F32), f((enc.shape[0], width), F32),
            f((8, 128), F32),
        ),
        in_specs=[vm] * 5 + [anyspace] * 5,
        out_specs=[anyspace] * 6 + [vm],
        scratch_shapes=[
            v((width, 3 * inner), BF16), v((width, 3 * inner), BF16),
            v((inner, width), BF16), v((inner, width), BF16), v((2, 4, 4, 2 * SHARD, inner), F32),
            v((2, 2, 2, 2, 2 * SHARD, inner), F32), v((2, 2, 2, 2 * SHARD, inner), F32),
            v((2, 2, 2 * SHARD, inner), F32), v((2, 2 * SHARD, inner), F32), v((2, 2, 2 * SHARD, inner), F32),
            v((2, 2, 2 * SHARD, inner), F32), v((7, 8, width), F32),
            v((TROWS, width), F32), v((TROWS, width), F32), v((120, width), F32), v((120, width), F32),
            v((SLOTS, part + 128), F32), v((SLOTS, part + 128), F32), v((SLOTS, part + 128), F32),
            v((SLOTS, part), F32), v((SLOTS, part), F32), v((SLOTS, part), F32),
            v((rows, width), F32), v((rows, width), F32), v((rows, width), F32),
            v((rows, 1), F32), v((rows, width), BF16), v((rows, width), BF16),
            v((rows, 3 * inner), F32), v((2 * inner // HEAD, rows // 2, rows // 2), F32),
            v((rows, inner), F32), v((rows, inner), F32), v((rows, 3 * inner), F32),
            v((8, width), F32), v((rows, width), F32), v((rows, width), F32), v((rows, inner), F32), v((rows, inner), F32),
            dma((5,)), dma((5,)), dma((7,)), dma((20,)), dma((20,)), dma((4, 15)), dma((4, 15)), dma((4, 7)), dma((4, 7)),
            dma((2, 17)), dma((2, 17)), dma((7,)), dma((7,)), pltpu.SemaphoreType.REGULAR,
        ],
        compiler_params=pltpu.CompilerParams(
            vmem_limit_bytes=63 * 2**20, collective_id=0, has_side_effects=True
        ),
        name="decoder_step",
    )(cell, pos, enc, mask, gain, cot, wq, wk, wv, wo)


def copy_kernel(*refs):
    for src, dst in zip(refs[:6], refs[7:13]):
        dst[...] = src[...]
    refs[13][...] = refs[6][0:1, :80].reshape(80)
    refs[14][...] = refs[6][1:2, :80].reshape(80)


def hand_over(arrays, own):
    vm = pl.BlockSpec(memory_space=pltpu.VMEM)
    short = jax.ShapeDtypeStruct((80,), F32)
    return pl.pallas_call(
        copy_kernel,
        out_shape=tuple(jax.ShapeDtypeStruct(x.shape, x.dtype) for x in arrays) + (short, short),
        in_specs=[vm] * 7,
        out_specs=[vm] * 8,
        compiler_params=pltpu.CompilerParams(vmem_limit_bytes=60 * 2**20),
        name="hand_over",
    )(*arrays, own)


def body(positions, encoded, mask_token, norm_gain, w_query, w_key, w_value, w_out, cotangent):
    model_width = encoded.shape[1]
    inner = w_out.shape[0]
    shard = (4, 4, 2 * SHARD, inner)
    tile_map = jnp.asarray(tile_rows_map())[None]
    *arrays, own = decoder_step(
        tile_map, positions[None], encoded, mask_token.reshape(-1, 128), norm_gain.reshape(-1, 128),
        cotangent.reshape(-1, model_width), w_query.reshape(shard), w_key.reshape(shard),
        w_value.reshape(shard), w_out.reshape(4, 4, SHARD, model_width),
    )
    decoded, grad_query, grad_key, grad_value, grad_out, grad_encoded, grad_mask, grad_gain = hand_over(arrays, own)
    return (decoded.reshape(cotangent.shape), grad_query, grad_key, grad_value, grad_out, grad_mask, grad_gain, grad_encoded)


def solution(mesh):
    return jax.shard_map(
        body,
        mesh=mesh,
        in_specs=(
            P(("lat", "lon")),
            P(("lat", "lon"), None),
            P(),
            P(),
            P(),
            P(),
            P(),
            P(),
            P("lat", "lon", None),
        ),
        out_specs=(
            P("lat", "lon", None),
            P("lon", None),
            P("lon", None),
            P("lon", None),
            P("lon", None),
            P("lon"),
            P("lon"),
            P(("lat", "lon"), None),
        ),
        check_vma=False,
    )
```

```python
import functools, math
import jax, jax.numpy as jnp
import numpy as np
from jax import lax
from jax.experimental import pallas as pl
from jax.experimental.pallas import tpu as pltpu
from jax.sharding import PartitionSpec as P

HEAD = 80
F32 = jnp.float32
BF16 = jnp.bfloat16


def split(x):
    hi = x.astype(BF16)
    return hi, (x - hi.astype(F32)).astype(BF16)


NN = (((1,), (0,)), ((), ()))
NT = (((1,), (1,)), ((), ()))
TN = (((0,), (0,)), ((), ()))


def dot(a, b, dims):
    return lax.dot_general(a, b, dims, preferred_element_type=F32)


def dot3(a, b, dims):
    if dims == TN:
        return dot(a[0], b[0], dims) + (dot(a[0], b[1], dims) + dot(a[1], b[0], dims))
    rows = a[0].shape[0]
    both = dot(jnp.concatenate([a[0], a[1]], axis=0), b[0], dims)
    return both[:rows] + (both[rows:] + dot(a[0], b[1], dims))


def head_lanes(h):
    low = h * HEAD // 128 * 128
    high = -(-(h + 1) * HEAD // 128) * 128
    return low, high


MESH = pl.DeviceIdType.MESH
SLOTS = 256
TROWS = 304
SHARD = 40
SCALE = 1.0 / 192.0


def tile_rows_map():
    def block(r0, c0, cols):
        return [(r0 + i) * 24 + c0 + j for i in range(6) for j in range(cols)]

    none = [-5] * 4
    order = block(6, 6, 12) + block(6, 18, 6) + none + block(0, 6, 12) + block(0, 18, 6) + none
    order += none + block(6, 0, 6) + none + block(0, 0, 6)
    return np.array(order, np.int32)


def pick(onehot, x, dims):
    hi, lo = split(x)
    return dot(onehot, hi, dims) + dot(onehot, lo, dims)


def onehot(cond):
    return jnp.where(cond, 1.0, 0.0).astype(BF16)


def swap_matrix():
    j = lax.broadcasted_iota(jnp.int32, (SLOTS, SLOTS), 0)
    i = lax.broadcasted_iota(jnp.int32, (SLOTS, SLOTS), 1)
    b = jnp.right_shift(j, 4)
    a = jnp.bitwise_and(jnp.right_shift(j, 1), 7)
    return onehot(i == a * 32 + b * 2 + jnp.bitwise_and(j, 1))


def flip_low(i):
    return i + 1 - 2 * (i % 2)


def flip_far(i):
    return 3 - i


def remote(src, dst, send, recv, device):
    copy = pltpu.make_async_remote_copy(
        src_ref=src, dst_ref=dst, send_sem=send, recv_sem=recv, device_id=device, device_id_type=MESH
    )
    copy.start()
    return copy


def rows_at(start, size):
    return pl.ds(pl.multiple_of(start, size), size)


def send_lon(src, dst, send, recv, a, b, lanes=None):
    cols = pl.ds(0, lanes or src.shape[1])
    copies = []
    for k in range(1, 16):
        peer = (b + k) % 16
        copies.append(remote(
            src.at[rows_at(peer * 16, 16), cols], dst.at[rows_at(b * 16, 16), cols], send.at[k - 1], recv.at[k - 1], (a, peer)
        ))
    dst[rows_at(b * 16, 16), :] = src[rows_at(b * 16, 16), :]
    return copies


def send_lat(src, dst, send, recv, a, b, lanes=None):
    cols = pl.ds(0, lanes or src.shape[1])
    copies = []
    for k in range(1, 8):
        peer = (a + k) % 8
        copies.append(remote(
            src.at[rows_at(peer * 32, 32), cols], dst.at[rows_at(a * 32, 32), cols], send.at[k - 1], recv.at[k - 1], (peer, b)
        ))
    dst[rows_at(a * 32, 32), :] = src[rows_at(a * 32, 32), :]
    return copies


def finish(copies):
    for copy in copies:
        copy.wait()


class Sum:
    def __init__(self, m, home, place, w, acc, r1, r2, r3, r4, r5, fin, send_sem, recv_sem):
        self.m, self.home, self.place = m, home, place
        self.w, self.acc, self.r = w, acc, (r1, r2, r3, r4, r5)
        self.fin, self.send_sem, self.recv_sem = fin, send_sem, recv_sem
        self.first = m % 2 == 0
        self.stage, self.slot, self.copies = 0, 0, []

    def chunk(self, i, half):
        rest = pl.ds(2 * half, 2)
        return (self.m, i, rest) if self.first else (self.m, rest, i)

    def piece(self, i, half):
        a, b, x, c, y, z = self.place
        rows = pl.ds(0, 24) if half == 0 else pl.ds(24, 16)
        return (self.m, y, i, rows) if self.first else (self.m, i, z, rows)

    def near(self, ring, i):
        a, b, x, c, y, z = self.place
        return (a, i * 4 + z) if ring == self.first else (a, y * 4 + i)

    def send(self, src, dst, device):
        k = self.slot
        self.slot += 1
        self.copies.append(remote(src, dst, self.send_sem.at[self.m, k], self.recv_sem.at[self.m, k], device))

    def begin(self):
        a, b, x, c, y, z = self.place
        m, acc, (r1, r2, r3, r4, r5) = self.m, self.acc, self.r
        me1, me2 = (y, z) if self.first else (z, y)
        s = self.stage
        if s == 0:
            self.send(self.w.at[self.home, :, :, 1 - c], acc.at[m], (a + 1 - 2 * c, b))
            return
        if s == 7:
            self.send(self.fin.at[m, c], self.fin.at[m, c], (a + 1 - 2 * c, b))
            return
        for half in range(2):
            q1, q2 = (flip_low, flip_far) if half == 0 else (flip_far, flip_low)
            rows = pl.ds(0, 24) if half == 0 else pl.ds(24, 16)
            if s == 1:
                p = q1(me1)
                self.send(acc.at[self.chunk(p, half)], r1.at[m, 0, half], self.near(True, p))
                self.send(acc.at[self.chunk(q2(p), half)], r1.at[m, 1, half], self.near(True, p))
            elif s == 2:
                p = q2(me1)
                self.send(acc.at[self.chunk(p, half)], r2.at[m, half], self.near(True, p))
            elif s == 3:
                p = q1(me2)
                self.send(acc.at[self.piece(p, half)], r3.at[m, 0, rows], self.near(False, p))
                self.send(acc.at[self.piece(q2(p), half)], r3.at[m, 1, rows], self.near(False, p))
            elif s == 4:
                p = q2(me2)
                self.send(acc.at[self.piece(p, half)], r4.at[m, rows], self.near(False, p))
            elif s == 5:
                self.send(acc.at[self.piece(me2, half)], r5.at[m, 0, rows], (q1(x) * 2 + c, b))
            elif s == 6:
                self.send(acc.at[self.piece(me2, half)], r5.at[m, 1, rows], (q2(x) * 2 + c, b))

    def end(self):
        a, b, x, c, y, z = self.place
        m, acc, (r1, r2, r3, r4, r5) = self.m, self.acc, self.r
        me1, me2 = (y, z) if self.first else (z, y)
        s = self.stage
        finish(self.copies)
        self.copies = []
        if s == 0:
            @pl.loop(0, 4)
            def _(i):
                acc[m, i] += self.w[self.home, i, :, c]
        for half in range(2):
            q2 = flip_far if half == 0 else flip_low
            rows = pl.ds(0, 24) if half == 0 else pl.ds(24, 16)
            if s == 1:
                acc[self.chunk(me1, half)] += r1[m, 0, half]
                acc[self.chunk(q2(me1), half)] += r1[m, 1, half]
            elif s == 2:
                acc[self.chunk(me1, half)] += r2[m, half]
            elif s == 3:
                acc[self.piece(me2, half)] += r3[m, 0, rows]
                acc[self.piece(q2(me2), half)] += r3[m, 1, rows]
            elif s == 4:
                acc[self.piece(me2, half)] += r4[m, rows]
            elif s == 5:
                acc[self.piece(me2, half)] += r5[m, 0, rows]
            elif s == 6:
                self.fin[m, c, rows] = (acc[self.piece(me2, half)] + r5[m, 1, rows]) * SCALE
        self.stage += 1

    def step(self):
        self.end()
        if self.stage < 8:
            self.begin()


def step_kernel(
    cell_ref, pos_ref, enc_ref, mask_ref, gain_ref, cot_hbm, wq_hbm, wk_hbm, wv_hbm, wo_hbm,
    decoded_hbm, dq_ref, dk_ref, dv_ref, do_ref, denc_ref, own_ref,
    w, w_hi, w_lo, o_hi, o_lo, acc, r1, r2, r3, r4, r5, fin, vr,
    tile_t, tile_g, land_t, land_g, sa0, ra0, rb0, sa1, ra1, rb1,
    t_ref, g_ref, xhat_ref, dn_ref, rstd_ref, n_hi, n_lo, qkv_ref, p_ref, att_ref, datt_ref, dqkv_ref,
    vec_ref, load_s, halo_s, halo_r, lon_s, lon_r, lat_s, lat_r, sum_s, sum_r, vec_s, vec_r, free_s,
):
    a, b = lax.axis_index("lat"), lax.axis_index("lon")
    x, c = a // 2, a % 2
    y, z = b // 4, b % 4
    rows, width = t_ref.shape
    inner = att_ref.shape[1]
    part = width // 2
    heads = inner // HEAD
    half = rows // 2
    up, right = (a + 1) % 8, (b + 1) % 16
    down, left = (a + 7) % 8, (b + 15) % 16

    load_cot = pltpu.make_async_copy(cot_hbm, xhat_ref, load_s.at[0])
    load_o = [
        pltpu.make_async_copy(wo_hbm.at[:, :, :, pl.ds(i * part, part)], w.at[0, :, :, i], load_s.at[1 + i])
        for i in range(2)
    ]
    load_v = pltpu.make_async_copy(wv_hbm, w.at[1], load_s.at[3])
    load_k = pltpu.make_async_copy(wk_hbm, w.at[0], load_s.at[4])
    load_q = pltpu.make_async_copy(wq_hbm, w.at[1], load_s.at[5])
    load_cot.start()
    load_o[0].start()
    load_o[1].start()
    load_v.start()

    def take_weight(load, home, which):
        load.wait()

        @pl.loop(0, 16)
        def _(i):
            r = pl.ds(pl.multiple_of(i * 80, 80), 80)
            cols = slice(which * inner, (which + 1) * inner)
            w_hi[r, cols], w_lo[r, cols] = split(w[home, i // 4, i % 4].reshape(80, inner))

    peers = [(a, (b + k) % 16) for k in range(1, 16)] + [((a + k) % 8, b) for k in range(1, 8)]
    peers += [(up, right), (down, left)]
    barrier = pltpu.get_barrier_semaphore()
    for peer in peers:
        pl.semaphore_signal(barrier, inc=1, device_id=peer, device_id_type=MESH)

    count = enc_ref.shape[0]
    pos = pos_ref[...].astype(F32)
    lat = jnp.floor((pos + 0.5) * (1.0 / 384.0))
    lon = pos - lat * 384.0
    tile_a = jnp.floor((lat + 0.5) * (1.0 / 12.0))
    tile_b = jnp.floor((lon + 0.5) * (1.0 / 24.0))
    cell = (lat - tile_a * 12.0) * 24.0 + lon - tile_b * 24.0
    target = tile_a * 16.0 + tile_b
    line = lax.broadcasted_iota(jnp.int32, (count, count), 0)
    lane = lax.broadcasted_iota(jnp.int32, (count, count), 1)

    def column(v):
        return jnp.sum(jnp.where(line == lane, v, 0.0), axis=1, keepdims=True)

    earlier = jnp.logical_and(column(target) == target, line < lane)
    rank = jnp.sum(jnp.where(earlier, 1.0, 0.0), axis=0, keepdims=True)
    index1 = target * 2.0 + rank
    index2 = tile_b * 16.0 + tile_a * 2.0 + rank
    column1, column2 = column(index1), column(index2)

    seats = lax.broadcasted_iota(jnp.int32, (SLOTS, count), 0).astype(F32)
    to2 = onehot(seats == index2)
    sa0[:, :part] = pick(to2, enc_ref[:, :part], NN)
    sa0[:, part:] = pick(to2, jnp.broadcast_to(column(cell) + 1.0, (count, 128)), NN)
    to1 = onehot(seats == index1)
    sa1[...] = pick(to1, enc_ref[:, part:], NN)

    pl.semaphore_wait(barrier, len(peers))
    go0 = send_lon(sa0, ra0, lon_s.at[0], lon_r.at[0], a, b)
    go1 = send_lat(sa1, ra1, lat_s.at[0], lat_r.at[0], a, b)

    def halo(tile, land, whole, first):
        moves = (
            (224, 40, land.at[pl.ds(0, 40)], (a, left)), (112, 72, whole.at[pl.ds(72, 72)], (down, b)),
            (184, 40, land.at[pl.ds(40, 40)], (down, b)), (264, 40, land.at[pl.ds(80, 40)], (down, left)),
        )
        return [
            remote(tile.at[pl.ds(row, size)], dst, halo_s.at[first + i], halo_r.at[first + i], device)
            for i, (row, size, dst, device) in enumerate(moves)
        ]

    def settle(tile, land, whole):
        whole[0:72, :] = tile[0:72, :]
        whole[144:180, :] = tile[72:108, :]
        whole[180:216, :] = land[4:40, :]
        whole[216:252, :] = land[40:76, :]
        whole[252:288, :] = land[84:120, :]

    def halo_back(src, tile, first, cols):
        moves = (
            (72, 72, 112, (up, b)), (216, 40, 184, (up, b)), (176, 40, 224, (a, right)), (248, 40, 264, (up, right)),
        )
        return [
            remote(
                src.at[pl.ds(row, size), cols], tile.at[pl.ds(to, size), cols],
                halo_s.at[first + i], halo_r.at[first + i], device,
            )
            for i, (row, size, to, device) in enumerate(moves)
        ]

    def keep_own(src, tile):
        tile[0:72, :] = src[0:72, :]
        tile[72:112, :] = src[144:184, :]

    place = onehot(lax.broadcasted_iota(jnp.int32, (rows, TROWS), 0) == cell_ref[...])
    load_cot.wait()
    for j in range(0, width, 256):
        tile_g[:, j:j + 256] = pick(place, xhat_ref[:, j:j + 256], TN)

    load_o[0].wait()
    load_o[1].wait()
    for i in range(2):
        for j in range(4):
            r = slice(j * 160, (j + 1) * 160)
            cols = slice(i * part, (i + 1) * part)
            o_hi[r, cols], o_lo[r, cols] = split(w[0, j, :, i].reshape(160, part))
    load_k.start()
    take_weight(load_v, 1, 2)
    load_q.start()

    swap = swap_matrix()
    finish(go0)
    sa0[...] = pick(swap, ra0[...], TN)
    go0 = send_lat(sa0, rb0, lat_s.at[1], lat_r.at[1], a, b)
    finish(go1)
    sa1[...] = pick(swap, ra1[...], NN)
    go1 = send_lon(sa1, rb1, lon_s.at[1], lon_r.at[1], a, b)

    take_weight(load_k, 0, 1)
    take_weight(load_q, 1, 0)

    finish(go0)
    table = onehot(rb0[:, part:part + 1] == (cell_ref[...] + 1).astype(F32))
    table2 = dot(swap, table, NN).astype(BF16)
    seen = jnp.sum(table.astype(F32), axis=0, keepdims=True)
    lead = lax.broadcasted_iota(jnp.int32, (16, 1), 0) == 0
    unseen = jnp.where(lead, 1.0 - seen, 0.0).astype(BF16)
    mask = jnp.broadcast_to(jnp.concatenate([mask_ref[i:i + 1, :] for i in range(10)], axis=1), (16, width))
    gain = jnp.concatenate([gain_ref[i:i + 1, :] for i in range(10)], axis=1)
    tile_t[:, :part] = pick(table, rb0[:, :part], TN) + pick(unseen, mask[:, :part], TN)
    finish(go1)
    tile_t[:, part:] = pick(table2, rb1[...], TN) + pick(unseen, mask[:, part:], TN)
    halo_t = halo(tile_t, land_t, t_ref, 4)
    finish(halo_t)
    halo_g = halo(tile_g, land_g, g_ref, 0)
    settle(tile_t, land_t, t_ref)

    step = 32

    @pl.loop(0, rows // step)
    def _(i):
        r = pl.ds(pl.multiple_of(i * step, step), step)
        t = t_ref[r, :]
        centred = t - jnp.mean(t, axis=-1, keepdims=True)
        rstd = lax.rsqrt(jnp.mean(centred * centred, axis=-1, keepdims=True) + 1e-5)
        xhat = centred * rstd
        xhat_ref[r, :] = xhat
        rstd_ref[r, :] = rstd
        n_hi[r, :], n_lo[r, :] = split(xhat * gain)

    @pl.loop(0, 3 * inner // 256)
    def _(j):
        cols = pl.ds(pl.multiple_of(j * 256, 256), 256)
        qkv_ref[:, cols] = dot3((n_hi[...], n_lo[...]), (w_hi[:, cols], w_lo[:, cols]), NN)

    qkv_ref[:, 1792:] = dot3((n_hi[...], n_lo[...]), (w_hi[:, 1792:], w_lo[:, 1792:]), NN)

    finish(halo_g)
    settle(tile_g, land_g, g_ref)

    for peer in peers:
        pl.semaphore_signal(free_s, inc=1, device_id=peer, device_id_type=MESH)

    datt_ref[...] = dot3(split(g_ref[...]), (o_hi[...], o_lo[...]), NT)

    att_ref[...] = jnp.zeros_like(att_ref)
    dqkv_ref[...] = jnp.zeros_like(dqkv_ref)
    is_last = a == 7
    low_q = lax.broadcasted_iota(jnp.int32, (half, half), 0) >= half // 2
    low_k = lax.broadcasted_iota(jnp.int32, (half, half), 1) >= half // 2
    blocked = jnp.logical_and(low_q != low_k, is_last)
    norm = 1.0 / math.sqrt(HEAD)

    def head(h):
        lo, hi = head_lanes(h)
        lane = lax.broadcasted_iota(jnp.int32, (half, hi - lo), 1) + lo
        return lo, hi, jnp.logical_and(lane >= h * HEAD, lane < (h + 1) * HEAD)

    @pl.loop(0, 2)
    def _(wd):
        r = pl.ds(pl.multiple_of(wd * half, 16), half)
        for h in range(heads):
            lo, hi, mine = head(h)
            q = split(jnp.where(mine, qkv_ref[r, lo:hi] * norm, 0.0))
            k = split(qkv_ref[r, inner + lo:inner + hi])
            v = split(qkv_ref[r, 2 * inner + lo:2 * inner + hi])
            do = split(jnp.where(mine, datt_ref[r, lo:hi], 0.0))
            s = dot3(q, k, NT)
            s = jnp.where(blocked, -1e30, s)
            e = jnp.exp(s - jnp.max(s, axis=-1, keepdims=True))
            p32 = e / jnp.sum(e, axis=-1, keepdims=True)
            p_ref[wd * heads + h] = p32
            p = split(p32)
            att_ref[r, lo:hi] += jnp.where(mine, dot3(p, v, NN), 0.0)
            dqkv_ref[r, 2 * inner + lo:2 * inner + hi] += dot3(p, do, TN)

    att = split(att_ref[...])
    att_row = jnp.concatenate([att[0], att[0], att[1]], axis=1)

    @pl.loop(0, width // 256)
    def _(j):
        cols = pl.ds(pl.multiple_of(j * 256, 256), 256)
        oh, ol = o_hi[:, cols], o_lo[:, cols]
        t_ref[:, cols] += dot(att_row, jnp.concatenate([oh, ol, oh], axis=0), NN)

    pl.semaphore_wait(free_s, len(peers))
    halo_o = halo_back(t_ref, tile_g, 12, pl.ds(0, width))
    keep_own(t_ref, tile_g)

    sums = [
        Sum(m, m % 2, (a, b, x, c, y, z), w, acc, r1, r2, r3, r4, r5, fin, sum_s, sum_r) for m in range(4)
    ]

    att3 = jnp.concatenate([att[0], att[0], att[1]], axis=0)
    gh, gl = split(g_ref[...])
    res = dot(att3, jnp.concatenate([gh, gl, gh], axis=0), TN)
    for i in range(2):
        w[0, :, :, i] = res[:, i * part:(i + 1) * part].reshape(4, 4, SHARD, part)
    sums[0].begin()

    def grad_rows(which):
        return split(dqkv_ref[:, which * inner:(which + 1) * inner])

    def to_tokens(which, dh, dl, add):
        d3 = jnp.concatenate([dh, dh, dl], axis=1)
        cols = slice(which * inner, (which + 1) * inner)
        for lo in range(0, width, 256):
            r = slice(lo, lo + 256)
            wh, wl = w_hi[r, cols], w_lo[r, cols]
            res = dot(d3, jnp.concatenate([wh, wl, wh], axis=1), NT)
            dn_ref[:, r] = dn_ref[:, r] + res if add else res

    def to_weight(cols, homes):
        dh, dl = split(dqkv_ref[:, cols])
        d3 = jnp.concatenate([dh, dl, dh], axis=0)
        for i in range(2):
            half = slice(i * part, (i + 1) * part)
            nh, nl = n_hi[:, half], n_lo[:, half]
            res = dot(jnp.concatenate([nh, nh, nl], axis=0), d3, TN)
            for j, home in enumerate(homes):
                block = res[:, j * inner:(j + 1) * inner]
                w[home, 2 * i:2 * i + 2] = block.reshape(2, 4, 2, SHARD, inner)

    to_weight(slice(2 * inner, 3 * inner), (1,))
    sums[1].begin()
    sums[0].step()
    dh, dl = grad_rows(2)
    to_tokens(2, dh, dl, False)
    sums[1].step()

    @pl.loop(0, 2)
    def _(wd):
        r = pl.ds(pl.multiple_of(wd * half, 16), half)
        for h in range(heads):
            lo, hi, mine = head(h)
            q = split(jnp.where(mine, qkv_ref[r, lo:hi] * norm, 0.0))
            k = split(qkv_ref[r, inner + lo:inner + hi])
            v = split(qkv_ref[r, 2 * inner + lo:2 * inner + hi])
            do = split(jnp.where(mine, datt_ref[r, lo:hi], 0.0))
            p32 = p_ref[wd * heads + h]
            dp = dot3(do, v, NT)
            ds = split(p32 * (dp - jnp.sum(dp * p32, axis=-1, keepdims=True)))
            dqkv_ref[r, lo:hi] += jnp.where(mine, dot3(ds, k, NN) * norm, 0.0)
            dqkv_ref[r, inner + lo:inner + hi] += dot3(ds, q, TN)

    to_weight(slice(0, 2 * inner), (1, 0))
    sums[2].begin()
    sums[3].begin()
    sums[0].step()
    sums[1].step()
    kh, kl = grad_rows(1)
    to_tokens(1, kh, kl, True)
    sums[2].step()
    sums[3].step()
    qh, ql = grad_rows(0)
    to_tokens(0, qh, ql, True)
    sums[0].step()
    sums[1].step()

    vec_ref[...] = jnp.zeros_like(vec_ref)

    @pl.loop(0, rows // step)
    def _(i):
        r = pl.ds(pl.multiple_of(i * step, step), step)
        dn = dn_ref[r, :]
        xhat = xhat_ref[r, :]
        vec_ref[1:2, :] += jnp.sum(dn * xhat, axis=0, keepdims=True)
        dx = dn * gain
        m1 = jnp.mean(dx, axis=-1, keepdims=True)
        m2 = jnp.mean(dx * xhat, axis=-1, keepdims=True)
        g_ref[r, :] += rstd_ref[r, :] * (dx - m1 - xhat * m2)

    halo_d = [halo_back(g_ref, tile_t, first, pl.ds(lane, part)) for first, lane in ((8, 0), (16, part))]
    keep_own(g_ref, tile_t)

    sums[0].step()
    sums[1].step()

    finish(halo_o)
    for j in range(0, width, 256):
        xhat_ref[:, j:j + 256] = pick(place, tile_g[:, j:j + 256], NN)
    store = pltpu.make_async_copy(xhat_ref, decoded_hbm, load_s.at[0])
    store.start()
    sums[2].step()
    sums[3].step()

    finish(halo_d[0])
    sa1[...] = pick(table, tile_t[:, :part], NN)
    back0 = send_lat(sa1, ra1, lat_s.at[2], lat_r.at[2], a, b)
    finish(halo_d[1])
    sa0[:, :part] = pick(table2, tile_t[:, part:], NN)
    back1 = send_lon(sa0, ra0, lon_s.at[2], lon_r.at[2], a, b, part)
    masked = jnp.where(cell_ref[...] >= 0, 1.0 - seen, 0.0)
    masked = jnp.where(lead, masked, 0.0)[:8].astype(BF16)
    vec_ref[...] += pick(masked, tile_t[...], NN)

    vec_devices = [
        (a + 1 - 2 * c, b), (flip_low(x) * 2 + c, b), (flip_far(x) * 2 + c, b),
        (a, flip_low(y) * 4 + z), (a, flip_far(y) * 4 + z), (a, y * 4 + flip_low(z)), (a, y * 4 + flip_far(z)),
    ]
    vec_copies = []

    def vec_begin(k):
        vec_copies.append(remote(vec_ref, vr.at[k], vec_s.at[k], vec_r.at[k], vec_devices[k]))

    def vec_step():
        k = len(vec_copies) - 1
        vec_copies[k].wait()
        vec_ref[...] += vr[k]
        if k < 6:
            vec_begin(k + 1)

    def round_of_sums():
        for total in sums:
            if total.stage < 8:
                total.step()
        if vec_copies and len(vec_copies) < 7:
            vec_step()

    vec_begin(0)
    round_of_sums()
    round_of_sums()

    finish(back0)
    sa1[...] = pick(swap, ra1[...], NN)
    back0 = send_lon(sa1, rb1, lon_s.at[3], lon_r.at[3], a, b)
    finish(back1)
    sa0[:, :part] = pick(swap, ra0[:, :part], TN)
    back1 = send_lat(sa0, rb0, lat_s.at[3], lat_r.at[3], a, b, part)

    for _ in range(4):
        round_of_sums()

    finish(back0)
    finish(back1)
    slots = lax.broadcasted_iota(jnp.int32, (count, SLOTS), 1).astype(F32)
    denc_ref[:, :part] = pick(onehot(slots == column2), rb1[...], NN)
    denc_ref[:, part:] = pick(onehot(slots == column1), rb0[:, :part], NN)

    while any(total.stage < 8 for total in sums) or len(vec_copies) < 7:
        round_of_sums()
    vec_step()
    lanes = lax.broadcasted_iota(jnp.int32, (width, 128), 1)
    mine = jnp.logical_and(lax.broadcasted_iota(jnp.int32, (width, 128), 0) == b * 80 + lanes, lanes < 80)
    mine = onehot(mine)
    hi, lo = split(vec_ref[...] * SCALE)
    own_ref[...] = dot(hi, mine, NN) + dot(lo, mine, NN)
    do_ref[:, :part] = fin[0, 0]
    do_ref[:, part:] = fin[0, 1]
    dv_ref[...] = fin[1]
    dk_ref[...] = fin[2]
    dq_ref[...] = fin[3]
    store.wait()


def decoder_step(cell, pos, enc, mask, gain, cot, wq, wk, wv, wo):
    rows, width = cot.shape
    part = width // 2
    inner = wo.shape[2] * 16
    vm = pl.BlockSpec(memory_space=pltpu.VMEM)
    anyspace = pl.BlockSpec(memory_space=pl.ANY)
    f = jax.ShapeDtypeStruct
    dma = pltpu.SemaphoreType.DMA
    v = pltpu.VMEM
    third = f((2, SHARD, inner), F32)
    return pl.pallas_call(
        step_kernel,
        out_shape=(
            f((rows, width), F32), third, third, third, f((SHARD, width), F32), f((enc.shape[0], width), F32),
            f((8, 128), F32),
        ),
        in_specs=[vm] * 5 + [anyspace] * 5,
        out_specs=[anyspace] + [vm] * 6,
        scratch_shapes=[
            v((2, 4, 4, 2, SHARD, inner), F32), v((width, 3 * inner), BF16), v((width, 3 * inner), BF16),
            v((inner, width), BF16), v((inner, width), BF16), v((4, 4, 4, SHARD, inner), F32),
            v((4, 2, 2, 2, SHARD, inner), F32), v((4, 2, 2, SHARD, inner), F32),
            v((4, 2, SHARD, inner), F32), v((4, SHARD, inner), F32), v((4, 2, SHARD, inner), F32),
            v((4, 2, SHARD, inner), F32), v((7, 8, width), F32),
            v((TROWS, width), F32), v((TROWS, width), F32), v((120, width), F32), v((120, width), F32),
            v((SLOTS, part + 128), F32), v((SLOTS, part + 128), F32), v((SLOTS, part + 128), F32),
            v((SLOTS, part), F32), v((SLOTS, part), F32), v((SLOTS, part), F32),
            v((rows, width), F32), v((rows, width), F32), v((rows, width), F32), v((rows, width), F32),
            v((rows, 1), F32), v((rows, width), BF16), v((rows, width), BF16),
            v((rows, 3 * inner), F32), v((2 * inner // HEAD, rows // 2, rows // 2), F32),
            v((rows, inner), F32), v((rows, inner), F32), v((rows, 3 * inner), F32),
            v((8, width), F32), dma((6,)), dma((20,)), dma((20,)), dma((4, 15)), dma((4, 15)), dma((4, 7)), dma((4, 7)),
            dma((4, 18)), dma((4, 18)), dma((7,)), dma((7,)), pltpu.SemaphoreType.REGULAR,
        ],
        compiler_params=pltpu.CompilerParams(
            vmem_limit_bytes=63 * 2**20, collective_id=0, has_side_effects=True
        ),
        name="decoder_step",
    )(cell, pos, enc, mask, gain, cot, wq, wk, wv, wo)


def copy_kernel(*refs):
    ins, outs, kept, sems = refs[:6], refs[7:13], refs[15:21], refs[21]
    loads = [pltpu.make_async_copy(src, via, sems.at[0, k]) for k, (src, via) in enumerate(zip(ins, kept))]
    stores = [pltpu.make_async_copy(via, dst, sems.at[1, k]) for k, (via, dst) in enumerate(zip(kept, outs))]
    for load in loads:
        load.start()
    refs[13][...] = refs[6][0:1, :80].reshape(80)
    refs[14][...] = refs[6][1:2, :80].reshape(80)
    for load, store in zip(loads[::-1], stores[::-1]):
        load.wait()
        store.start()
    for store in stores:
        store.wait()


def hand_over(arrays, own):
    vm = pl.BlockSpec(memory_space=pltpu.VMEM)
    anyspace = pl.BlockSpec(memory_space=pl.ANY)
    short = jax.ShapeDtypeStruct((80,), F32)
    return pl.pallas_call(
        copy_kernel,
        out_shape=tuple(jax.ShapeDtypeStruct(x.shape, x.dtype) for x in arrays) + (short, short),
        in_specs=[anyspace] * 6 + [vm],
        out_specs=[anyspace] * 6 + [vm] * 2,
        scratch_shapes=[pltpu.VMEM(x.shape, x.dtype) for x in arrays] + [pltpu.SemaphoreType.DMA((2, 6))],
        compiler_params=pltpu.CompilerParams(vmem_limit_bytes=60 * 2**20),
        name="hand_over",
    )(*arrays, own)


def body(positions, encoded, mask_token, norm_gain, w_query, w_key, w_value, w_out, cotangent):
    model_width = encoded.shape[1]
    inner = w_out.shape[0]
    shard = (4, 4, 2, SHARD, inner)
    tile_map = jnp.asarray(tile_rows_map())[None]
    *arrays, own = decoder_step(
        tile_map, positions[None], encoded, mask_token.reshape(-1, 128), norm_gain.reshape(-1, 128),
        cotangent.reshape(-1, model_width), w_query.reshape(shard), w_key.reshape(shard),
        w_value.reshape(shard), w_out.reshape(4, 4, SHARD, model_width),
    )
    decoded, grad_query, grad_key, grad_value, grad_out, grad_encoded, grad_mask, grad_gain = hand_over(arrays, own)
    matrices = (g.reshape(-1, inner) for g in (grad_query, grad_key, grad_value))
    return (decoded.reshape(cotangent.shape), *matrices, grad_out, grad_mask, grad_gain, grad_encoded)


def solution(mesh):
    return jax.shard_map(
        body,
        mesh=mesh,
        in_specs=(
            P(("lat", "lon")),
            P(("lat", "lon"), None),
            P(),
            P(),
            P(),
            P(),
            P(),
            P(),
            P("lat", "lon", None),
        ),
        out_specs=(
            P("lat", "lon", None),
            P("lon", None),
            P("lon", None),
            P("lon", None),
            P("lon", None),
            P("lon"),
            P("lon"),
            P(("lat", "lon"), None),
        ),
        check_vma=False,
    )
```

```python
import functools, math
import jax, jax.numpy as jnp
import numpy as np
from jax import lax
from jax.experimental import pallas as pl
from jax.experimental.pallas import tpu as pltpu
from jax.sharding import PartitionSpec as P

HEAD = 80
F32 = jnp.float32
BF16 = jnp.bfloat16


def split(x):
    hi = x.astype(BF16)
    return hi, (x - hi.astype(F32)).astype(BF16)


NN = (((1,), (0,)), ((), ()))
NT = (((1,), (1,)), ((), ()))
TN = (((0,), (0,)), ((), ()))


def dot(a, b, dims):
    return lax.dot_general(a, b, dims, preferred_element_type=F32)


def dot3(a, b, dims):
    if dims == TN:
        return dot(a[0], b[0], dims) + (dot(a[0], b[1], dims) + dot(a[1], b[0], dims))
    rows = a[0].shape[0]
    both = dot(jnp.concatenate([a[0], a[1]], axis=0), b[0], dims)
    return both[:rows] + (both[rows:] + dot(a[0], b[1], dims))


def head_lanes(h):
    low = h * HEAD // 128 * 128
    high = -(-(h + 1) * HEAD // 128) * 128
    return low, high


MESH = pl.DeviceIdType.MESH
SLOTS = 256
TROWS = 304
SHARD = 40
SCALE = 1.0 / 192.0


def tile_rows_map():
    def block(r0, c0, cols):
        return [(r0 + i) * 24 + c0 + j for i in range(6) for j in range(cols)]

    none = [-5] * 4
    order = block(6, 6, 12) + block(6, 18, 6) + none + block(0, 6, 12) + block(0, 18, 6) + none
    order += none + block(6, 0, 6) + none + block(0, 0, 6)
    return np.array(order, np.int32)


def pick(onehot, x, dims):
    hi, lo = split(x)
    return dot(onehot, hi, dims) + dot(onehot, lo, dims)


def onehot(cond):
    return jnp.where(cond, 1.0, 0.0).astype(BF16)


def swap_matrix():
    j = lax.broadcasted_iota(jnp.int32, (SLOTS, SLOTS), 0)
    i = lax.broadcasted_iota(jnp.int32, (SLOTS, SLOTS), 1)
    b = jnp.right_shift(j, 4)
    a = jnp.bitwise_and(jnp.right_shift(j, 1), 7)
    return onehot(i == a * 32 + b * 2 + jnp.bitwise_and(j, 1))


def flip_low(i):
    return i + 1 - 2 * (i % 2)


def flip_far(i):
    return 3 - i


def remote(src, dst, send, recv, device):
    copy = pltpu.make_async_remote_copy(
        src_ref=src, dst_ref=dst, send_sem=send, recv_sem=recv, device_id=device, device_id_type=MESH
    )
    copy.start()
    return copy


def rows_at(start, size):
    return pl.ds(pl.multiple_of(start, size), size)


def send_lon(src, dst, send, recv, a, b, lanes=None):
    cols = pl.ds(0, lanes or src.shape[1])
    copies = []
    for k in range(1, 16):
        peer = (b + k) % 16
        copies.append(remote(
            src.at[rows_at(peer * 16, 16), cols], dst.at[rows_at(b * 16, 16), cols], send.at[k - 1], recv.at[k - 1], (a, peer)
        ))
    dst[rows_at(b * 16, 16), :] = src[rows_at(b * 16, 16), :]
    return copies


def send_lat(src, dst, send, recv, a, b, lanes=None):
    cols = pl.ds(0, lanes or src.shape[1])
    copies = []
    for k in range(1, 8):
        peer = (a + k) % 8
        copies.append(remote(
            src.at[rows_at(peer * 32, 32), cols], dst.at[rows_at(a * 32, 32), cols], send.at[k - 1], recv.at[k - 1], (peer, b)
        ))
    dst[rows_at(a * 32, 32), :] = src[rows_at(a * 32, 32), :]
    return copies


def finish(copies):
    for copy in copies:
        copy.wait()


class Sum:
    def __init__(self, m, home, place, w, acc, r1, r2, r3, r4, r5, fin, send_sem, recv_sem):
        self.m, self.home, self.place = m, home, place
        self.w, self.acc, self.r = w, acc, (r1, r2, r3, r4, r5)
        self.fin, self.send_sem, self.recv_sem = fin, send_sem, recv_sem
        self.first = m % 2 == 0
        self.stage, self.slot, self.copies = 0, 0, []

    def chunk(self, i, half):
        rest = pl.ds(2 * half, 2)
        return (self.m, i, rest) if self.first else (self.m, rest, i)

    def piece(self, i, half):
        a, b, x, c, y, z = self.place
        rows = pl.ds(0, 24) if half == 0 else pl.ds(24, 16)
        return (self.m, y, i, rows) if self.first else (self.m, i, z, rows)

    def near(self, ring, i):
        a, b, x, c, y, z = self.place
        return (a, i * 4 + z) if ring == self.first else (a, y * 4 + i)

    def send(self, src, dst, device):
        k = self.slot
        self.slot += 1
        self.copies.append(remote(src, dst, self.send_sem.at[self.m, k], self.recv_sem.at[self.m, k], device))

    def begin(self):
        a, b, x, c, y, z = self.place
        m, acc, (r1, r2, r3, r4, r5) = self.m, self.acc, self.r
        me1, me2 = (y, z) if self.first else (z, y)
        s = self.stage
        if s == 0:
            self.send(self.w.at[self.home, :, :, 1 - c], acc.at[m], (a + 1 - 2 * c, b))
            return
        if s == 7:
            self.send(self.fin.at[m, c], self.fin.at[m, c], (a + 1 - 2 * c, b))
            return
        for half in range(2):
            q1, q2 = (flip_low, flip_far) if half == 0 else (flip_far, flip_low)
            rows = pl.ds(0, 24) if half == 0 else pl.ds(24, 16)
            if s == 1:
                p = q1(me1)
                self.send(acc.at[self.chunk(p, half)], r1.at[m, 0, half], self.near(True, p))
                self.send(acc.at[self.chunk(q2(p), half)], r1.at[m, 1, half], self.near(True, p))
            elif s == 2:
                p = q2(me1)
                self.send(acc.at[self.chunk(p, half)], r2.at[m, half], self.near(True, p))
            elif s == 3:
                p = q1(me2)
                self.send(acc.at[self.piece(p, half)], r3.at[m, 0, rows], self.near(False, p))
                self.send(acc.at[self.piece(q2(p), half)], r3.at[m, 1, rows], self.near(False, p))
            elif s == 4:
                p = q2(me2)
                self.send(acc.at[self.piece(p, half)], r4.at[m, rows], self.near(False, p))
            elif s == 5:
                self.send(acc.at[self.piece(me2, half)], r5.at[m, 0, rows], (q1(x) * 2 + c, b))
            elif s == 6:
                self.send(acc.at[self.piece(me2, half)], r5.at[m, 1, rows], (q2(x) * 2 + c, b))

    def end(self):
        a, b, x, c, y, z = self.place
        m, acc, (r1, r2, r3, r4, r5) = self.m, self.acc, self.r
        me1, me2 = (y, z) if self.first else (z, y)
        s = self.stage
        finish(self.copies)
        self.copies = []
        if s == 0:
            @pl.loop(0, 4)
            def _(i):
                acc[m, i] += self.w[self.home, i, :, c]
        for half in range(2):
            q2 = flip_far if half == 0 else flip_low
            rows = pl.ds(0, 24) if half == 0 else pl.ds(24, 16)
            if s == 1:
                acc[self.chunk(me1, half)] += r1[m, 0, half]
                acc[self.chunk(q2(me1), half)] += r1[m, 1, half]
            elif s == 2:
                acc[self.chunk(me1, half)] += r2[m, half]
            elif s == 3:
                acc[self.piece(me2, half)] += r3[m, 0, rows]
                acc[self.piece(q2(me2), half)] += r3[m, 1, rows]
            elif s == 4:
                acc[self.piece(me2, half)] += r4[m, rows]
            elif s == 5:
                acc[self.piece(me2, half)] += r5[m, 0, rows]
            elif s == 6:
                self.fin[m, c, rows] = (acc[self.piece(me2, half)] + r5[m, 1, rows]) * SCALE
        self.stage += 1

    def step(self):
        self.end()
        if self.stage < 8:
            self.begin()


def step_kernel(
    cell_ref, pos_ref, enc_ref, mask_ref, gain_ref, cot_hbm, wq_hbm, wk_hbm, wv_hbm, wo_hbm,
    decoded_hbm, dq_ref, dk_ref, dv_ref, do_ref, denc_ref, own_ref,
    w, w_hi, w_lo, o_hi, o_lo, acc, r1, r2, r3, r4, r5, fin, vr,
    tile_t, tile_g, land_t, land_g, sa0, ra0, rb0, sa1, ra1, rb1,
    t_ref, g_ref, xhat_ref, dn_ref, rstd_ref, n_hi, n_lo, qkv_ref, p_ref, att_ref, datt_ref, dqkv_ref,
    vec_ref, load_s, halo_s, halo_r, lon_s, lon_r, lat_s, lat_r, sum_s, sum_r, vec_s, vec_r, free_s,
):
    a, b = lax.axis_index("lat"), lax.axis_index("lon")
    x, c = a // 2, a % 2
    y, z = b // 4, b % 4
    rows, width = t_ref.shape
    inner = att_ref.shape[1]
    part = width // 2
    heads = inner // HEAD
    half = rows // 2
    up, right = (a + 1) % 8, (b + 1) % 16
    down, left = (a + 7) % 8, (b + 15) % 16

    load_cot = pltpu.make_async_copy(cot_hbm, xhat_ref, load_s.at[0])
    load_o = [
        pltpu.make_async_copy(wo_hbm.at[:, :, :, pl.ds(i * part, part)], w.at[0, :, :, i], load_s.at[1 + i])
        for i in range(2)
    ]
    load_v = pltpu.make_async_copy(wv_hbm, w.at[1], load_s.at[3])
    load_k = pltpu.make_async_copy(wk_hbm, w.at[0], load_s.at[4])
    load_q = pltpu.make_async_copy(wq_hbm, w.at[1], load_s.at[5])
    load_cot.start()
    load_o[0].start()
    load_o[1].start()
    load_v.start()

    def take_weight(load, home, which):
        load.wait()

        @pl.loop(0, 16)
        def _(i):
            r = pl.ds(pl.multiple_of(i * 80, 80), 80)
            cols = slice(which * inner, (which + 1) * inner)
            w_hi[r, cols], w_lo[r, cols] = split(w[home, i // 4, i % 4].reshape(80, inner))

    peers = [(a, (b + k) % 16) for k in range(1, 16)] + [((a + k) % 8, b) for k in range(1, 8)]
    peers += [(up, right), (down, left)]
    barrier = pltpu.get_barrier_semaphore()
    for peer in peers:
        pl.semaphore_signal(barrier, inc=1, device_id=peer, device_id_type=MESH)

    count = enc_ref.shape[0]
    pos = pos_ref[...].astype(F32)
    lat = jnp.floor((pos + 0.5) * (1.0 / 384.0))
    lon = pos - lat * 384.0
    tile_a = jnp.floor((lat + 0.5) * (1.0 / 12.0))
    tile_b = jnp.floor((lon + 0.5) * (1.0 / 24.0))
    cell = (lat - tile_a * 12.0) * 24.0 + lon - tile_b * 24.0
    target = tile_a * 16.0 + tile_b
    line = lax.broadcasted_iota(jnp.int32, (count, count), 0)
    lane = lax.broadcasted_iota(jnp.int32, (count, count), 1)

    def column(v):
        return jnp.sum(jnp.where(line == lane, v, 0.0), axis=1, keepdims=True)

    earlier = jnp.logical_and(column(target) == target, line < lane)
    rank = jnp.sum(jnp.where(earlier, 1.0, 0.0), axis=0, keepdims=True)
    index1 = target * 2.0 + rank
    index2 = tile_b * 16.0 + tile_a * 2.0 + rank
    column1, column2 = column(index1), column(index2)

    seats = lax.broadcasted_iota(jnp.int32, (SLOTS, count), 0).astype(F32)
    to2 = onehot(seats == index2)
    sa0[:, :part] = pick(to2, enc_ref[:, :part], NN)
    sa0[:, part:] = pick(to2, jnp.broadcast_to(column(cell) + 1.0, (count, 128)), NN)
    to1 = onehot(seats == index1)
    sa1[...] = pick(to1, enc_ref[:, part:], NN)

    pl.semaphore_wait(barrier, len(peers))
    go0 = send_lon(sa0, ra0, lon_s.at[0], lon_r.at[0], a, b)
    go1 = send_lat(sa1, ra1, lat_s.at[0], lat_r.at[0], a, b)

    def halo(tile, land, whole, first):
        moves = (
            (224, 40, land.at[pl.ds(0, 40)], (a, left)), (112, 72, whole.at[pl.ds(72, 72)], (down, b)),
            (184, 40, land.at[pl.ds(40, 40)], (down, b)), (264, 40, land.at[pl.ds(80, 40)], (down, left)),
        )
        return [
            remote(tile.at[pl.ds(row, size)], dst, halo_s.at[first + i], halo_r.at[first + i], device)
            for i, (row, size, dst, device) in enumerate(moves)
        ]

    def settle(tile, land, whole):
        whole[0:72, :] = tile[0:72, :]
        whole[144:180, :] = tile[72:108, :]
        whole[180:216, :] = land[4:40, :]
        whole[216:252, :] = land[40:76, :]
        whole[252:288, :] = land[84:120, :]

    def halo_back(src, tile, first, cols):
        moves = (
            (72, 72, 112, (up, b)), (216, 40, 184, (up, b)), (176, 40, 224, (a, right)), (248, 40, 264, (up, right)),
        )
        return [
            remote(
                src.at[pl.ds(row, size), cols], tile.at[pl.ds(to, size), cols],
                halo_s.at[first + i], halo_r.at[first + i], device,
            )
            for i, (row, size, to, device) in enumerate(moves)
        ]

    def keep_own(src, tile):
        tile[0:72, :] = src[0:72, :]
        tile[72:112, :] = src[144:184, :]

    place = onehot(lax.broadcasted_iota(jnp.int32, (rows, TROWS), 0) == cell_ref[...])
    load_cot.wait()
    for j in range(0, width, 256):
        tile_g[:, j:j + 256] = pick(place, xhat_ref[:, j:j + 256], TN)

    load_o[0].wait()
    load_o[1].wait()
    for i in range(2):
        for j in range(4):
            r = slice(j * 160, (j + 1) * 160)
            cols = slice(i * part, (i + 1) * part)
            o_hi[r, cols], o_lo[r, cols] = split(w[0, j, :, i].reshape(160, part))
    load_k.start()
    take_weight(load_v, 1, 2)
    load_q.start()

    swap = swap_matrix()
    finish(go0)
    sa0[...] = pick(swap, ra0[...], TN)
    go0 = send_lat(sa0, rb0, lat_s.at[1], lat_r.at[1], a, b)
    finish(go1)
    sa1[...] = pick(swap, ra1[...], NN)
    go1 = send_lon(sa1, rb1, lon_s.at[1], lon_r.at[1], a, b)

    take_weight(load_k, 0, 1)
    take_weight(load_q, 1, 0)

    finish(go0)
    table = onehot(rb0[:, part:part + 1] == (cell_ref[...] + 1).astype(F32))
    table2 = dot(swap, table, NN).astype(BF16)
    seen = jnp.sum(table.astype(F32), axis=0, keepdims=True)
    lead = lax.broadcasted_iota(jnp.int32, (16, 1), 0) == 0
    unseen = jnp.where(lead, 1.0 - seen, 0.0).astype(BF16)
    mask = jnp.broadcast_to(jnp.concatenate([mask_ref[i:i + 1, :] for i in range(10)], axis=1), (16, width))
    gain = jnp.concatenate([gain_ref[i:i + 1, :] for i in range(10)], axis=1)
    tile_t[:, :part] = pick(table, rb0[:, :part], TN) + pick(unseen, mask[:, :part], TN)
    finish(go1)
    tile_t[:, part:] = pick(table2, rb1[...], TN) + pick(unseen, mask[:, part:], TN)
    halo_t = halo(tile_t, land_t, t_ref, 4)
    finish(halo_t)
    halo_g = halo(tile_g, land_g, g_ref, 0)
    settle(tile_t, land_t, t_ref)

    step = 32

    @pl.loop(0, rows // step)
    def _(i):
        r = pl.ds(pl.multiple_of(i * step, step), step)
        t = t_ref[r, :]
        centred = t - jnp.mean(t, axis=-1, keepdims=True)
        rstd = lax.rsqrt(jnp.mean(centred * centred, axis=-1, keepdims=True) + 1e-5)
        xhat = centred * rstd
        xhat_ref[r, :] = xhat
        rstd_ref[r, :] = rstd
        n_hi[r, :], n_lo[r, :] = split(xhat * gain)

    @pl.loop(0, 3 * inner // 256)
    def _(j):
        cols = pl.ds(pl.multiple_of(j * 256, 256), 256)
        qkv_ref[:, cols] = dot3((n_hi[...], n_lo[...]), (w_hi[:, cols], w_lo[:, cols]), NN)

    qkv_ref[:, 1792:] = dot3((n_hi[...], n_lo[...]), (w_hi[:, 1792:], w_lo[:, 1792:]), NN)

    att_ref[...] = jnp.zeros_like(att_ref)
    dqkv_ref[...] = jnp.zeros_like(dqkv_ref)
    is_last = a == 7
    low_q = lax.broadcasted_iota(jnp.int32, (half, half), 0) >= half // 2
    low_k = lax.broadcasted_iota(jnp.int32, (half, half), 1) >= half // 2
    blocked = jnp.logical_and(low_q != low_k, is_last)
    norm = 1.0 / math.sqrt(HEAD)

    def head(h):
        lo, hi = head_lanes(h)
        lane = lax.broadcasted_iota(jnp.int32, (half, hi - lo), 1) + lo
        return lo, hi, jnp.logical_and(lane >= h * HEAD, lane < (h + 1) * HEAD)

    @pl.loop(0, 2)
    def _(wd):
        r = pl.ds(pl.multiple_of(wd * half, 16), half)
        for h in range(heads):
            lo, hi, mine = head(h)
            q = split(jnp.where(mine, qkv_ref[r, lo:hi] * norm, 0.0))
            k = split(qkv_ref[r, inner + lo:inner + hi])
            v = split(qkv_ref[r, 2 * inner + lo:2 * inner + hi])
            s = dot3(q, k, NT)
            s = jnp.where(blocked, -1e30, s)
            e = jnp.exp(s - jnp.max(s, axis=-1, keepdims=True))
            p32 = e / jnp.sum(e, axis=-1, keepdims=True)
            p_ref[wd * heads + h] = p32
            p = split(p32)
            att_ref[r, lo:hi] += jnp.where(mine, dot3(p, v, NN), 0.0)

    finish(halo_g)
    settle(tile_g, land_g, g_ref)

    for peer in peers:
        pl.semaphore_signal(free_s, inc=1, device_id=peer, device_id_type=MESH)

    datt_ref[...] = dot3(split(g_ref[...]), (o_hi[...], o_lo[...]), NT)

    @pl.loop(0, 2)
    def _(wd):
        r = pl.ds(pl.multiple_of(wd * half, 16), half)
        for h in range(heads):
            lo, hi, mine = head(h)
            do = split(jnp.where(mine, datt_ref[r, lo:hi], 0.0))
            dqkv_ref[r, 2 * inner + lo:2 * inner + hi] += dot3(split(p_ref[wd * heads + h]), do, TN)

    sums = [
        Sum(m, m % 2, (a, b, x, c, y, z), w, acc, r1, r2, r3, r4, r5, fin, sum_s, sum_r) for m in range(4)
    ]

    def grad_rows(which):
        return split(dqkv_ref[:, which * inner:(which + 1) * inner])

    def to_tokens(which, dh, dl, add):
        d3 = jnp.concatenate([dh, dh, dl], axis=1)
        cols = slice(which * inner, (which + 1) * inner)
        for lo in range(0, width, 256):
            r = slice(lo, lo + 256)
            wh, wl = w_hi[r, cols], w_lo[r, cols]
            res = dot(d3, jnp.concatenate([wh, wl, wh], axis=1), NT)
            dn_ref[:, r] = dn_ref[:, r] + res if add else res

    def to_weight(cols, homes):
        dh, dl = split(dqkv_ref[:, cols])
        d3 = jnp.concatenate([dh, dl, dh], axis=0)
        for i in range(2):
            half = slice(i * part, (i + 1) * part)
            nh, nl = n_hi[:, half], n_lo[:, half]
            res = dot(jnp.concatenate([nh, nh, nl], axis=0), d3, TN)
            for j, home in enumerate(homes):
                block = res[:, j * inner:(j + 1) * inner]
                w[home, 2 * i:2 * i + 2] = block.reshape(2, 4, 2, SHARD, inner)

    to_weight(slice(2 * inner, 3 * inner), (1,))
    sums[1].begin()
    att = split(att_ref[...])
    att3 = jnp.concatenate([att[0], att[0], att[1]], axis=0)
    gh, gl = split(g_ref[...])
    res = dot(att3, jnp.concatenate([gh, gl, gh], axis=0), TN)
    for i in range(2):
        w[0, :, :, i] = res[:, i * part:(i + 1) * part].reshape(4, 4, SHARD, part)
    sums[0].begin()

    att_row = jnp.concatenate([att[0], att[0], att[1]], axis=1)

    @pl.loop(0, width // 256)
    def _(j):
        cols = pl.ds(pl.multiple_of(j * 256, 256), 256)
        oh, ol = o_hi[:, cols], o_lo[:, cols]
        t_ref[:, cols] += dot(att_row, jnp.concatenate([oh, ol, oh], axis=0), NN)

    pl.semaphore_wait(free_s, len(peers))
    halo_o = halo_back(t_ref, tile_g, 12, pl.ds(0, width))
    keep_own(t_ref, tile_g)

    dh, dl = grad_rows(2)
    to_tokens(2, dh, dl, False)
    sums[1].step()
    sums[0].step()

    @pl.loop(0, 2)
    def _(wd):
        r = pl.ds(pl.multiple_of(wd * half, 16), half)
        for h in range(heads):
            lo, hi, mine = head(h)
            q = split(jnp.where(mine, qkv_ref[r, lo:hi] * norm, 0.0))
            k = split(qkv_ref[r, inner + lo:inner + hi])
            v = split(qkv_ref[r, 2 * inner + lo:2 * inner + hi])
            do = split(jnp.where(mine, datt_ref[r, lo:hi], 0.0))
            p32 = p_ref[wd * heads + h]
            dp = dot3(do, v, NT)
            ds = split(p32 * (dp - jnp.sum(dp * p32, axis=-1, keepdims=True)))
            dqkv_ref[r, lo:hi] += jnp.where(mine, dot3(ds, k, NN) * norm, 0.0)
            dqkv_ref[r, inner + lo:inner + hi] += dot3(ds, q, TN)

    to_weight(slice(0, 2 * inner), (1, 0))
    sums[2].begin()
    sums[3].begin()
    sums[0].step()
    sums[1].step()
    kh, kl = grad_rows(1)
    to_tokens(1, kh, kl, True)
    qh, ql = grad_rows(0)
    to_tokens(0, qh, ql, True)
    sums[0].step()
    sums[1].step()

    vec_ref[...] = jnp.zeros_like(vec_ref)

    @pl.loop(0, rows // step)
    def _(i):
        r = pl.ds(pl.multiple_of(i * step, step), step)
        dn = dn_ref[r, :]
        xhat = xhat_ref[r, :]
        vec_ref[1:2, :] += jnp.sum(dn * xhat, axis=0, keepdims=True)
        dx = dn * gain
        m1 = jnp.mean(dx, axis=-1, keepdims=True)
        m2 = jnp.mean(dx * xhat, axis=-1, keepdims=True)
        g_ref[r, :] += rstd_ref[r, :] * (dx - m1 - xhat * m2)

    halo_d = [halo_back(g_ref, tile_t, first, pl.ds(lane, part)) for first, lane in ((8, 0), (16, part))]
    sums[2].step()
    sums[3].step()
    keep_own(g_ref, tile_t)

    sums[0].step()
    sums[1].step()

    finish(halo_o)
    for j in range(0, width, 256):
        xhat_ref[:, j:j + 256] = pick(place, tile_g[:, j:j + 256], NN)
    store = pltpu.make_async_copy(xhat_ref, decoded_hbm, load_s.at[0])
    store.start()

    finish(halo_d[0])
    sa1[...] = pick(table, tile_t[:, :part], NN)
    back0 = send_lat(sa1, ra1, lat_s.at[2], lat_r.at[2], a, b)
    finish(halo_d[1])
    sa0[:, :part] = pick(table2, tile_t[:, part:], NN)
    back1 = send_lon(sa0, ra0, lon_s.at[2], lon_r.at[2], a, b, part)
    masked = jnp.where(cell_ref[...] >= 0, 1.0 - seen, 0.0)
    masked = jnp.where(lead, masked, 0.0)[:8].astype(BF16)
    vec_ref[...] += pick(masked, tile_t[...], NN)

    vec_devices = [
        (a + 1 - 2 * c, b), (flip_low(x) * 2 + c, b), (flip_far(x) * 2 + c, b),
        (a, flip_low(y) * 4 + z), (a, flip_far(y) * 4 + z), (a, y * 4 + flip_low(z)), (a, y * 4 + flip_far(z)),
    ]
    vec_copies = []

    def vec_begin(k):
        vec_copies.append(remote(vec_ref, vr.at[k], vec_s.at[k], vec_r.at[k], vec_devices[k]))

    def vec_step():
        k = len(vec_copies) - 1
        vec_copies[k].wait()
        vec_ref[...] += vr[k]
        if k < 6:
            vec_begin(k + 1)

    def round_of_sums():
        for total in sums:
            if total.stage < 8:
                total.step()
        if vec_copies and len(vec_copies) < 7:
            vec_step()

    vec_begin(0)
    round_of_sums()
    round_of_sums()

    finish(back0)
    sa1[...] = pick(swap, ra1[...], NN)
    back0 = send_lon(sa1, rb1, lon_s.at[3], lon_r.at[3], a, b)
    finish(back1)
    sa0[:, :part] = pick(swap, ra0[:, :part], TN)
    back1 = send_lat(sa0, rb0, lat_s.at[3], lat_r.at[3], a, b, part)

    for _ in range(4):
        round_of_sums()

    finish(back0)
    finish(back1)
    slots = lax.broadcasted_iota(jnp.int32, (count, SLOTS), 1).astype(F32)
    denc_ref[:, :part] = pick(onehot(slots == column2), rb1[...], NN)
    denc_ref[:, part:] = pick(onehot(slots == column1), rb0[:, :part], NN)

    while any(total.stage < 8 for total in sums) or len(vec_copies) < 7:
        round_of_sums()
    vec_step()
    lanes = lax.broadcasted_iota(jnp.int32, (width, 128), 1)
    mine = jnp.logical_and(lax.broadcasted_iota(jnp.int32, (width, 128), 0) == b * 80 + lanes, lanes < 80)
    mine = onehot(mine)
    hi, lo = split(vec_ref[...] * SCALE)
    own_ref[...] = dot(hi, mine, NN) + dot(lo, mine, NN)
    do_ref[:, :part] = fin[0, 0]
    do_ref[:, part:] = fin[0, 1]
    dv_ref[...] = fin[1]
    dk_ref[...] = fin[2]
    dq_ref[...] = fin[3]
    store.wait()


def decoder_step(cell, pos, enc, mask, gain, cot, wq, wk, wv, wo):
    rows, width = cot.shape
    part = width // 2
    inner = wo.shape[2] * 16
    vm = pl.BlockSpec(memory_space=pltpu.VMEM)
    anyspace = pl.BlockSpec(memory_space=pl.ANY)
    f = jax.ShapeDtypeStruct
    dma = pltpu.SemaphoreType.DMA
    v = pltpu.VMEM
    third = f((2, SHARD, inner), F32)
    return pl.pallas_call(
        step_kernel,
        out_shape=(
            f((rows, width), F32), third, third, third, f((SHARD, width), F32), f((enc.shape[0], width), F32),
            f((8, 128), F32),
        ),
        in_specs=[vm] * 5 + [anyspace] * 5,
        out_specs=[anyspace] + [vm] * 6,
        scratch_shapes=[
            v((2, 4, 4, 2, SHARD, inner), F32), v((width, 3 * inner), BF16), v((width, 3 * inner), BF16),
            v((inner, width), BF16), v((inner, width), BF16), v((4, 4, 4, SHARD, inner), F32),
            v((4, 2, 2, 2, SHARD, inner), F32), v((4, 2, 2, SHARD, inner), F32),
            v((4, 2, SHARD, inner), F32), v((4, SHARD, inner), F32), v((4, 2, SHARD, inner), F32),
            v((4, 2, SHARD, inner), F32), v((7, 8, width), F32),
            v((TROWS, width), F32), v((TROWS, width), F32), v((120, width), F32), v((120, width), F32),
            v((SLOTS, part + 128), F32), v((SLOTS, part + 128), F32), v((SLOTS, part + 128), F32),
            v((SLOTS, part), F32), v((SLOTS, part), F32), v((SLOTS, part), F32),
            v((rows, width), F32), v((rows, width), F32), v((rows, width), F32), v((rows, width), F32),
            v((rows, 1), F32), v((rows, width), BF16), v((rows, width), BF16),
            v((rows, 3 * inner), F32), v((2 * inner // HEAD, rows // 2, rows // 2), F32),
            v((rows, inner), F32), v((rows, inner), F32), v((rows, 3 * inner), F32),
            v((8, width), F32), dma((6,)), dma((20,)), dma((20,)), dma((4, 15)), dma((4, 15)), dma((4, 7)), dma((4, 7)),
            dma((4, 18)), dma((4, 18)), dma((7,)), dma((7,)), pltpu.SemaphoreType.REGULAR,
        ],
        compiler_params=pltpu.CompilerParams(
            vmem_limit_bytes=63 * 2**20, collective_id=0, has_side_effects=True
        ),
        name="decoder_step",
    )(cell, pos, enc, mask, gain, cot, wq, wk, wv, wo)


def copy_kernel(*refs):
    for src, dst in zip(refs[:6], refs[7:13]):
        dst[...] = src[...]
    refs[13][...] = refs[6][0:1, :80].reshape(80)
    refs[14][...] = refs[6][1:2, :80].reshape(80)


def hand_over(arrays, own):
    vm = pl.BlockSpec(memory_space=pltpu.VMEM)
    short = jax.ShapeDtypeStruct((80,), F32)
    return pl.pallas_call(
        copy_kernel,
        out_shape=tuple(jax.ShapeDtypeStruct(x.shape, x.dtype) for x in arrays) + (short, short),
        in_specs=[vm] * 7,
        out_specs=[vm] * 8,
        compiler_params=pltpu.CompilerParams(vmem_limit_bytes=60 * 2**20),
        name="hand_over",
    )(*arrays, own)


def body(positions, encoded, mask_token, norm_gain, w_query, w_key, w_value, w_out, cotangent):
    model_width = encoded.shape[1]
    inner = w_out.shape[0]
    shard = (4, 4, 2, SHARD, inner)
    tile_map = jnp.asarray(tile_rows_map())[None]
    *arrays, own = decoder_step(
        tile_map, positions[None], encoded, mask_token.reshape(-1, 128), norm_gain.reshape(-1, 128),
        cotangent.reshape(-1, model_width), w_query.reshape(shard), w_key.reshape(shard),
        w_value.reshape(shard), w_out.reshape(4, 4, SHARD, model_width),
    )
    decoded, grad_query, grad_key, grad_value, grad_out, grad_encoded, grad_mask, grad_gain = hand_over(arrays, own)
    matrices = (g.reshape(-1, inner) for g in (grad_query, grad_key, grad_value))
    return (decoded.reshape(cotangent.shape), *matrices, grad_out, grad_mask, grad_gain, grad_encoded)


def solution(mesh):
    return jax.shard_map(
        body,
        mesh=mesh,
        in_specs=(
            P(("lat", "lon")),
            P(("lat", "lon"), None),
            P(),
            P(),
            P(),
            P(),
            P(),
            P(),
            P("lat", "lon", None),
        ),
        out_specs=(
            P("lat", "lon", None),
            P("lon", None),
            P("lon", None),
            P("lon", None),
            P("lon", None),
            P("lon"),
            P("lon"),
            P(("lat", "lon"), None),
        ),
        check_vma=False,
    )
```
